32 devices in a mesh: blk: 16 (over z, y, x), rep: 2 (over core).
Axes of the slice: x: 2, y: 2, z: 4, core: 2. Of those that a mesh axis runs over, the one named last changes fastest.
Arguments:
- hidden_pre: bfloat16 [2048, 1024], P('blk'), may hold values from -6 to 6
- adj_vals: bfloat16 [16, 16, 128, 128], P('blk', 'rep'), may hold values from -0.125 to 0.125
- adj_cols: int32 [16, 16], P('blk', 'rep'), may hold values from 0 to 15, as said below
- w_out: bfloat16 [1024, 1024], replicated, may hold values from -0.1875 to 0.1875
- cotangent: bfloat16 [2048, 1024], P('blk'), may hold values from -6 to 6
Outputs:
- aggregated: bfloat16 [2048, 1024], P('blk', 'rep')
- grad_weight: float32 [1024, 1024], P('blk', 'rep')
- grad_pre: bfloat16 [2048, 1024], P('blk', 'rep')
The draws below stay inside these ranges and needn't reach their ends.
Inputs may be any that keep to these rules, and one draw needn't show every extreme that they name: For block-row i, let b = i // 1 and, for slot k, s = (b - adj_cols[i, k]) mod (16). Then s // 8 == k // 8, and the slots of one block-row with equal k // 8 have distinct s.
All inputs are finite; a program needn't handle non-finite values.
Results may differ from the reference program's by a relative error of at most 0.014.
Values may be sent and summed in bfloat16 or wider, within the bound.
No kernel may reach another device: no remote copies, remote signals or barrier semaphores. Data moves between devices by JAX's collectives and lax.ppermute only.
A program may use at most 64 MiB of HBM per device.

```python
import jax
import jax.numpy as jnp
from jax import lax

D = 1024
TILE = 128
SLOTS = 16
RB = 1
NB = 16
ROWS = 2048
SPAN = 8
SLOTS_REP = 8


def draw_adj_cols(key, part):
    owner_count = NB // RB
    groups = SLOTS // SLOTS_REP
    first_key, second_key = jax.random.split(key)
    row_owner = jnp.arange(NB, dtype=jnp.int32) // RB
    scores = jax.random.randint(first_key, (NB, groups, SPAN), 0, 1 << 20) * SPAN + jnp.arange(SPAN, dtype=jnp.int32)
    order_idx = jnp.argsort(scores, axis=-1)[:, :, :SLOTS_REP].astype(jnp.int32)
    sections = jnp.arange(groups, dtype=jnp.int32)[None, :, None] * SPAN + order_idx
    target = jnp.mod(row_owner[:, None, None] - sections, owner_count)
    inner = jax.random.randint(second_key, (NB, groups, SLOTS_REP), 0, RB)
    return (target * RB + inner).reshape(NB, SLOTS).astype(jnp.int32)


def block_levels(key, dims, cuts, low, high):
    level = 1.0
    for position, parts in cuts:
        draws = jax.random.uniform(jax.random.fold_in(jax.random.fold_in(key, 6), position), (parts,), jnp.float32, low / len(cuts), high / len(cuts))
        level = level * jnp.repeat(jnp.exp(draws), dims[position] // parts).reshape((-1,) + (1,) * (len(dims) - 1 - position))
    return level


def scatter_about(own_key, shape, deviation, most, pieces=(), kind=jnp.bfloat16):
    factor_of = block_levels(own_key, shape, pieces, -0.22, 0.18) if pieces else 1.0
    drawn = jax.random.normal(own_key, shape, jnp.float32) * deviation * factor_of
    return jnp.minimum(jnp.maximum(drawn, -most), most).astype(kind)


def setup_inputs(seed: int = 0) -> dict:
    key_of = jax.random.split(jax.random.key(seed), 6)
    return {
        "hidden_pre": scatter_about(key_of[0], (ROWS, D), 1.0, 6.0, ((0, 16),)),
        "adj_vals": scatter_about(key_of[1], (NB, SLOTS, TILE, TILE), (TILE * SLOTS) ** -0.5, 0.125, ((0, 16), (1, 2))),
        "adj_cols": draw_adj_cols(jax.random.fold_in(key_of[5], 71), 0),
        "w_out": scatter_about(key_of[3], (D, D), D ** -0.5, 0.1875),
        "cotangent": scatter_about(key_of[4], (ROWS, D), 1.0, 6.0, ((0, 16),)),
    }


def aggregate(adj_vals, adj_cols, features):
    blocks = features.reshape(NB, TILE, D)

    def one_row(row_pair):
        tile_vals, columns = row_pair
        picked = blocks[columns].astype(jnp.float32)
        return jnp.einsum('kab,kbd->ad', tile_vals.astype(jnp.float32), picked)

    return lax.map(one_row, (adj_vals, adj_cols)).reshape(ROWS, D)


def transposed(adj_vals, adj_cols, features):
    blocks = features.reshape(NB, TILE, D)

    def one_row(row_pair):
        tile_vals, grad_block = row_pair
        return jnp.einsum('kab,ad->kbd', tile_vals.astype(jnp.float32), grad_block.astype(jnp.float32))

    contribution = lax.map(one_row, (adj_vals, blocks))
    summed = jax.ops.segment_sum(contribution.reshape(NB * SLOTS, TILE, D), adj_cols.reshape(-1).astype(jnp.int32), num_segments=NB)
    return summed.reshape(ROWS, D)


def reference(hidden_pre, adj_vals, adj_cols, w_out, cotangent):
    hidden_act = jnp.maximum(hidden_pre, 0)
    projected = jnp.dot(hidden_act, w_out, preferred_element_type=jnp.float32).astype(jnp.bfloat16)
    aggregated = aggregate(adj_vals, adj_cols, projected).astype(jnp.bfloat16)
    back_grad = transposed(adj_vals, adj_cols, cotangent).astype(jnp.bfloat16)
    grad_weight = jnp.dot(hidden_act.T, back_grad, preferred_element_type=jnp.float32)
    grad_in = jnp.dot(back_grad, w_out.T, preferred_element_type=jnp.float32)
    grad_pre = jnp.where(hidden_pre > 0, grad_in, 0.0).astype(jnp.bfloat16)
    return aggregated, grad_weight, grad_pre
```

```python
import jax
import jax.numpy as jnp
from jax import lax
from jax.sharding import PartitionSpec as P


def grid_of(blk_count, section_span):
    inner = 1 << ((blk_count.bit_length() - 1) // 2)
    while section_span % inner:
        inner //= 2
    return blk_count // inner, inner


def shards(hidden_pre, adj_vals, adj_cols, w_out, cotangent):
    feature_width = hidden_pre.shape[1]
    tile_size = adj_vals.shape[2]
    blk_count = lax.axis_size("blk")
    rep_count = lax.axis_size("rep")
    section_span = blk_count // rep_count
    outer, inner = grid_of(blk_count, section_span)
    per_core = section_span // inner
    blk_pos = lax.axis_index("blk")
    rep_pos = lax.axis_index("rep")
    outer_pos = blk_pos // inner
    inner_pos = blk_pos % inner
    cols_here = feature_width // rep_count
    rows_here = feature_width // blk_count
    bf16 = jnp.bfloat16

    def along_inner(value, steps):
        if steps % inner == 0:
            return value
        pairs = [
            (o * inner + i, o * inner + (i + steps) % inner)
            for o in range(outer)
            for i in range(inner)
        ]
        return lax.ppermute(value, "blk", pairs)

    def along_outer(value, steps):
        if steps % outer == 0:
            return value
        pairs = [
            (o * inner + i, (o + steps) % outer * inner + i)
            for o in range(outer)
            for i in range(inner)
        ]
        return lax.ppermute(value, "blk", pairs)

    def dot(lhs, rhs, dims):
        return lax.dot_general(lhs, rhs, (dims, ((), ())), preferred_element_type=jnp.float32)

    hidden_part = jnp.maximum(
        lax.dynamic_slice_in_dim(hidden_pre, rep_pos * cols_here, cols_here, 1), 0
    )
    grad_part = lax.dynamic_slice_in_dim(cotangent, rep_pos * cols_here, cols_here, 1)
    hidden_stack = jnp.concatenate([along_outer(hidden_part, e) for e in range(outer)], 0)

    within = jnp.mod(blk_pos - adj_cols[0], blk_count) - rep_pos * section_span
    hit = within[None, :] == jnp.arange(section_span, dtype=jnp.int32)[:, None]
    ordered = jnp.sum(
        jnp.where(hit[:, :, None, None], adj_vals[0][None].astype(jnp.float32), 0.0), axis=1
    ).astype(bf16)
    ordered = ordered.reshape(per_core, inner, tile_size, tile_size)
    received = jnp.stack([along_inner(ordered[:, t], -t) for t in range(inner)])
    grad_stack = jnp.concatenate([along_inner(grad_part, -t) for t in range(inner)], 0)
    everyone = lax.all_gather(received, "rep", axis=1)
    everyone = everyone.reshape(inner, outer, tile_size, tile_size)
    wrapped = (inner_pos + jnp.arange(inner, dtype=jnp.int32)) >= inner
    block = jnp.where(wrapped[:, None, None, None], jnp.roll(everyone, 1, 1), everyone)
    block = block.transpose(0, 2, 1, 3).reshape(inner * tile_size, outer * tile_size)

    mixed_t = dot(hidden_stack, block, ((0,), (1,))).astype(bf16)
    by_group = mixed_t.reshape(per_core, inner, rows_here, inner * tile_size)
    mixed_cols = 0.0
    for d in range(inner):
        piece = lax.dynamic_index_in_dim(by_group, (inner_pos + d) % inner, 1, keepdims=False)
        piece = jnp.roll(piece, -d * tile_size, 2)
        mixed_cols = mixed_cols + along_inner(piece, d).astype(jnp.float32)
    mixed_cols = mixed_cols.astype(bf16)
    mixed_rows = 0.0
    for t in range(inner):
        piece = mixed_t[:, t * tile_size : (t + 1) * tile_size]
        mixed_rows = mixed_rows + along_inner(piece, t).astype(jnp.float32)
    mixed_rows = mixed_rows.astype(bf16)

    back_stack = dot(block, grad_stack, ((0,), (0,))).astype(bf16)
    back_part = 0.0
    for e in range(outer):
        piece = back_stack[e * tile_size : (e + 1) * tile_size]
        back_part = back_part + along_outer(piece, -e).astype(jnp.float32)
    back_part = back_part.astype(bf16)

    mixed_cols = lax.all_gather(mixed_cols, "rep", axis=0, tiled=True)
    weight_part = dot(
        mixed_cols.reshape(outer * rows_here, inner * tile_size), grad_stack, ((1,), (0,))
    ).astype(bf16)
    weight_part = weight_part.reshape(outer, rows_here, cols_here)
    grad_weight = 0.0
    for e in range(outer):
        piece = lax.dynamic_index_in_dim(weight_part, (outer_pos + e) % outer, 0, keepdims=False)
        grad_weight = grad_weight + along_outer(piece, e).astype(jnp.float32)

    mixed_rows = lax.all_gather(mixed_rows, "rep", axis=0, tiled=True)
    w_columns = lax.dynamic_slice_in_dim(w_out, rep_pos * cols_here, cols_here, 1)
    out_part = dot(mixed_rows, w_columns, ((0,), (0,))).astype(bf16)

    back_full = lax.all_gather(back_part, "rep", axis=1, tiled=True)
    w_rows = lax.dynamic_slice_in_dim(w_out, rep_pos * cols_here, cols_here, 0)
    grad_in = dot(back_full, w_rows, ((1,), (1,)))
    pre_part = lax.dynamic_slice_in_dim(hidden_pre, rep_pos * cols_here, cols_here, 1)
    grad_pre = jnp.where(pre_part > 0, grad_in, 0.0).astype(bf16)
    return (out_part, grad_weight, grad_pre)


def solution(mesh):
    placed = (P("blk", None), P("blk", "rep", None, None), P("blk", "rep"), P(), P("blk", None))
    return jax.shard_map(
        shards,
        mesh=mesh,
        in_specs=placed,
        out_specs=(P("blk", "rep"), P("blk", "rep"), P("blk", "rep")),
        check_vma=False,
    )
```

```python
import jax
import jax.numpy as jnp
from jax import lax
from jax.sharding import PartitionSpec as P


def grid_of(blk_count, section_span):
    inner = 1 << ((blk_count.bit_length() - 1) // 2)
    while section_span % inner:
        inner //= 2
    return blk_count // inner, inner


def shards(hidden_pre, adj_vals, adj_cols, w_out, cotangent):
    feature_width = hidden_pre.shape[1]
    tile_size = adj_vals.shape[2]
    blk_count = lax.axis_size("blk")
    rep_count = lax.axis_size("rep")
    section_span = blk_count // rep_count
    outer, inner = grid_of(blk_count, section_span)
    per_core = section_span // inner
    blk_pos = lax.axis_index("blk")
    rep_pos = lax.axis_index("rep")
    outer_pos = blk_pos // inner
    inner_pos = blk_pos % inner
    cols_here = feature_width // rep_count
    rows_here = feature_width // blk_count
    bf16 = jnp.bfloat16
    inner_groups = [[o * inner + i for i in range(inner)] for o in range(outer)]
    outer_groups = [[o * inner + i for o in range(outer)] for i in range(inner)]

    def swap_all(value, groups):
        return lax.all_to_all(value, "blk", 0, 0, axis_index_groups=groups)

    def dot(lhs, rhs, dims):
        return lax.dot_general(lhs, rhs, (dims, ((), ())), preferred_element_type=jnp.float32)

    hidden_part = jnp.maximum(
        lax.dynamic_slice_in_dim(hidden_pre, rep_pos * cols_here, cols_here, 1), 0
    )
    hidden_stack = swap_all(
        jnp.broadcast_to(hidden_part[None], (outer, tile_size, cols_here)), outer_groups
    ).reshape(outer * tile_size, cols_here)

    order = jnp.arange(section_span, dtype=jnp.int32).reshape(per_core, inner).T.reshape(-1)
    hit = (adj_cols[0] % section_span)[None, :] == order[:, None]
    ordered = jnp.sum(
        jnp.where(hit[:, :, None, None], adj_vals[0][None].astype(jnp.float32), 0.0), axis=1
    ).astype(bf16)
    ordered = ordered.reshape(inner, per_core, tile_size, tile_size).transpose(0, 2, 1, 3)
    ordered = ordered.reshape(inner, tile_size, per_core * tile_size)
    grad_part = lax.dynamic_slice_in_dim(cotangent, rep_pos * cols_here, cols_here, 1)
    grad_copies = jnp.broadcast_to(grad_part[None], (inner, tile_size, cols_here))
    arrived = swap_all(jnp.concatenate([ordered, grad_copies], 2), inner_groups)
    arrived = arrived.reshape(inner * tile_size, per_core * tile_size + cols_here)
    grad_stack = arrived[:, per_core * tile_size :]
    everyone = lax.all_gather(arrived[:, : per_core * tile_size], "rep", axis=0)

    row_block = outer_pos * inner + jnp.repeat(jnp.arange(inner, dtype=jnp.int32), tile_size)
    pieces = []
    for o in range(outer):
        column = o * inner + inner_pos
        group = jnp.mod(row_block - column, blk_count) // section_span
        m = o % per_core
        piece = everyone[0, :, m * tile_size : (m + 1) * tile_size]
        for r in range(1, rep_count):
            other = everyone[r, :, m * tile_size : (m + 1) * tile_size]
            piece = jnp.where((group == r)[:, None], other, piece)
        pieces.append(piece)
    block = jnp.concatenate(pieces, 1)

    back_stack = dot(block, grad_stack, ((0,), (0,))).astype(bf16)
    back_arrived = swap_all(back_stack.reshape(outer, tile_size, cols_here), outer_groups)

    mixed = dot(block, hidden_stack, ((1,), (0,))).astype(bf16)
    mixed_t = dot(hidden_stack, block, ((0,), (1,))).astype(bf16)
    by_group = mixed_t.reshape(per_core, inner, rows_here, inner * tile_size)
    by_group = by_group.transpose(1, 0, 2, 3).reshape(
        inner, per_core * rows_here, inner * tile_size
    )
    mixed_rows = swap_all(mixed.reshape(inner, tile_size, cols_here), inner_groups)
    mixed_cols = swap_all(by_group, inner_groups)
    mixed_rows = jnp.sum(mixed_rows.astype(jnp.float32), 0).astype(bf16)
    mixed_cols = jnp.sum(mixed_cols.astype(jnp.float32), 0).astype(bf16)

    mixed_cols = lax.all_gather(mixed_cols, "rep", axis=0, tiled=True)
    weight_part = dot(mixed_cols, grad_stack, ((1,), (0,))).astype(bf16)
    weight_arrived = swap_all(weight_part.reshape(outer, rows_here, cols_here), outer_groups)
    grad_weight = jnp.sum(weight_arrived.astype(jnp.float32), 0)

    mixed_rows = lax.all_gather(mixed_rows, "rep", axis=1, tiled=True)
    w_columns = lax.dynamic_slice_in_dim(w_out, rep_pos * cols_here, cols_here, 1)
    out_part = dot(mixed_rows, w_columns, ((1,), (0,))).astype(bf16)

    back_part = jnp.sum(back_arrived.astype(jnp.float32), 0).astype(bf16)
    back_full = lax.all_gather(back_part, "rep", axis=1, tiled=True)
    w_rows = lax.dynamic_slice_in_dim(w_out, rep_pos * cols_here, cols_here, 0)
    grad_in = dot(back_full, w_rows, ((1,), (1,)))
    pre_part = lax.dynamic_slice_in_dim(hidden_pre, rep_pos * cols_here, cols_here, 1)
    grad_pre = jnp.where(pre_part > 0, grad_in, 0.0).astype(bf16)
    return (out_part, grad_weight, grad_pre)


def solution(mesh):
    placed = (P("blk", None), P("blk", "rep", None, None), P("blk", "rep"), P(), P("blk", None))
    return jax.shard_map(
        shards,
        mesh=mesh,
        in_specs=placed,
        out_specs=(P("blk", "rep"), P("blk", "rep"), P("blk", "rep")),
        check_vma=False,
    )
```

```python
import jax
import jax.numpy as jnp
from jax import lax
from jax.sharding import PartitionSpec as P


def grid_of(blk_count, section_span):
    inner = 1 << ((blk_count.bit_length() - 1) // 2)
    while section_span % inner:
        inner //= 2
    return blk_count // inner, inner


def shards(hidden_pre, adj_vals, adj_cols, w_out, cotangent):
    feature_width = hidden_pre.shape[1]
    tile_size = adj_vals.shape[2]
    blk_count = lax.axis_size("blk")
    rep_count = lax.axis_size("rep")
    section_span = blk_count // rep_count
    outer, inner = grid_of(blk_count, section_span)
    per_core = section_span // inner
    blk_pos = lax.axis_index("blk")
    rep_pos = lax.axis_index("rep")
    outer_pos = blk_pos // inner
    inner_pos = blk_pos % inner
    cols_here = feature_width // rep_count
    rows_here = feature_width // blk_count
    bf16 = jnp.bfloat16
    inner_groups = [[o * inner + i for i in range(inner)] for o in range(outer)]
    outer_groups = [[o * inner + i for o in range(outer)] for i in range(inner)]

    def along_inner(value, turn):
        pairs = [
            (o * inner + i, o * inner + (i ^ turn)) for o in range(outer) for i in range(inner)
        ]
        return lax.ppermute(value, "blk", pairs) if turn else value

    def along_outer(value, turn):
        pairs = [
            (o * inner + i, (o ^ turn) * inner + i) for o in range(outer) for i in range(inner)
        ]
        return lax.ppermute(value, "blk", pairs) if turn else value

    def pick(value, index):
        return lax.dynamic_index_in_dim(value, index, 0, keepdims=False)

    def summed(arrived):
        return sum(part.astype(jnp.float32) for part in arrived)

    def dot(lhs, rhs, dims):
        return lax.dot_general(lhs, rhs, (dims, ((), ())), preferred_element_type=jnp.float32)

    hidden_part = jnp.maximum(
        lax.dynamic_slice_in_dim(hidden_pre, rep_pos * cols_here, cols_here, 1), 0
    )
    hidden_stack = lax.all_gather(
        hidden_part, "blk", axis=0, axis_index_groups=outer_groups, tiled=True
    )
    grad_part = lax.dynamic_slice_in_dim(cotangent, rep_pos * cols_here, cols_here, 1)
    grad_stack = lax.all_gather(
        grad_part, "blk", axis=0, axis_index_groups=inner_groups, tiled=True
    )

    order = jnp.arange(section_span, dtype=jnp.int32).reshape(per_core, inner).T.reshape(-1)
    hit = (adj_cols[0] % section_span)[None, :] == order[:, None]
    ordered = jnp.sum(
        jnp.where(hit[:, :, None, None], adj_vals[0][None].astype(jnp.float32), 0.0), axis=1
    ).astype(bf16)
    ordered = ordered.reshape(inner, per_core, tile_size, tile_size)
    arrived = jnp.stack(
        [along_inner(pick(ordered, inner_pos ^ t), t) for t in range(inner)]
    )
    everyone = lax.all_gather(arrived, "rep", axis=0)
    everyone = jnp.stack(
        [
            lax.dynamic_index_in_dim(everyone, inner_pos ^ i, 1, keepdims=False)
            for i in range(inner)
        ],
        1,
    )
    everyone = everyone.transpose(0, 1, 3, 2, 4).reshape(
        rep_count, inner * tile_size, per_core * tile_size
    )

    row_block = outer_pos * inner + jnp.repeat(jnp.arange(inner, dtype=jnp.int32), tile_size)
    pieces = []
    for o in range(outer):
        column = o * inner + inner_pos
        group = jnp.mod(row_block - column, blk_count) // section_span
        m = o % per_core
        piece = everyone[0, :, m * tile_size : (m + 1) * tile_size]
        for r in range(1, rep_count):
            other = everyone[r, :, m * tile_size : (m + 1) * tile_size]
            piece = jnp.where((group == r)[:, None], other, piece)
        pieces.append(piece)
    block = jnp.concatenate(pieces, 1)

    back_stack = dot(block, grad_stack, ((0,), (0,))).astype(bf16)
    back_part = lax.psum_scatter(
        back_stack, "blk", scatter_dimension=0, axis_index_groups=outer_groups, tiled=True
    )

    mixed_t = dot(hidden_stack, block, ((0,), (1,))).astype(bf16)
    by_group = mixed_t.reshape(per_core, inner, rows_here, inner * tile_size)
    by_group = by_group.transpose(1, 0, 2, 3).reshape(
        inner, per_core * rows_here, inner * tile_size
    )
    mixed = dot(block, hidden_stack, ((1,), (0,))).astype(bf16)
    mixed = mixed.reshape(inner, tile_size, cols_here)
    mixed_cols = summed([along_inner(pick(by_group, inner_pos ^ t), t) for t in range(inner)])
    mixed_cols = mixed_cols.astype(bf16)
    mixed_rows = summed([along_inner(pick(mixed, inner_pos ^ t), t) for t in range(inner)])
    mixed_rows = mixed_rows.astype(bf16)

    mixed_cols = lax.all_gather(mixed_cols, "rep", axis=0, tiled=True)
    weight_part = dot(mixed_cols, grad_stack, ((1,), (0,))).astype(bf16)
    weight_part = weight_part.reshape(outer, rows_here, cols_here)
    grad_weight = summed([along_outer(pick(weight_part, outer_pos ^ t), t) for t in range(outer)])

    mixed_rows = lax.all_gather(mixed_rows, "rep", axis=1, tiled=True)
    w_columns = lax.dynamic_slice_in_dim(w_out, rep_pos * cols_here, cols_here, 1)
    out_part = dot(mixed_rows, w_columns, ((1,), (0,))).astype(bf16)

    back_full = lax.all_gather(back_part, "rep", axis=1, tiled=True)
    w_rows = lax.dynamic_slice_in_dim(w_out, rep_pos * cols_here, cols_here, 0)
    grad_in = dot(back_full, w_rows, ((1,), (1,)))
    pre_part = lax.dynamic_slice_in_dim(hidden_pre, rep_pos * cols_here, cols_here, 1)
    grad_pre = jnp.where(pre_part > 0, grad_in, 0.0).astype(bf16)
    return (out_part, grad_weight, grad_pre)


def solution(mesh):
    placed = (P("blk", None), P("blk", "rep", None, None), P("blk", "rep"), P(), P("blk", None))
    return jax.shard_map(
        shards,
        mesh=mesh,
        in_specs=placed,
        out_specs=(P("blk", "rep"), P("blk", "rep"), P("blk", "rep")),
        check_vma=False,
    )
```

```python
import jax
import jax.numpy as jnp
from jax import lax
from jax.sharding import PartitionSpec as P


def shards(hidden_pre, adj_vals, adj_cols, w_out, cotangent):
    feature_width = hidden_pre.shape[1]
    tile_size = adj_vals.shape[2]
    blk_count = lax.axis_size("blk")
    rep_count = lax.axis_size("rep")
    section_span = blk_count // rep_count
    side = 1 << ((blk_count.bit_length() - 1) // 2)
    per_core = section_span // side
    groups = rep_count // 2
    wide = feature_width // groups
    rows_here = feature_width // blk_count
    half = wide // 2
    blk_pos = lax.axis_index("blk")
    rep_pos = lax.axis_index("rep")
    outer_pos, inner_pos = blk_pos // side, blk_pos % side
    role, group = rep_pos % 2, rep_pos // 2
    first_role = role == 0
    mates = [[g * 2 + r for g in range(groups)] for r in range(2)]
    bf16 = jnp.bfloat16
    turns = range(side)

    def routed(value, *routes):
        pairs = []
        for source_role, target in routes:
            for o in turns:
                for i in turns:
                    to_o, to_i, to_role = target(o, i)
                    for g in range(groups):
                        pairs.append(
                            (
                                (o * side + i) * rep_count + g * 2 + source_role,
                                (to_o * side + to_i) * rep_count + g * 2 + to_role,
                            )
                        )
        return lax.ppermute(value, ("blk", "rep"), pairs)

    def dot(lhs, rhs, dims):
        return lax.dot_general(lhs, rhs, (dims, ((), ())), preferred_element_type=jnp.float32)

    def summed(parts):
        return sum(part.astype(jnp.float32) for part in parts)

    def group_part(value, axis):
        if groups == 1:
            return value
        return lax.dynamic_slice_in_dim(value, group * wide, wide, axis)

    def all_groups(value):
        if groups == 1:
            return value
        return lax.all_gather(value, "rep", axis=0, tiled=True, axis_index_groups=mates)

    hidden_part = group_part(hidden_pre, 1)
    own = jnp.where(first_role, jnp.maximum(hidden_part, 0), group_part(cotangent, 1))
    stack = [own]
    for t in turns[1:]:
        stack.append(
            routed(own, (0, lambda o, i: (o ^ t, i, 0)), (1, lambda o, i: (o, i ^ t, 1)))
        )
    stack = jnp.concatenate(stack, 0)

    columns = adj_cols[0]
    place = ((columns % side) ^ inner_pos) * per_core + ((columns // side) ^ outer_pos) % per_core
    hit = place[None, :] == jnp.arange(section_span, dtype=jnp.int32)[:, None]
    ordered = jnp.sum(
        jnp.where(hit[:, :, None, None], adj_vals[0][None].astype(jnp.float32), 0.0), axis=1
    ).astype(bf16)
    ordered = ordered.reshape(side, per_core, tile_size, tile_size).transpose(0, 2, 1, 3)
    ordered = ordered.reshape(side, tile_size, per_core * tile_size)
    arrived = [ordered[0]]
    for t in turns[1:]:
        arrived.append(
            routed(ordered[t], *[(r, lambda o, i, r=r: (o, i ^ t, r)) for r in range(2)])
        )
    everyone = lax.all_gather(jnp.concatenate(arrived, 0), "rep", axis=0)

    turn_of_row = jnp.repeat(jnp.arange(side, dtype=jnp.int32), tile_size)
    row_block = outer_pos * side + (inner_pos ^ turn_of_row)
    pieces = []
    for e in turns:
        holder = jnp.mod(row_block - (outer_pos ^ e) * side - inner_pos, blk_count) // section_span
        m = e % per_core
        piece = everyone[0, :, m * tile_size : (m + 1) * tile_size]
        for r in range(1, rep_count):
            other = everyone[r, :, m * tile_size : (m + 1) * tile_size]
            piece = jnp.where((holder == r)[:, None], other, piece)
        pieces.append(piece)
    block = jnp.concatenate(pieces, 1)
    block = jnp.where(first_role, block, block.T)

    product = dot(stack, block, ((0,), (1,))).astype(bf16)
    parts = [product[:, t * tile_size : (t + 1) * tile_size] for t in turns]
    outer_share = side // groups
    by_owner = product.reshape(outer_share, side, rows_here, side * tile_size)
    sums = []
    for t in turns:
        chosen = lax.dynamic_index_in_dim(by_owner, inner_pos ^ t, 1, keepdims=False)
        chosen = chosen.reshape(outer_share * rows_here, side * tile_size)
        chosen = jnp.concatenate(
            [chosen[:, (u ^ t) * tile_size : ((u ^ t) + 1) * tile_size] for u in turns], 0
        )
        sums.append(
            routed(
                jnp.where(first_role, chosen, parts[t]),
                (0, lambda o, i: (o, i ^ t, 1)),
                (1, lambda o, i: (o ^ t, i, 0)),
            )
        )
    crossed = summed(sums).astype(bf16)
    rows_sum = summed(
        [parts[0]] + [routed(parts[t], (0, lambda o, i: (o, i ^ t, 0))) for t in turns[1:]]
    ).astype(bf16)

    share = outer_share * rows_here
    mixed = jnp.concatenate([crossed[u * share : (u + 1) * share] for u in turns], 1)
    weight_part = dot(all_groups(mixed), stack, ((1,), (0,))).astype(bf16)
    weight_part = weight_part.reshape(side, rows_here, wide)
    weight_sum = []
    for t in turns:
        chosen = lax.dynamic_index_in_dim(weight_part, outer_pos ^ t, 0, keepdims=False)
        weight_sum.append(routed(chosen, (1, lambda o, i: (o ^ t, i, 1))) if t else chosen)
    weight_sum = summed(weight_sum)

    out_wide = dot(all_groups(rows_sum), group_part(w_out, 1), ((0,), (0,))).astype(bf16)
    grad_in = dot(all_groups(crossed), group_part(w_out, 0), ((0,), (1,)))
    pre_wide = jnp.where(hidden_part > 0, grad_in, 0.0).astype(bf16)
    both = jnp.concatenate([out_wide, pre_wide], 0)
    both = jnp.where(
        first_role, both[:, :half], routed(both[:, half:], (0, lambda o, i: (o, i, 1)))
    )
    grad_weight = jnp.where(
        first_role,
        routed(weight_sum[:, :half], (1, lambda o, i: (o, i, 0))),
        weight_sum[:, half:],
    )
    return (both[:tile_size], grad_weight, both[tile_size:])


def solution(mesh):
    placed = (P("blk", None), P("blk", "rep", None, None), P("blk", "rep"), P(), P("blk", None))
    return jax.shard_map(
        shards,
        mesh=mesh,
        in_specs=placed,
        out_specs=(P("blk", "rep"), P("blk", "rep"), P("blk", "rep")),
        check_vma=False,
    )
```

```python
import jax
import jax.numpy as jnp
from jax import lax
from jax.sharding import PartitionSpec as P


def shards(hidden_pre, adj_vals, adj_cols, w_out, cotangent):
    feature_width = hidden_pre.shape[1]
    tile_size = adj_vals.shape[2]
    blk_count = lax.axis_size("blk")
    rep_count = lax.axis_size("rep")
    section_span = blk_count // rep_count
    side = 1 << ((blk_count.bit_length() - 1) // 2)
    per_core = section_span // side
    blk_pos = lax.axis_index("blk")
    rep_pos = lax.axis_index("rep")
    outer_pos, inner_pos = blk_pos // side, blk_pos % side
    cols_here = feature_width // rep_count
    rows_here = feature_width // blk_count
    bf16 = jnp.bfloat16
    turns = range(side)

    def along_inner(value, turn):
        pairs = [(o * side + i, o * side + (i ^ turn)) for o in turns for i in turns]
        return lax.ppermute(value, "blk", pairs) if turn else value

    def along_outer(value, turn):
        pairs = [(o * side + i, (o ^ turn) * side + i) for o in turns for i in turns]
        return lax.ppermute(value, "blk", pairs) if turn else value

    def dot(lhs, rhs, dims):
        return lax.dot_general(lhs, rhs, (dims, ((), ())), preferred_element_type=jnp.float32)

    def summed(parts):
        return sum(part.astype(jnp.float32) for part in parts)

    def lanes(value, index):
        return value[:, index * tile_size : (index + 1) * tile_size]

    hidden_part = jnp.maximum(
        lax.dynamic_slice_in_dim(hidden_pre, rep_pos * cols_here, cols_here, 1), 0
    )
    hidden_stack = jnp.concatenate([along_outer(hidden_part, e) for e in turns], 0)

    columns = adj_cols[0]
    place = ((columns % side) ^ inner_pos) * per_core + ((columns // side) ^ outer_pos) % per_core
    hit = place[None, :] == jnp.arange(section_span, dtype=jnp.int32)[:, None]
    ordered = jnp.sum(
        jnp.where(hit[:, :, None, None], adj_vals[0][None].astype(jnp.float32), 0.0), axis=1
    ).astype(bf16)
    grad_part = lax.dynamic_slice_in_dim(cotangent, rep_pos * cols_here, cols_here, 1)
    arrived = []
    for t in turns:
        message = [ordered[t * per_core + m] for m in range(per_core)] + [grad_part]
        arrived.append(along_inner(jnp.concatenate(message, 1), t))
    arrived = jnp.concatenate(arrived, 0)
    held = per_core * tile_size
    grad_stack = arrived[:, held:]
    everyone = lax.all_gather(arrived[:, :held], "rep", axis=0)

    turn_of_row = jnp.repeat(jnp.arange(side, dtype=jnp.int32), tile_size)
    row_block = outer_pos * side + (inner_pos ^ turn_of_row)
    pieces = []
    for e in turns:
        holder = jnp.mod(row_block - (outer_pos ^ e) * side - inner_pos, blk_count) // section_span
        piece = lanes(everyone[0], e % per_core)
        for r in range(1, rep_count):
            piece = jnp.where((holder == r)[:, None], lanes(everyone[r], e % per_core), piece)
        pieces.append(piece)
    block = jnp.concatenate(pieces, 1)

    back_stack = dot(block, grad_stack, ((0,), (0,))).astype(bf16)
    back_part = summed(
        [along_outer(back_stack[e * tile_size : (e + 1) * tile_size], e) for e in turns]
    ).astype(bf16)

    mixed = dot(hidden_stack, block, ((0,), (1,))).astype(bf16)
    share = cols_here // side
    by_owner = mixed.reshape(share // rows_here, side, rows_here, side * tile_size)
    exchanged = []
    for t in turns:
        chosen = lax.dynamic_index_in_dim(by_owner, inner_pos ^ t, 1, keepdims=False)
        chosen = chosen.reshape(share, side * tile_size)
        message = [lanes(mixed, t)] + [lanes(chosen, u ^ t) for u in turns]
        exchanged.append(along_inner(jnp.concatenate(message, 0), t))
    exchanged = summed(exchanged).astype(bf16)
    exchanged = lax.all_gather(exchanged, "rep", axis=0)
    mixed_rows = exchanged[:, :cols_here].reshape(feature_width, tile_size)
    mixed_cols = exchanged[:, cols_here:].reshape(rep_count, side, share, tile_size)
    mixed_cols = mixed_cols.transpose(0, 2, 1, 3).reshape(rep_count * share, side * tile_size)

    weight_part = dot(mixed_cols, grad_stack, ((1,), (0,))).astype(bf16)
    weight_part = weight_part.reshape(side, rows_here, cols_here)
    grad_weight = summed(
        [
            along_outer(
                lax.dynamic_index_in_dim(weight_part, outer_pos ^ t, 0, keepdims=False), t
            )
            for t in turns
        ]
    )

    w_columns = lax.dynamic_slice_in_dim(w_out, rep_pos * cols_here, cols_here, 1)
    out_part = dot(mixed_rows, w_columns, ((0,), (0,))).astype(bf16)

    back_full = lax.all_gather(back_part, "rep", axis=1, tiled=True)
    w_rows = lax.dynamic_slice_in_dim(w_out, rep_pos * cols_here, cols_here, 0)
    grad_in = dot(back_full, w_rows, ((1,), (1,)))
    pre_part = lax.dynamic_slice_in_dim(hidden_pre, rep_pos * cols_here, cols_here, 1)
    grad_pre = jnp.where(pre_part > 0, grad_in, 0.0).astype(bf16)
    return (out_part, grad_weight, grad_pre)


def solution(mesh):
    placed = (P("blk", None), P("blk", "rep", None, None), P("blk", "rep"), P(), P("blk", None))
    return jax.shard_map(
        shards,
        mesh=mesh,
        in_specs=placed,
        out_specs=(P("blk", "rep"), P("blk", "rep"), P("blk", "rep")),
        check_vma=False,
    )
```

```python
import functools

import jax
import jax.numpy as jnp
from jax import lax
from jax.experimental import pallas as pl
from jax.experimental.pallas import tpu as pltpu
from jax.sharding import PartitionSpec as P


def prepare_kernel(side, per_core, place_ref, cols_ref, hidden_ref, cot_ref, vals_ref, *outs):
    hidden_out, cot_out, blocks_out = outs
    hidden_out[...] = jnp.maximum(hidden_ref[...], 0)
    cot_out[...] = cot_ref[...]
    slots, spans = vals_ref.shape[1], blocks_out.shape[0]
    if slots < spans:
        blocks_out[...] = jnp.zeros_like(blocks_out)
    for k in range(slots):
        column = cols_ref[0, k]
        turn = (column % side) ^ place_ref[1]
        level = (column // side) ^ place_ref[2]
        blocks_out[turn * per_core + level % per_core] = vals_ref[0, k]


def prepared(hidden_pre, cotangent, adj_vals, adj_cols, place, side, per_core, cols_here):
    tile_size = hidden_pre.shape[0]
    part = pl.BlockSpec((tile_size, cols_here), lambda i, place, cols: (0, place[0]))
    whole = pl.BlockSpec((tile_size, cols_here), lambda i, place, cols: (0, 0))
    spans = side * per_core
    return pl.pallas_call(
        functools.partial(prepare_kernel, side, per_core),
        grid_spec=pltpu.PrefetchScalarGridSpec(
            num_scalar_prefetch=2,
            grid=(1,),
            in_specs=[
                part,
                part,
                pl.BlockSpec(adj_vals.shape, lambda i, place, cols: (0, 0, 0, 0)),
            ],
            out_specs=[
                whole,
                whole,
                pl.BlockSpec((spans, tile_size, tile_size), lambda i, place, cols: (0, 0, 0)),
            ],
        ),
        out_shape=[
            jax.ShapeDtypeStruct((tile_size, cols_here), jnp.bfloat16),
            jax.ShapeDtypeStruct((tile_size, cols_here), jnp.bfloat16),
            jax.ShapeDtypeStruct((spans, tile_size, tile_size), jnp.bfloat16),
        ],
    )(place, adj_cols, hidden_pre, cotangent, adj_vals)


def shards(hidden_pre, adj_vals, adj_cols, w_out, cotangent):
    feature_width = hidden_pre.shape[1]
    tile_size = adj_vals.shape[2]
    blk_count = lax.axis_size("blk")
    rep_count = lax.axis_size("rep")
    section_span = blk_count // rep_count
    bits = (blk_count.bit_length() - 1) // 2
    side = 1 << bits
    per_core = section_span // side
    blk_pos = lax.axis_index("blk")
    rep_pos = lax.axis_index("rep")
    outer_pos, inner_pos = blk_pos // side, blk_pos % side
    cols_here = feature_width // rep_count
    rows_here = feature_width // blk_count
    bf16 = jnp.bfloat16
    turns = range(side)
    rising = [1 << b for b in range(bits)]
    falling = rising[::-1]

    def along_inner(value, turn):
        pairs = [(o * side + i, o * side + (i ^ turn)) for o in turns for i in turns]
        return lax.ppermute(value, "blk", pairs) if turn else value

    def along_outer(value, turn):
        pairs = [(o * side + i, (o ^ turn) * side + i) for o in turns for i in turns]
        return lax.ppermute(value, "blk", pairs) if turn else value

    def doubled(value, move, order):
        held = {0: value}
        for bit in order:
            keys = list(held)
            size = held[keys[0]].shape[0]
            got = move(jnp.concatenate([held[k] for k in keys], 0), bit)
            for n, k in enumerate(keys):
                held[k ^ bit] = got[n * size : (n + 1) * size]
        return jnp.concatenate([held[k] for k in turns], 0)

    def halved(parts, move, order):
        parts = dict(enumerate(parts))
        size = parts[0].shape[0]
        for bit in order:
            keys = [k for k in parts if not k & bit]
            sent = jnp.concatenate([parts[k ^ bit].astype(bf16) for k in keys], 0)
            got = move(sent, bit)
            parts = {
                k: parts[k].astype(jnp.float32)
                + got[n * size : (n + 1) * size].astype(jnp.float32)
                for n, k in enumerate(keys)
            }
        return parts[0]

    def dealt(parts, move, order):
        held = {(0, k): part for k, part in enumerate(parts)}
        size = parts[0].shape[0]
        for bit in order:
            keys = [key for key in held if not key[1] & bit]
            got = move(jnp.concatenate([held[s, k ^ bit] for s, k in keys], 0), bit)
            kept = {key: held[key] for key in keys}
            for n, (s, k) in enumerate(keys):
                kept[s ^ bit, k] = got[n * size : (n + 1) * size]
            held = kept
        return [held[s, 0] for s in turns]

    def dot(lhs, rhs, dims):
        return lax.dot_general(lhs, rhs, (dims, ((), ())), preferred_element_type=jnp.float32)

    def after(value, other):
        return lax.optimization_barrier((value, other))[0]

    def lanes(value, index):
        return value[:, index * tile_size : (index + 1) * tile_size]

    place = jnp.stack([rep_pos, inner_pos, outer_pos]).astype(jnp.int32)
    hidden_part, grad_part, ordered = prepared(
        hidden_pre, cotangent, adj_vals, adj_cols, place, side, per_core, cols_here
    )
    hidden_stack = doubled(hidden_part, along_outer, falling)
    arrived = dealt(
        [ordered[t * per_core : (t + 1) * per_core] for t in turns], along_inner, rising
    )
    grad_stack = doubled(grad_part, along_inner, falling)
    everyone = lax.all_gather(jnp.concatenate(arrived, 0), "rep", axis=0)

    rows = []
    for t in turns:
        row_block = outer_pos * side + (inner_pos ^ t)
        row = []
        for e in turns:
            column_block = (outer_pos ^ e) * side + inner_pos
            holder = jnp.mod(row_block - column_block, blk_count) // section_span
            index = t * per_core + e % per_core
            piece = everyone[0, index]
            for r in range(1, rep_count):
                piece = jnp.where(holder == r, everyone[r, index], piece)
            row.append(piece)
        rows.append(jnp.concatenate(row, 1))
    block = jnp.concatenate(rows, 0)

    mixed = dot(hidden_stack, block, ((0,), (1,))).astype(bf16)
    share = cols_here // side
    by_owner = mixed.reshape(share // rows_here, side, rows_here, side * tile_size)
    mixed_cols = 0.0
    for t in turns:
        chosen = lax.dynamic_index_in_dim(by_owner, inner_pos ^ t, 1, keepdims=False)
        chosen = chosen.reshape(share, side * tile_size)
        chosen = jnp.concatenate([lanes(chosen, u ^ t) for u in turns], 1)
        mixed_cols = mixed_cols + along_inner(chosen, t).astype(jnp.float32)
    mixed_cols = lax.all_gather(mixed_cols.astype(bf16), "rep", axis=0, tiled=True)
    weight_part = dot(mixed_cols, grad_stack, ((1,), (0,)))
    weight_part = weight_part.reshape(side, rows_here, cols_here)
    weight_part = [
        lax.dynamic_index_in_dim(weight_part, outer_pos ^ t, 0, keepdims=False) for t in turns
    ]
    grad_weight = halved(weight_part, along_outer, rising)

    back_stack = dot(after(block, mixed), grad_stack, ((0,), (0,)))
    back_part = halved(
        [back_stack[e * tile_size : (e + 1) * tile_size] for e in turns], along_outer, rising
    ).astype(bf16)

    mixed_rows = halved([lanes(mixed, t) for t in turns], along_inner, rising).astype(bf16)
    mixed_rows = lax.all_gather(after(mixed_rows, weight_part[0]), "rep", axis=0, tiled=True)
    w_columns = lax.dynamic_slice_in_dim(w_out, rep_pos * cols_here, cols_here, 1)
    out_part = dot(mixed_rows, w_columns, ((0,), (0,))).astype(bf16)

    back_full = lax.all_gather(after(back_part, weight_part[0]), "rep", axis=1, tiled=True)
    w_rows = lax.dynamic_slice_in_dim(w_out, rep_pos * cols_here, cols_here, 0)
    grad_in = dot(back_full, w_rows, ((1,), (1,)))
    pre_part = lax.dynamic_slice_in_dim(hidden_pre, rep_pos * cols_here, cols_here, 1)
    grad_pre = jnp.where(pre_part > 0, grad_in, 0.0).astype(bf16)
    return (out_part, grad_weight, grad_pre)


def solution(mesh):
    placed = (P("blk", None), P("blk", "rep", None, None), P("blk", "rep"), P(), P("blk", None))
    return jax.shard_map(
        shards,
        mesh=mesh,
        in_specs=placed,
        out_specs=(P("blk", "rep"), P("blk", "rep"), P("blk", "rep")),
        check_vma=False,
    )
```

```python
import jax
import jax.numpy as jnp
from jax import lax
from jax.sharding import PartitionSpec as P


def shards(hidden_pre, adj_vals, adj_cols, w_out, cotangent):
    feature_width = hidden_pre.shape[1]
    slots, tile_size = adj_vals.shape[1:3]
    blk_count = lax.axis_size("blk")
    rep_count = lax.axis_size("rep")
    section_span = blk_count // rep_count
    bits = (blk_count.bit_length() - 1) // 2
    side = 1 << bits
    per_core = section_span // side
    blk_pos = lax.axis_index("blk")
    rep_pos = lax.axis_index("rep")
    outer_pos, inner_pos = blk_pos >> bits, blk_pos & (side - 1)
    span_bits = section_span.bit_length() - 1
    cols_here = feature_width // rep_count
    rows_here = feature_width // blk_count
    bf16 = jnp.bfloat16
    turns = range(side)
    rising = [1 << b for b in range(bits)]

    def along_inner(value, turn):
        pairs = [(o * side + i, o * side + (i ^ turn)) for o in turns for i in turns]
        return lax.ppermute(value, "blk", pairs) if turn else value

    def along_outer(value, turn):
        pairs = [(o * side + i, (o ^ turn) * side + i) for o in turns for i in turns]
        return lax.ppermute(value, "blk", pairs) if turn else value

    def halved(parts, move, order, last_after):
        parts = dict(enumerate(parts))
        size = parts[0].shape[0]
        for bit in order:
            keys = [k for k in parts if not k & bit]
            sent = jnp.concatenate([parts[k ^ bit].astype(bf16) for k in keys], 0)
            got = move(after(sent, last_after) if bit == order[-1] else sent, bit)
            parts = {
                k: parts[k].astype(jnp.float32)
                + got[n * size : (n + 1) * size].astype(jnp.float32)
                for n, k in enumerate(keys)
            }
        return parts[0]

    def dot(lhs, rhs, dims):
        return lax.dot_general(lhs, rhs, (dims, ((), ())), preferred_element_type=jnp.float32)

    def after(value, *others):
        return lax.optimization_barrier((value,) + others)[0]

    def lanes(value, index):
        return value[:, index * tile_size : (index + 1) * tile_size]

    hidden_part = jnp.maximum(
        lax.dynamic_slice_in_dim(hidden_pre, rep_pos * cols_here, cols_here, 1), 0
    )
    hidden_stack = jnp.concatenate([along_outer(hidden_part, e) for e in turns], 0)

    columns = adj_cols[0]
    turn_of = (columns & (side - 1)) ^ inner_pos
    level_of = (columns >> bits) ^ outer_pos
    place = turn_of * per_core + (level_of & (per_core - 1))
    hit = place[None, :] == jnp.arange(section_span, dtype=jnp.int32)[:, None]
    ordered = jnp.zeros((section_span, tile_size, tile_size), bf16)
    for k in range(slots):
        ordered = jnp.where(hit[:, k, None, None], adj_vals[0, k][None], ordered)
    arrived = []
    for t in turns:
        message = ordered[t * per_core : (t + 1) * per_core]
        if t > 2:
            message = after(message, arrived[t - 2])
        arrived.append(along_inner(message, t))
    grad_part = lax.dynamic_slice_in_dim(cotangent, rep_pos * cols_here, cols_here, 1)
    grad_part = after(grad_part, arrived[2])
    grad_stack = jnp.concatenate([along_inner(grad_part, t) for t in turns], 0)
    everyone = lax.all_gather(jnp.concatenate(arrived, 0), "rep", axis=0)

    rows = []
    for t in turns:
        row_block = outer_pos * side + (inner_pos ^ t)
        row = []
        for e in turns:
            column_block = (outer_pos ^ e) * side + inner_pos
            holder = ((row_block - column_block) & (blk_count - 1)) >> span_bits
            index = t * per_core + e % per_core
            piece = everyone[0, index]
            for r in range(1, rep_count):
                piece = jnp.where(holder == r, everyone[r, index], piece)
            row.append(piece)
        rows.append(jnp.concatenate(row, 1))
    block = jnp.concatenate(rows, 0)

    mixed = dot(hidden_stack, block, ((0,), (1,))).astype(bf16)
    share = cols_here // side
    by_owner = mixed.reshape(share // rows_here, side, rows_here, side * tile_size)
    mixed_cols = []
    for t in turns:
        chosen = lax.dynamic_index_in_dim(by_owner, inner_pos ^ t, 1, keepdims=False)
        chosen = chosen.reshape(share, side * tile_size)
        chosen = jnp.concatenate([lanes(chosen, u ^ t) for u in turns], 1)
        mixed_cols.append(along_inner(chosen, t))
    first_col = mixed_cols[1]
    mixed_cols = sum(part.astype(jnp.float32) for part in mixed_cols).astype(bf16)
    mixed_cols = lax.all_gather(mixed_cols, "rep", axis=0, tiled=True)
    weight_part = dot(mixed_cols, grad_stack, ((1,), (0,))).astype(bf16)
    by_outer = weight_part.reshape(side, rows_here, cols_here)
    weight_got = [
        along_outer(lax.dynamic_index_in_dim(by_outer, outer_pos ^ t, 0, keepdims=False), t)
        for t in turns
    ]

    back = dot(after(grad_stack, mixed), block, ((0,), (0,)))
    back = halved([lanes(back, e) for e in turns], along_outer, rising, weight_part)
    rows_sum = halved(
        [lanes(after(mixed, first_col), t) for t in turns], along_inner, rising, weight_part
    )
    both = jnp.concatenate([rows_sum, back], 0).astype(bf16)
    both = lax.all_gather(both, "rep", axis=0)
    mixed_rows = both[:, :cols_here].reshape(feature_width, tile_size)
    back_full = both[:, cols_here:].reshape(feature_width, tile_size)

    w_columns = lax.dynamic_slice_in_dim(w_out, rep_pos * cols_here, cols_here, 1)
    out_part = dot(mixed_rows, w_columns, ((0,), (0,))).astype(bf16)
    w_rows = lax.dynamic_slice_in_dim(w_out, rep_pos * cols_here, cols_here, 0)
    grad_in = dot(back_full, w_rows, ((0,), (1,)))
    pre_part = lax.dynamic_slice_in_dim(hidden_pre, rep_pos * cols_here, cols_here, 1)
    grad_pre = jnp.where(pre_part > 0, grad_in, 0.0).astype(bf16)

    weight_got[1:], out_part, grad_pre = lax.optimization_barrier(
        (weight_got[1:], out_part, grad_pre)
    )
    grad_weight = sum(part.astype(jnp.float32) for part in weight_got)
    return (out_part, grad_weight, grad_pre)


def solution(mesh):
    placed = (P("blk", None), P("blk", "rep", None, None), P("blk", "rep"), P(), P("blk", None))
    return jax.shard_map(
        shards,
        mesh=mesh,
        in_specs=placed,
        out_specs=(P("blk", "rep"), P("blk", "rep"), P("blk", "rep")),
        check_vma=False,
    )
```

```python
import jax
import jax.numpy as jnp
from jax import lax
from jax.sharding import PartitionSpec as P


def shards(hidden_pre, adj_vals, adj_cols, w_out, cotangent):
    feature_width = hidden_pre.shape[1]
    slots, tile_size = adj_vals.shape[1:3]
    blk_count = lax.axis_size("blk")
    rep_count = lax.axis_size("rep")
    section_span = blk_count // rep_count
    bits = (blk_count.bit_length() - 1) // 2
    side = 1 << bits
    per_core = section_span // side
    blk_pos = lax.axis_index("blk")
    rep_pos = lax.axis_index("rep")
    outer_pos, inner_pos = blk_pos >> bits, blk_pos & (side - 1)
    span_bits = section_span.bit_length() - 1
    cols_here = feature_width // rep_count
    rows_here = feature_width // blk_count
    bf16 = jnp.bfloat16
    turns = range(side)
    rising = [1 << b for b in range(bits)]

    def along_inner(value, turn):
        pairs = [(o * side + i, o * side + (i ^ turn)) for o in turns for i in turns]
        return lax.ppermute(value, "blk", pairs) if turn else value

    def along_outer(value, turn):
        pairs = [(o * side + i, (o ^ turn) * side + i) for o in turns for i in turns]
        return lax.ppermute(value, "blk", pairs) if turn else value

    def halved(parts, move, order):
        parts = dict(enumerate(parts))
        size = parts[0].shape[0]
        for bit in order:
            keys = [k for k in parts if not k & bit]
            sent = jnp.concatenate([parts[k ^ bit].astype(bf16) for k in keys], 0)
            got = move(sent, bit)
            parts = {
                k: parts[k].astype(jnp.float32)
                + got[n * size : (n + 1) * size].astype(jnp.float32)
                for n, k in enumerate(keys)
            }
        return parts

    def dot(lhs, rhs, dims):
        return lax.dot_general(lhs, rhs, (dims, ((), ())), preferred_element_type=jnp.float32)

    def after(value, *others):
        return lax.optimization_barrier((value,) + others)[0]

    def lanes(value, index):
        return value[:, index * tile_size : (index + 1) * tile_size]

    hidden_part = jnp.maximum(
        lax.dynamic_slice_in_dim(hidden_pre, rep_pos * cols_here, cols_here, 1), 0
    )
    held = {0: hidden_part}
    for bit in rising[::-1]:
        keys = list(held)
        got = along_outer(jnp.concatenate([held[k] for k in keys], 0), bit)
        for n, k in enumerate(keys):
            held[k ^ bit] = got[n * tile_size : (n + 1) * tile_size]
    hidden_stack = jnp.concatenate([held[e] for e in turns], 0)

    columns = after(adj_cols, hidden_part)[0]
    turn_of = (columns & (side - 1)) ^ inner_pos
    level_of = (columns >> bits) ^ outer_pos
    place = turn_of * per_core + (level_of & (per_core - 1))
    hit = place[None, :] == jnp.arange(section_span, dtype=jnp.int32)[:, None]
    ordered = jnp.zeros((section_span, tile_size, tile_size), bf16)
    for k in range(slots):
        ordered = jnp.where(hit[:, k, None, None], adj_vals[0, k][None], ordered)
    arrived = []
    for t in turns:
        message = ordered[t * per_core : (t + 1) * per_core]
        arrived.append(along_inner(message, t))
    grad_part = lax.dynamic_slice_in_dim(cotangent, rep_pos * cols_here, cols_here, 1)
    grad_part = after(grad_part, *arrived[1:])
    grad_stack = jnp.concatenate([along_inner(grad_part, t) for t in turns], 0)
    everyone = lax.all_gather(jnp.concatenate(arrived, 0), "rep", axis=0)

    rows = []
    for t in turns:
        row_block = outer_pos * side + (inner_pos ^ t)
        row = []
        for e in turns:
            column_block = (outer_pos ^ e) * side + inner_pos
            holder = ((row_block - column_block) & (blk_count - 1)) >> span_bits
            index = t * per_core + e % per_core
            piece = everyone[0, index]
            for r in range(1, rep_count):
                piece = jnp.where(holder == r, everyone[r, index], piece)
            row.append(piece)
        rows.append(jnp.concatenate(row, 1))
    block = jnp.concatenate(rows, 0)

    mixed = dot(hidden_stack, block, ((0,), (1,))).astype(bf16)
    share = cols_here // side
    by_owner = mixed.reshape(share // rows_here, side, rows_here, side * tile_size)
    mixed_cols = []
    for t in turns:
        chosen = lax.dynamic_index_in_dim(by_owner, inner_pos ^ t, 1, keepdims=False)
        chosen = chosen.reshape(share, side * tile_size)
        chosen = jnp.concatenate([lanes(chosen, u ^ t) for u in turns], 1)
        mixed_cols.append(along_inner(chosen, t))
    mixed_cols = sum(part.astype(jnp.float32) for part in mixed_cols).astype(bf16)
    mixed_cols = lax.all_gather(mixed_cols, "rep", axis=0, tiled=True)
    back = dot(after(grad_stack, mixed), block, ((0,), (0,)))
    rows = after(mixed, back)
    back = halved([lanes(back, e) for e in turns], along_outer, rising[:-1])
    rows = halved([lanes(rows, t) for t in turns], along_inner, rising[:-1])

    mixed_cols, back[0] = lax.optimization_barrier((mixed_cols, back[0]))
    weight_part = dot(mixed_cols, grad_stack, ((1,), (0,))).astype(bf16)
    by_outer = weight_part.reshape(side, rows_here, cols_here)
    weight_got = [
        along_outer(lax.dynamic_index_in_dim(by_outer, outer_pos ^ t, 0, keepdims=False), t)
        for t in turns
    ]

    last = rising[-1]
    back_got = along_outer(back[last].astype(bf16), last).astype(jnp.float32)
    rows_got = after(rows[last].astype(bf16), weight_part)
    rows_got = along_inner(rows_got, last).astype(jnp.float32)
    rows_sum, back = rows[0] + rows_got, back[0] + back_got
    both = jnp.concatenate([rows_sum, back], 0).astype(bf16)
    both = lax.all_gather(both, "rep", axis=0)
    mixed_rows = both[:, :cols_here].reshape(feature_width, tile_size)
    back_full = both[:, cols_here:].reshape(feature_width, tile_size)

    w_columns = lax.dynamic_slice_in_dim(w_out, rep_pos * cols_here, cols_here, 1)
    out_part = dot(mixed_rows, w_columns, ((0,), (0,))).astype(bf16)
    w_rows = lax.dynamic_slice_in_dim(w_out, rep_pos * cols_here, cols_here, 0)
    grad_in = dot(back_full, w_rows, ((0,), (1,)))
    pre_part = lax.dynamic_slice_in_dim(hidden_pre, rep_pos * cols_here, cols_here, 1)
    grad_pre = jnp.where(pre_part > 0, grad_in, 0.0).astype(bf16)

    weight_got[1:], out_part, grad_pre = lax.optimization_barrier(
        (weight_got[1:], out_part, grad_pre)
    )
    grad_weight = sum(part.astype(jnp.float32) for part in weight_got)
    return (out_part, grad_weight, grad_pre)


def solution(mesh):
    placed = (P("blk", None), P("blk", "rep", None, None), P("blk", "rep"), P(), P("blk", None))
    return jax.shard_map(
        shards,
        mesh=mesh,
        in_specs=placed,
        out_specs=(P("blk", "rep"), P("blk", "rep"), P("blk", "rep")),
        check_vma=False,
    )
```

```python
import jax
import jax.numpy as jnp
from jax import lax
from jax.sharding import PartitionSpec as P


def shards(hidden_pre, adj_vals, adj_cols, w_out, cotangent):
    feature_width = hidden_pre.shape[1]
    slots, tile_size = adj_vals.shape[1:3]
    blk_count = lax.axis_size("blk")
    rep_count = lax.axis_size("rep")
    section_span = blk_count // rep_count
    bits = (blk_count.bit_length() - 1) // 2
    side = 1 << bits
    per_core = section_span // side
    blk_pos = lax.axis_index("blk")
    rep_pos = lax.axis_index("rep")
    outer_pos, inner_pos = blk_pos >> bits, blk_pos & (side - 1)
    span_bits = section_span.bit_length() - 1
    cols_here = feature_width // rep_count
    rows_here = feature_width // blk_count
    bf16 = jnp.bfloat16
    turns = range(side)
    rising = [1 << b for b in range(bits)]

    def along_inner(value, turn):
        pairs = [(o * side + i, o * side + (i ^ turn)) for o in turns for i in turns]
        return lax.ppermute(value, "blk", pairs) if turn else value

    def along_outer(value, turn):
        pairs = [(o * side + i, (o ^ turn) * side + i) for o in turns for i in turns]
        return lax.ppermute(value, "blk", pairs) if turn else value

    def halved(parts, move, order):
        parts = dict(enumerate(parts))
        size = parts[0].shape[0]
        for bit in order:
            keys = [k for k in parts if not k & bit]
            sent = jnp.concatenate([parts[k ^ bit].astype(bf16) for k in keys], 0)
            got = move(sent, bit)
            parts = {
                k: parts[k].astype(jnp.float32)
                + got[n * size : (n + 1) * size].astype(jnp.float32)
                for n, k in enumerate(keys)
            }
        return parts

    def dot(lhs, rhs, dims):
        return lax.dot_general(lhs, rhs, (dims, ((), ())), preferred_element_type=jnp.float32)

    def after(value, *others):
        return lax.optimization_barrier((value,) + others)[0]

    def lanes(value, index):
        return value[:, index * tile_size : (index + 1) * tile_size]

    hidden_part = jnp.maximum(
        lax.dynamic_slice_in_dim(hidden_pre, rep_pos * cols_here, cols_here, 1), 0
    )
    hidden_stack = jnp.concatenate([along_outer(hidden_part, e) for e in turns], 0)

    columns = after(adj_cols, hidden_part)[0]
    turn_of = (columns & (side - 1)) ^ inner_pos
    level_of = (columns >> bits) ^ outer_pos
    place = turn_of * per_core + (level_of & (per_core - 1))
    hit = place[None, :] == jnp.arange(section_span, dtype=jnp.int32)[:, None]
    ordered = jnp.zeros((section_span, tile_size, tile_size), bf16)
    for k in range(slots):
        ordered = jnp.where(hit[:, k, None, None], adj_vals[0, k][None], ordered)
    everyone = lax.all_gather(ordered, "rep", axis=0)
    row_block = outer_pos * side + inner_pos
    rows = []
    for t in turns:
        row = []
        for e in turns:
            column_block = (outer_pos ^ e) * side + (inner_pos ^ t)
            holder = ((row_block - column_block) & (blk_count - 1)) >> span_bits
            index = t * per_core + e % per_core
            piece = everyone[0, index]
            for r in range(1, rep_count):
                piece = jnp.where(holder == r, everyone[r, index], piece)
            row.append(piece)
        rows.append(along_inner(jnp.concatenate(row, 1), t))
    block = jnp.concatenate(rows, 0)

    grad_part = lax.dynamic_slice_in_dim(cotangent, rep_pos * cols_here, cols_here, 1)
    grad_part = after(grad_part, rows[1])
    grad_stack = jnp.concatenate([along_inner(grad_part, t) for t in turns], 0)

    mixed = dot(hidden_stack, block, ((0,), (1,))).astype(bf16)
    share = cols_here // side
    by_owner = mixed.reshape(share // rows_here, side, rows_here, side * tile_size)
    mixed_cols = []
    for t in turns:
        chosen = lax.dynamic_index_in_dim(by_owner, inner_pos ^ t, 1, keepdims=False)
        chosen = chosen.reshape(share, side * tile_size)
        chosen = jnp.concatenate([lanes(chosen, u ^ t) for u in turns], 1)
        mixed_cols.append(along_inner(chosen, t))
    mixed_cols = sum(part.astype(jnp.float32) for part in mixed_cols).astype(bf16)
    back = dot(after(grad_stack, mixed), block, ((0,), (0,)))
    back = halved([lanes(back, e) for e in turns], along_outer, rising[:-1])
    rows = [lanes(after(mixed, mixed_cols), t) for t in turns]
    rows = halved(rows, along_inner, rising[:-1])

    mixed_cols = lax.all_gather(mixed_cols, "rep", axis=0, tiled=True)
    mixed_cols, back[0] = lax.optimization_barrier((mixed_cols, back[0]))
    weight_part = dot(mixed_cols, grad_stack, ((1,), (0,))).astype(bf16)
    by_outer = weight_part.reshape(side, rows_here, cols_here)
    weight_got = [
        along_outer(lax.dynamic_index_in_dim(by_outer, outer_pos ^ t, 0, keepdims=False), t)
        for t in turns
    ]

    last = rising[-1]
    back_got = along_outer(back[last].astype(bf16), last).astype(jnp.float32)
    rows_got = after(rows[last].astype(bf16), weight_part)
    rows_got = along_inner(rows_got, last).astype(jnp.float32)
    rows_sum, back = rows[0] + rows_got, back[0] + back_got
    both = jnp.concatenate([rows_sum, back], 0).astype(bf16)
    both = lax.all_gather(both, "rep", axis=0)
    mixed_rows = both[:, :cols_here].reshape(feature_width, tile_size)
    back_full = both[:, cols_here:].reshape(feature_width, tile_size)

    w_columns = lax.dynamic_slice_in_dim(w_out, rep_pos * cols_here, cols_here, 1)
    out_part = dot(mixed_rows, w_columns, ((0,), (0,))).astype(bf16)
    w_rows = lax.dynamic_slice_in_dim(w_out, rep_pos * cols_here, cols_here, 0)
    grad_in = dot(back_full, w_rows, ((0,), (1,)))
    pre_part = lax.dynamic_slice_in_dim(hidden_pre, rep_pos * cols_here, cols_here, 1)
    grad_pre = jnp.where(pre_part > 0, grad_in, 0.0).astype(bf16)

    weight_got[1:], out_part, grad_pre = lax.optimization_barrier(
        (weight_got[1:], out_part, grad_pre)
    )
    grad_weight = sum(part.astype(jnp.float32) for part in weight_got)
    return (out_part, grad_weight, grad_pre)


def solution(mesh):
    placed = (P("blk", None), P("blk", "rep", None, None), P("blk", "rep"), P(), P("blk", None))
    return jax.shard_map(
        shards,
        mesh=mesh,
        in_specs=placed,
        out_specs=(P("blk", "rep"), P("blk", "rep"), P("blk", "rep")),
        check_vma=False,
    )
```

```python
import jax
import jax.numpy as jnp
from jax import lax
from jax.sharding import PartitionSpec as P


def shards(hidden_pre, adj_vals, adj_cols, w_out, cotangent):
    feature_width = hidden_pre.shape[1]
    slots, tile_size = adj_vals.shape[1:3]
    blk_count = lax.axis_size("blk")
    rep_count = lax.axis_size("rep")
    section_span = blk_count // rep_count
    bits = (blk_count.bit_length() - 1) // 2
    side = 1 << bits
    per_core = section_span // side
    blk_pos = lax.axis_index("blk")
    rep_pos = lax.axis_index("rep")
    outer_pos, inner_pos = blk_pos >> bits, blk_pos & (side - 1)
    span_bits = section_span.bit_length() - 1
    cols_here = feature_width // rep_count
    rows_here = feature_width // blk_count
    bf16 = jnp.bfloat16
    turns = range(side)
    rising = [1 << b for b in range(bits)]

    def along_inner(value, turn):
        pairs = [(o * side + i, o * side + (i ^ turn)) for o in turns for i in turns]
        return lax.ppermute(value, "blk", pairs) if turn else value

    def along_outer(value, turn):
        pairs = [(o * side + i, (o ^ turn) * side + i) for o in turns for i in turns]
        return lax.ppermute(value, "blk", pairs) if turn else value

    def halved(parts, move, order):
        parts = dict(enumerate(parts))
        size = parts[0].shape[0]
        for bit in order:
            keys = [k for k in parts if not k & bit]
            sent = jnp.concatenate([parts[k ^ bit].astype(bf16) for k in keys], 0)
            got = move(sent, bit)
            parts = {
                k: parts[k].astype(jnp.float32)
                + got[n * size : (n + 1) * size].astype(jnp.float32)
                for n, k in enumerate(keys)
            }
        return parts

    def dot(lhs, rhs, dims):
        return lax.dot_general(lhs, rhs, (dims, ((), ())), preferred_element_type=jnp.float32)

    def after(value, *others):
        firsts = [lax.slice(other, (0,) * other.ndim, (1,) * other.ndim) for other in others]
        zero = sum(first.astype(jnp.float32).reshape(()) * 0 for first in firsts)
        return value + zero.astype(value.dtype)

    def lanes(value, index):
        return value[:, index * tile_size : (index + 1) * tile_size]

    hidden_part = jnp.maximum(
        lax.dynamic_slice_in_dim(hidden_pre, rep_pos * cols_here, cols_here, 1), 0
    )
    columns = adj_cols[0]
    turn_of = (columns & (side - 1)) ^ inner_pos
    level_of = (columns >> bits) ^ outer_pos
    place = turn_of * per_core + (level_of & (per_core - 1))
    hit = place[None, :] == jnp.arange(section_span, dtype=jnp.int32)[:, None]
    ordered = jnp.zeros((section_span, tile_size, tile_size), bf16)
    for k in range(slots):
        ordered = jnp.where(hit[:, k, None, None], adj_vals[0, k][None], ordered)
    arrived = []
    for t in turns:
        message = ordered[t * per_core : (t + 1) * per_core]
        arrived.append(along_inner(message, t))
    held = {0: hidden_part}
    for bit in rising[::-1]:
        keys = list(held)
        sent = jnp.concatenate([held[k] for k in keys], 0)
        got = along_outer(after(sent, *arrived[1:]) if len(keys) > 1 else sent, bit)
        for n, k in enumerate(keys):
            held[k ^ bit] = got[n * tile_size : (n + 1) * tile_size]
    hidden_stack = jnp.concatenate([held[e] for e in turns], 0)

    grad_part = lax.dynamic_slice_in_dim(cotangent, rep_pos * cols_here, cols_here, 1)
    grad_part = after(grad_part, *arrived[1:], held[rising[-1]])
    grad_stack = [along_inner(grad_part, t) for t in turns]
    everyone = after(jnp.concatenate(arrived, 0), held[side - 1], *grad_stack[1:])
    everyone = lax.all_gather(everyone, "rep", axis=0)
    grad_stack = jnp.concatenate(grad_stack, 0)

    rows = []
    for t in turns:
        row_block = outer_pos * side + (inner_pos ^ t)
        row = []
        for e in turns:
            column_block = (outer_pos ^ e) * side + inner_pos
            holder = ((row_block - column_block) & (blk_count - 1)) >> span_bits
            index = t * per_core + e % per_core
            piece = everyone[0, index]
            for r in range(1, rep_count):
                piece = jnp.where(holder == r, everyone[r, index], piece)
            row.append(piece)
        rows.append(jnp.concatenate(row, 1))
    block = jnp.concatenate(rows, 0)

    mixed = dot(hidden_stack, block, ((0,), (1,))).astype(bf16)
    share = cols_here // side
    by_owner = mixed.reshape(share // rows_here, side, rows_here, side * tile_size)
    mixed_cols = []
    for t in turns:
        chosen = lax.dynamic_index_in_dim(by_owner, inner_pos ^ t, 1, keepdims=False)
        chosen = chosen.reshape(share, side * tile_size)
        chosen = jnp.concatenate([lanes(chosen, u ^ t) for u in turns], 1)
        mixed_cols.append(along_inner(chosen, t))
    mixed_cols = sum(part.astype(jnp.float32) for part in mixed_cols).astype(bf16)
    back = after(dot(grad_stack, block, ((0,), (0,))), mixed)
    back = halved([lanes(back, e) for e in turns], along_outer, rising[:-1])
    rows = [lanes(after(mixed, mixed_cols), t) for t in turns]
    rows = halved(rows, along_inner, rising[:-1])

    mixed_cols = lax.all_gather(mixed_cols, "rep", axis=0, tiled=True)
    weight_part = after(dot(mixed_cols, grad_stack, ((1,), (0,))), back[0]).astype(bf16)
    by_outer = weight_part.reshape(side, rows_here, cols_here)
    weight_got = [
        along_outer(lax.dynamic_index_in_dim(by_outer, outer_pos ^ t, 0, keepdims=False), t)
        for t in turns
    ]

    last = rising[-1]
    back_got = along_outer(back[last].astype(bf16), last).astype(jnp.float32)
    rows_got = after(rows[last].astype(bf16), weight_part)
    rows_got = along_inner(rows_got, last).astype(jnp.float32)
    rows_sum, back = rows[0] + rows_got, back[0] + back_got
    both = jnp.concatenate([rows_sum, back], 0).astype(bf16)
    both = lax.all_gather(both, "rep", axis=0)
    mixed_rows = both[:, :cols_here].reshape(feature_width, tile_size)
    back_full = both[:, cols_here:].reshape(feature_width, tile_size)

    w_columns = lax.dynamic_slice_in_dim(w_out, rep_pos * cols_here, cols_here, 1)
    out_part = dot(mixed_rows, w_columns, ((0,), (0,))).astype(bf16)
    w_rows = lax.dynamic_slice_in_dim(w_out, rep_pos * cols_here, cols_here, 0)
    grad_in = dot(back_full, w_rows, ((0,), (1,)))
    pre_part = lax.dynamic_slice_in_dim(hidden_pre, rep_pos * cols_here, cols_here, 1)
    grad_pre = jnp.where(pre_part > 0, grad_in, 0.0).astype(bf16)

    grad_weight = after(sum(part.astype(jnp.float32) for part in weight_got), out_part)
    return (out_part, grad_weight, grad_pre)


def solution(mesh):
    placed = (P("blk", None), P("blk", "rep", None, None), P("blk", "rep"), P(), P("blk", None))
    return jax.shard_map(
        shards,
        mesh=mesh,
        in_specs=placed,
        out_specs=(P("blk", "rep"), P("blk", "rep"), P("blk", "rep")),
        check_vma=False,
    )
```

```python
import jax
import jax.numpy as jnp
from jax import lax
from jax.sharding import PartitionSpec as P


def shards(hidden_pre, adj_vals, adj_cols, w_out, cotangent):
    feature_width = hidden_pre.shape[1]
    slots, tile_size = adj_vals.shape[1:3]
    blk_count = lax.axis_size("blk")
    rep_count = lax.axis_size("rep")
    section_span = blk_count // rep_count
    bits = (blk_count.bit_length() - 1) // 2
    side = 1 << bits
    per_core = section_span // side
    blk_pos = lax.axis_index("blk")
    rep_pos = lax.axis_index("rep")
    outer_pos, inner_pos = blk_pos >> bits, blk_pos & (side - 1)
    span_bits = section_span.bit_length() - 1
    cols_here = feature_width // rep_count
    rows_here = feature_width // blk_count
    bf16 = jnp.bfloat16
    turns = range(side)
    rising = [1 << b for b in range(bits)]

    def along_inner(value, turn):
        pairs = [(o * side + i, o * side + (i ^ turn)) for o in turns for i in turns]
        return lax.ppermute(value, "blk", pairs) if turn else value

    def along_outer(value, turn):
        pairs = [(o * side + i, (o ^ turn) * side + i) for o in turns for i in turns]
        return lax.ppermute(value, "blk", pairs) if turn else value

    def halved(parts, move, order):
        parts = dict(enumerate(parts))
        size = parts[0].shape[0]
        for bit in order:
            keys = [k for k in parts if not k & bit]
            sent = jnp.concatenate([parts[k ^ bit].astype(bf16) for k in keys], 0)
            got = move(sent, bit)
            parts = {
                k: parts[k].astype(jnp.float32)
                + got[n * size : (n + 1) * size].astype(jnp.float32)
                for n, k in enumerate(keys)
            }
        return parts

    def dot(lhs, rhs, dims):
        return lax.dot_general(lhs, rhs, (dims, ((), ())), preferred_element_type=jnp.float32)

    def after(value, *others):
        row = 0.0
        for other in others:
            flat = other[0] if other.ndim == 3 else other
            row = row + flat[:1, :tile_size].astype(jnp.float32) * 0
        row = jnp.concatenate([row.astype(value.dtype)] * (value.shape[-1] // tile_size), 1)
        return value + row

    def lanes(value, index):
        return value[:, index * tile_size : (index + 1) * tile_size]

    hidden_part = jnp.maximum(
        lax.dynamic_slice_in_dim(hidden_pre, rep_pos * cols_here, cols_here, 1), 0
    )
    columns = adj_cols[0]
    turn_of = (columns & (side - 1)) ^ inner_pos
    level_of = (columns >> bits) ^ outer_pos
    place = turn_of * per_core + (level_of & (per_core - 1))
    hit = place[None, :] == jnp.arange(section_span, dtype=jnp.int32)[:, None]
    ordered = jnp.zeros((section_span, tile_size, tile_size), bf16)
    for k in range(slots):
        ordered = jnp.where(hit[:, k, None, None], adj_vals[0, k][None], ordered)
    arrived = []
    for t in turns:
        message = ordered[t * per_core : (t + 1) * per_core]
        arrived.append(along_inner(message, t))
    held = {0: hidden_part}
    for bit in rising[::-1]:
        keys = list(held)
        sent = jnp.concatenate([held[k] for k in keys], 0)
        got = along_outer(after(sent, *arrived[1:]) if len(keys) > 1 else sent, bit)
        for n, k in enumerate(keys):
            held[k ^ bit] = got[n * tile_size : (n + 1) * tile_size]
    hidden_stack = jnp.concatenate([held[e] for e in turns], 0)

    grad_part = lax.dynamic_slice_in_dim(cotangent, rep_pos * cols_here, cols_here, 1)
    grad_part = after(grad_part, *arrived[1:], held[rising[-1]])
    grad_stack = [along_inner(grad_part, t) for t in turns]
    everyone = after(jnp.concatenate(arrived, 0), held[side - 1], *grad_stack[1:])
    everyone = lax.all_gather(everyone, "rep", axis=0)
    grad_stack = jnp.concatenate(grad_stack, 0)

    rows = []
    for t in turns:
        row_block = outer_pos * side + (inner_pos ^ t)
        row = []
        for e in turns:
            column_block = (outer_pos ^ e) * side + inner_pos
            holder = ((row_block - column_block) & (blk_count - 1)) >> span_bits
            index = t * per_core + e % per_core
            piece = everyone[0, index]
            for r in range(1, rep_count):
                piece = jnp.where(holder == r, everyone[r, index], piece)
            row.append(piece)
        rows.append(jnp.concatenate(row, 1))
    block = jnp.concatenate(rows, 0)

    mixed = dot(hidden_stack, block, ((0,), (1,))).astype(bf16)
    share = cols_here // side
    by_owner = mixed.reshape(share // rows_here, side, rows_here, side * tile_size)
    mixed_cols = []
    for t in turns:
        chosen = lax.dynamic_index_in_dim(by_owner, inner_pos ^ t, 1, keepdims=False)
        chosen = chosen.reshape(share, side * tile_size)
        chosen = jnp.concatenate([lanes(chosen, u ^ t) for u in turns], 1)
        mixed_cols.append(along_inner(chosen, t))
    mixed_cols = sum(part.astype(jnp.float32) for part in mixed_cols).astype(bf16)
    back = dot(grad_stack, block, ((0,), (0,)))
    back = halved([lanes(back, e) for e in turns], along_outer, rising[:-1])
    rows = [lanes(after(mixed, mixed_cols), t) for t in turns]
    rows = halved(rows, along_inner, rising[:-1])

    mixed_cols = lax.all_gather(mixed_cols, "rep", axis=0, tiled=True)
    weight_part = after(dot(mixed_cols, grad_stack, ((1,), (0,))), back[0]).astype(bf16)
    by_outer = weight_part.reshape(side, rows_here, cols_here)
    weight_got = [
        along_outer(lax.dynamic_index_in_dim(by_outer, outer_pos ^ t, 0, keepdims=False), t)
        for t in turns
    ]

    last = rising[-1]
    back_got = along_outer(back[last].astype(bf16), last).astype(jnp.float32)
    rows_got = after(rows[last].astype(bf16), weight_part)
    rows_got = along_inner(rows_got, last).astype(jnp.float32)
    rows_sum, back = rows[0] + rows_got, back[0] + back_got
    both = jnp.concatenate([rows_sum, back], 0).astype(bf16)
    both = lax.all_gather(both, "rep", axis=0)
    mixed_rows = both[:, :cols_here].reshape(feature_width, tile_size)
    back_full = both[:, cols_here:].reshape(feature_width, tile_size)

    w_columns = lax.dynamic_slice_in_dim(w_out, rep_pos * cols_here, cols_here, 1)
    out_part = dot(mixed_rows, w_columns, ((0,), (0,))).astype(bf16)
    w_rows = lax.dynamic_slice_in_dim(w_out, rep_pos * cols_here, cols_here, 0)
    grad_in = dot(back_full, w_rows, ((0,), (1,)))
    pre_part = lax.dynamic_slice_in_dim(hidden_pre, rep_pos * cols_here, cols_here, 1)
    grad_pre = jnp.where(pre_part > 0, grad_in, 0.0).astype(bf16)

    grad_weight = after(sum(part.astype(jnp.float32) for part in weight_got), out_part)
    return (out_part, grad_weight, grad_pre)


def solution(mesh):
    placed = (P("blk", None), P("blk", "rep", None, None), P("blk", "rep"), P(), P("blk", None))
    return jax.shard_map(
        shards,
        mesh=mesh,
        in_specs=placed,
        out_specs=(P("blk", "rep"), P("blk", "rep"), P("blk", "rep")),
        check_vma=False,
    )
```

```python
import jax
import jax.numpy as jnp
from jax import lax
from jax.sharding import PartitionSpec as P


def shards(hidden_pre, adj_vals, adj_cols, w_out, cotangent):
    feature_width = hidden_pre.shape[1]
    slots, tile_size = adj_vals.shape[1:3]
    blk_count = lax.axis_size("blk")
    rep_count = lax.axis_size("rep")
    section_span = blk_count // rep_count
    bits = (blk_count.bit_length() - 1) // 2
    side = 1 << bits
    per_core = section_span // side
    blk_pos = lax.axis_index("blk")
    rep_pos = lax.axis_index("rep")
    outer_pos, inner_pos = blk_pos >> bits, blk_pos & (side - 1)
    span_bits = section_span.bit_length() - 1
    cols_here = feature_width // rep_count
    rows_here = feature_width // blk_count
    bf16 = jnp.bfloat16
    turns = range(side)
    rising = [1 << b for b in range(bits)]

    def along_inner(value, turn):
        pairs = [(o * side + i, o * side + (i ^ turn)) for o in turns for i in turns]
        return lax.ppermute(value, "blk", pairs) if turn else value

    def along_outer(value, turn):
        pairs = [(o * side + i, (o ^ turn) * side + i) for o in turns for i in turns]
        return lax.ppermute(value, "blk", pairs) if turn else value

    def halved(parts, move, order):
        parts = dict(enumerate(parts))
        size = parts[0].shape[0]
        for bit in order:
            keys = [k for k in parts if not k & bit]
            sent = jnp.concatenate([parts[k ^ bit].astype(bf16) for k in keys], 0)
            got = move(sent, bit)
            parts = {
                k: parts[k].astype(jnp.float32)
                + got[n * size : (n + 1) * size].astype(jnp.float32)
                for n, k in enumerate(keys)
            }
        return parts

    def dot(lhs, rhs, dims):
        return lax.dot_general(lhs, rhs, (dims, ((), ())), preferred_element_type=jnp.float32)

    def after(value, *others):
        row = 0.0
        for other in others:
            flat = other[0] if other.ndim == 3 else other
            row = row + flat[:1, :tile_size].astype(jnp.float32) * 0
        row = jnp.concatenate([row.astype(value.dtype)] * (value.shape[-1] // tile_size), 1)
        return value + row

    def lanes(value, index):
        return value[:, index * tile_size : (index + 1) * tile_size]

    hidden_part = jnp.maximum(
        lax.dynamic_slice_in_dim(hidden_pre, rep_pos * cols_here, cols_here, 1), 0
    )
    hidden_stack = [along_outer(hidden_part, e) for e in turns]

    columns = adj_cols[0]
    turn_of = (columns & (side - 1)) ^ inner_pos
    level_of = (columns >> bits) ^ outer_pos
    place = turn_of * per_core + (level_of & (per_core - 1))
    hit = place[None, :] == jnp.arange(section_span, dtype=jnp.int32)[:, None]
    ordered = jnp.zeros((section_span, tile_size, tile_size), bf16)
    for k in range(slots):
        ordered = jnp.where(hit[:, k, None, None], adj_vals[0, k][None], ordered)
    arrived = []
    for t in turns:
        message = ordered[t * per_core : (t + 1) * per_core]
        if t > 2:
            message = after(message, hidden_stack[1])
        arrived.append(along_inner(message, t))
    hidden_stack = jnp.concatenate(hidden_stack, 0)
    everyone = lax.all_gather(jnp.concatenate(arrived, 0), "rep", axis=0)
    grad_part = lax.dynamic_slice_in_dim(cotangent, rep_pos * cols_here, cols_here, 1)
    grad_stack = jnp.concatenate([along_inner(grad_part, t) for t in turns], 0)

    rows = []
    for t in turns:
        row_block = outer_pos * side + (inner_pos ^ t)
        row = []
        for e in turns:
            column_block = (outer_pos ^ e) * side + inner_pos
            holder = ((row_block - column_block) & (blk_count - 1)) >> span_bits
            index = t * per_core + e % per_core
            piece = everyone[0, index]
            for r in range(1, rep_count):
                piece = jnp.where(holder == r, everyone[r, index], piece)
            row.append(piece)
        rows.append(jnp.concatenate(row, 1))
    block = jnp.concatenate(rows, 0)

    mixed = dot(hidden_stack, block, ((0,), (1,))).astype(bf16)
    share = cols_here // side
    by_owner = mixed.reshape(share // rows_here, side, rows_here, side * tile_size)
    mixed_cols = []
    for t in turns:
        chosen = lax.dynamic_index_in_dim(by_owner, inner_pos ^ t, 1, keepdims=False)
        chosen = chosen.reshape(share, side * tile_size)
        chosen = jnp.concatenate([lanes(chosen, u ^ t) for u in turns], 1)
        mixed_cols.append(along_inner(chosen, t))
    mixed_cols = sum(part.astype(jnp.float32) for part in mixed_cols).astype(bf16)
    back = dot(grad_stack, block, ((0,), (0,))).astype(bf16)
    back = sum(along_outer(lanes(back, e), e).astype(jnp.float32) for e in turns)
    rows = [lanes(after(mixed, mixed_cols), t) for t in turns]
    rows = halved(rows, along_inner, rising[:-1])

    mixed_cols = lax.all_gather(mixed_cols, "rep", axis=0, tiled=True)
    weight_part = dot(mixed_cols, grad_stack, ((1,), (0,))).astype(bf16)
    by_outer = weight_part.reshape(side, rows_here, cols_here)
    weight_got = [
        along_outer(lax.dynamic_index_in_dim(by_outer, outer_pos ^ t, 0, keepdims=False), t)
        for t in turns
    ]

    last = rising[-1]
    rows_got = after(rows[last].astype(bf16), weight_part)
    rows_sum = rows[0] + along_inner(rows_got, last).astype(jnp.float32)
    both = jnp.concatenate([rows_sum, back], 0).astype(bf16)
    both = lax.all_gather(both, "rep", axis=0)
    mixed_rows = both[:, :cols_here].reshape(feature_width, tile_size)
    back_full = both[:, cols_here:].reshape(feature_width, tile_size)

    w_columns = lax.dynamic_slice_in_dim(w_out, rep_pos * cols_here, cols_here, 1)
    out_part = dot(mixed_rows, w_columns, ((0,), (0,))).astype(bf16)
    w_rows = lax.dynamic_slice_in_dim(w_out, rep_pos * cols_here, cols_here, 0)
    grad_in = dot(back_full, w_rows, ((0,), (1,)))
    pre_part = lax.dynamic_slice_in_dim(hidden_pre, rep_pos * cols_here, cols_here, 1)
    grad_pre = jnp.where(pre_part > 0, grad_in, 0.0).astype(bf16)

    grad_weight = sum(part.astype(jnp.float32) for part in weight_got)
    return (out_part, grad_weight, grad_pre)


def solution(mesh):
    placed = (P("blk", None), P("blk", "rep", None, None), P("blk", "rep"), P(), P("blk", None))
    return jax.shard_map(
        shards,
        mesh=mesh,
        in_specs=placed,
        out_specs=(P("blk", "rep"), P("blk", "rep"), P("blk", "rep")),
        check_vma=False,
    )
```

```python
import jax
import jax.numpy as jnp
from jax import lax
from jax.sharding import PartitionSpec as P


def shards(hidden_pre, adj_vals, adj_cols, w_out, cotangent):
    feature_width = hidden_pre.shape[1]
    slots, tile_size = adj_vals.shape[1:3]
    blk_count = lax.axis_size("blk")
    rep_count = lax.axis_size("rep")
    section_span = blk_count // rep_count
    bits = (blk_count.bit_length() - 1) // 2
    side = 1 << bits
    per_core = section_span // side
    blk_pos = lax.axis_index("blk")
    rep_pos = lax.axis_index("rep")
    outer_pos, inner_pos = blk_pos >> bits, blk_pos & (side - 1)
    span_bits = section_span.bit_length() - 1
    cols_here = feature_width // rep_count
    rows_here = feature_width // blk_count
    lane_blocks = cols_here // tile_size
    bf16 = jnp.bfloat16
    turns = range(side)
    rising = [1 << b for b in range(bits)]

    def along_inner(value, turn):
        pairs = [(o * side + i, o * side + (i ^ turn)) for o in turns for i in turns]
        return lax.ppermute(value, "blk", pairs) if turn else value

    def along_outer(value, turn):
        pairs = [(o * side + i, (o ^ turn) * side + i) for o in turns for i in turns]
        return lax.ppermute(value, "blk", pairs) if turn else value

    def from_two(value, turn, outer):
        pairs = []
        for o in turns:
            for i in turns:
                for r in range(2):
                    there = (o ^ (turn + r)) * side + i if outer else o * side + (i ^ (turn + r))
                    pairs.append(((o * side + i) * 2 + r, there * 2 + r))
        return lax.ppermute(value, ("blk", "rep"), pairs)

    def halved(parts, move):
        parts = dict(enumerate(parts))
        size = parts[0].shape[0]
        for bit in rising:
            keys = [k for k in parts if not k & bit]
            sent = jnp.concatenate([parts[k ^ bit].astype(bf16) for k in keys], 0)
            got = move(sent, bit)
            parts = {
                k: parts[k].astype(jnp.float32)
                + got[n * size : (n + 1) * size].astype(jnp.float32)
                for n, k in enumerate(keys)
            }
        return parts[0]

    def dot(lhs, rhs, dims):
        return lax.dot_general(lhs, rhs, (dims, ((), ())), preferred_element_type=jnp.float32)

    def lanes(value, index):
        return value[:, index * tile_size : (index + 1) * tile_size]

    def columns_of(value, index):
        return lax.dynamic_slice_in_dim(value, index * cols_here, cols_here, 1)

    pair_up = rep_count == 2
    direct = turns[1:2] if pair_up else turns[1:]
    hidden_far = [from_two(hidden_pre, t, True) for t in turns[2::2]] if pair_up else []
    hidden_part = jnp.maximum(columns_of(hidden_pre, rep_pos), 0)
    hidden_stack = [hidden_part] + [along_outer(hidden_part, t) for t in direct]

    columns = adj_cols[0]
    turn_of = (columns & (side - 1)) ^ inner_pos
    level_of = (columns >> bits) ^ outer_pos
    place = turn_of * per_core + (level_of & (per_core - 1))
    hit = place[None, :] == jnp.arange(section_span, dtype=jnp.int32)[:, None]
    ordered = jnp.zeros((section_span, tile_size, tile_size), bf16)
    for k in range(slots):
        ordered = jnp.where(hit[:, k, None, None], adj_vals[0, k][None], ordered)
    swapped = [
        along_inner(ordered[t * per_core : (t + 1) * per_core], t) for t in turns
    ]

    grad_far = [from_two(cotangent, t, False) for t in turns[2::2]] if pair_up else []
    grad_part = columns_of(cotangent, rep_pos)
    grad_stack = [grad_part] + [along_inner(grad_part, t) for t in direct]

    for far in hidden_far + grad_far:
        other = columns_of(far, 1 - rep_pos)
        swapped.append(jnp.stack([lanes(other, n) for n in range(lane_blocks)]))
    everyone = lax.all_gather(jnp.concatenate(swapped, 0), "rep", axis=0)

    for index, far in enumerate(hidden_far + grad_far):
        mine = columns_of(far, rep_pos)
        start = section_span + index * lane_blocks
        both = everyone[:, start : start + lane_blocks]
        other = jnp.where(rep_pos == 0, both[1], both[0])
        other = jnp.concatenate([other[n] for n in range(lane_blocks)], 1)
        blocks = [jnp.where(rep_pos == 0, mine, other), jnp.where(rep_pos == 0, other, mine)]
        if index < len(hidden_far):
            hidden_stack.extend(jnp.maximum(part, 0) for part in blocks)
        else:
            grad_stack.extend(blocks)
    hidden_stack = jnp.concatenate(hidden_stack, 0)
    grad_stack = jnp.concatenate(grad_stack, 0)

    rows = []
    for t in turns:
        row_block = outer_pos * side + (inner_pos ^ t)
        row = []
        for e in turns:
            column_block = (outer_pos ^ e) * side + inner_pos
            holder = ((row_block - column_block) & (blk_count - 1)) >> span_bits
            index = t * per_core + e % per_core
            piece = everyone[0, index]
            for r in range(1, rep_count):
                piece = jnp.where(holder == r, everyone[r, index], piece)
            row.append(piece)
        rows.append(jnp.concatenate(row, 1))
    block = jnp.concatenate(rows, 0)

    mixed = dot(hidden_stack, block, ((0,), (1,))).astype(bf16)
    share = cols_here // side
    by_owner = mixed.reshape(share // rows_here, side, rows_here, side * tile_size)
    mixed_cols = 0.0
    for t in turns:
        chosen = lax.dynamic_index_in_dim(by_owner, inner_pos ^ t, 1, keepdims=False)
        chosen = chosen.reshape(share, side * tile_size)
        chosen = jnp.concatenate([lanes(chosen, u ^ t) for u in turns], 1)
        mixed_cols = mixed_cols + along_inner(chosen, t).astype(jnp.float32)

    back = dot(grad_stack, block, ((0,), (0,)))
    back = halved([lanes(back, e) for e in turns], along_outer).astype(bf16)

    mixed_cols = lax.all_gather(mixed_cols.astype(bf16), "rep", axis=0, tiled=True)
    weight_part = dot(mixed_cols, grad_stack, ((1,), (0,))).astype(bf16)
    by_outer = weight_part.reshape(side, rows_here, cols_here)
    grad_weight = sum(
        along_outer(
            lax.dynamic_index_in_dim(by_outer, outer_pos ^ t, 0, keepdims=False), t
        ).astype(jnp.float32)
        for t in turns
    )

    w_share = w_out.reshape(side, side, rows_here, feature_width)
    w_share = lax.dynamic_index_in_dim(w_share, inner_pos, 1, keepdims=False)
    w_share = columns_of(w_share.reshape(side * rows_here, feature_width), rep_pos)
    out_part = dot(mixed_cols, w_share, ((0,), (0,)))
    out_part = halved(
        [out_part[t * tile_size : (t + 1) * tile_size] for t in turns], along_inner
    ).astype(bf16)

    back_full = lax.all_gather(back, "rep", axis=0, tiled=True)
    w_rows = lax.dynamic_slice_in_dim(w_out, rep_pos * cols_here, cols_here, 0)
    grad_in = dot(back_full, w_rows, ((0,), (1,)))
    pre_part = columns_of(hidden_pre, rep_pos)
    grad_pre = jnp.where(pre_part > 0, grad_in, 0.0).astype(bf16)
    return (out_part, grad_weight, grad_pre)


def solution(mesh):
    placed = (P("blk", None), P("blk", "rep", None, None), P("blk", "rep"), P(), P("blk", None))
    return jax.shard_map(
        shards,
        mesh=mesh,
        in_specs=placed,
        out_specs=(P("blk", "rep"), P("blk", "rep"), P("blk", "rep")),
        check_vma=False,
    )
```

```python
import jax
import jax.numpy as jnp
from jax import lax
from jax.sharding import PartitionSpec as P


def shards(hidden_pre, adj_vals, adj_cols, w_out, cotangent):
    feature_width = hidden_pre.shape[1]
    slots, tile_size = adj_vals.shape[1:3]
    blk_count = lax.axis_size("blk")
    rep_count = lax.axis_size("rep")
    section_span = blk_count // rep_count
    bits = (blk_count.bit_length() - 1) // 2
    side = 1 << bits
    per_core = section_span // side
    blk_pos = lax.axis_index("blk")
    rep_pos = lax.axis_index("rep")
    outer_pos, inner_pos = blk_pos >> bits, blk_pos & (side - 1)
    span_bits = section_span.bit_length() - 1
    cols_here = feature_width // rep_count
    rows_here = feature_width // blk_count
    bf16 = jnp.bfloat16
    turns = range(side)
    rising = [1 << b for b in range(bits)]

    def along_inner(value, turn):
        pairs = [(o * side + i, o * side + (i ^ turn)) for o in turns for i in turns]
        return lax.ppermute(value, "blk", pairs) if turn else value

    def along_outer(value, turn):
        pairs = [(o * side + i, (o ^ turn) * side + i) for o in turns for i in turns]
        return lax.ppermute(value, "blk", pairs) if turn else value

    def halved(parts, move):
        parts = dict(enumerate(parts))
        size = parts[0].shape[0]
        for bit in rising:
            keys = [k for k in parts if not k & bit]
            sent = jnp.concatenate([parts[k ^ bit].astype(bf16) for k in keys], 0)
            got = move(sent, bit)
            parts = {
                k: parts[k].astype(jnp.float32)
                + got[n * size : (n + 1) * size].astype(jnp.float32)
                for n, k in enumerate(keys)
            }
        return parts[0]

    def dot(lhs, rhs, dims):
        return lax.dot_general(lhs, rhs, (dims, ((), ())), preferred_element_type=jnp.float32)

    def lanes(value, index):
        return value[:, index * tile_size : (index + 1) * tile_size]

    def after(value, other):
        row = other[:1, :tile_size] * 0
        return value + jnp.concatenate([row] * (value.shape[1] // tile_size), 1)

    def columns_of(value, index):
        return lax.dynamic_slice_in_dim(value, index * cols_here, cols_here, 1)

    hidden_part = jnp.maximum(columns_of(hidden_pre, rep_pos), 0)

    columns = adj_cols[0]
    turn_of = (columns & (side - 1)) ^ inner_pos
    level_of = (columns >> bits) ^ outer_pos
    place = turn_of * per_core + (level_of & (per_core - 1))
    hit = place[None, :] == jnp.arange(section_span, dtype=jnp.int32)[:, None]
    ordered = jnp.zeros((section_span, tile_size, tile_size), bf16)
    for k in range(slots):
        ordered = jnp.where(hit[:, k, None, None], adj_vals[0, k][None], ordered)
    everyone = lax.all_gather(ordered, "rep", axis=0)
    row_block = outer_pos * side + inner_pos
    rows = []
    for t in turns:
        row = []
        for e in turns:
            column_block = (outer_pos ^ e) * side + (inner_pos ^ t)
            holder = ((row_block - column_block) & (blk_count - 1)) >> span_bits
            index = t * per_core + e % per_core
            piece = everyone[0, index]
            for r in range(1, rep_count):
                piece = jnp.where(holder == r, everyone[r, index], piece)
            row.append(piece)
        rows.append(along_inner(jnp.concatenate(row, 1), t))
    block = jnp.concatenate(rows, 0)

    hidden_stack = [hidden_part]
    for t in turns[1:]:
        message = after(hidden_part, rows[1]) if t == 1 else hidden_part
        hidden_stack.append(along_outer(message, t))
    hidden_stack = jnp.concatenate(hidden_stack, 0)
    grad_part = columns_of(cotangent, rep_pos)
    grad_stack = jnp.concatenate([along_inner(grad_part, t) for t in turns], 0)

    mixed = dot(hidden_stack, block, ((0,), (1,))).astype(bf16)
    share = cols_here // side
    by_owner = mixed.reshape(share // rows_here, side, rows_here, side * tile_size)
    mixed_cols = 0.0
    for t in turns:
        chosen = lax.dynamic_index_in_dim(by_owner, inner_pos ^ t, 1, keepdims=False)
        chosen = chosen.reshape(share, side * tile_size)
        chosen = jnp.concatenate([lanes(chosen, u ^ t) for u in turns], 1)
        mixed_cols = mixed_cols + along_inner(chosen, t).astype(jnp.float32)

    back = dot(grad_stack, block, ((0,), (0,))).astype(bf16)
    back = sum(along_outer(lanes(back, e), e).astype(jnp.float32) for e in turns).astype(bf16)

    mixed_cols = lax.all_gather(mixed_cols.astype(bf16), "rep", axis=0, tiled=True)
    weight_part = dot(mixed_cols, grad_stack, ((1,), (0,))).astype(bf16)
    by_outer = weight_part.reshape(side, rows_here, cols_here)
    grad_weight = sum(
        along_outer(
            lax.dynamic_index_in_dim(by_outer, outer_pos ^ t, 0, keepdims=False), t
        ).astype(jnp.float32)
        for t in turns
    )

    w_share = w_out.reshape(side, side, rows_here, feature_width)
    w_share = lax.dynamic_index_in_dim(w_share, inner_pos, 1, keepdims=False)
    w_share = columns_of(w_share.reshape(side * rows_here, feature_width), rep_pos)
    out_part = dot(mixed_cols, w_share, ((0,), (0,)))
    out_part = halved(
        [out_part[t * tile_size : (t + 1) * tile_size] for t in turns], along_inner
    ).astype(bf16)

    back_full = lax.all_gather(back, "rep", axis=0, tiled=True)
    w_rows = lax.dynamic_slice_in_dim(w_out, rep_pos * cols_here, cols_here, 0)
    grad_in = dot(back_full, w_rows, ((0,), (1,)))
    pre_part = columns_of(hidden_pre, rep_pos)
    grad_pre = jnp.where(pre_part > 0, grad_in, 0.0).astype(bf16)
    return (out_part, grad_weight, grad_pre)


def solution(mesh):
    placed = (P("blk", None), P("blk", "rep", None, None), P("blk", "rep"), P(), P("blk", None))
    return jax.shard_map(
        shards,
        mesh=mesh,
        in_specs=placed,
        out_specs=(P("blk", "rep"), P("blk", "rep"), P("blk", "rep")),
        check_vma=False,
    )
```

```python
import jax
import jax.numpy as jnp
from jax import lax
from jax.sharding import PartitionSpec as P


def shards(hidden_pre, adj_vals, adj_cols, w_out, cotangent):
    feature_width = hidden_pre.shape[1]
    slots, tile_size = adj_vals.shape[1:3]
    blk_count = lax.axis_size("blk")
    rep_count = lax.axis_size("rep")
    section_span = blk_count // rep_count
    bits = (blk_count.bit_length() - 1) // 2
    side = 1 << bits
    per_core = section_span // side
    blk_pos = lax.axis_index("blk")
    rep_pos = lax.axis_index("rep")
    outer_pos, inner_pos = blk_pos >> bits, blk_pos & (side - 1)
    span_bits = section_span.bit_length() - 1
    cols_here = feature_width // rep_count
    rows_here = feature_width // blk_count
    bf16 = jnp.bfloat16
    turns = range(side)
    rising = [1 << b for b in range(bits)]

    def along_inner(value, turn):
        pairs = [(o * side + i, o * side + (i ^ turn)) for o in turns for i in turns]
        return lax.ppermute(value, "blk", pairs) if turn else value

    def along_outer(value, turn):
        pairs = [(o * side + i, (o ^ turn) * side + i) for o in turns for i in turns]
        return lax.ppermute(value, "blk", pairs) if turn else value

    def halved(parts, move):
        parts = dict(enumerate(parts))
        size = parts[0].shape[0]
        for bit in rising:
            keys = [k for k in parts if not k & bit]
            sent = jnp.concatenate([parts[k ^ bit].astype(bf16) for k in keys], 0)
            got = move(sent, bit)
            parts = {
                k: parts[k].astype(jnp.float32)
                + got[n * size : (n + 1) * size].astype(jnp.float32)
                for n, k in enumerate(keys)
            }
        return parts[0]

    def dot(lhs, rhs, dims):
        return lax.dot_general(lhs, rhs, (dims, ((), ())), preferred_element_type=jnp.float32)

    def lanes(value, index):
        return value[:, index * tile_size : (index + 1) * tile_size]

    def after(value, other):
        height, width = (min(a, b) for a, b in zip(value.shape, other.shape))
        part = other[:height, :width].astype(value.dtype) * 0
        part = jnp.concatenate([part] * (value.shape[1] // width), 1)
        return value + jnp.concatenate([part] * (value.shape[0] // height), 0)

    def columns_of(value, index):
        return lax.dynamic_slice_in_dim(value, index * cols_here, cols_here, 1)

    hidden_part = jnp.maximum(columns_of(hidden_pre, rep_pos), 0)

    columns = adj_cols[0]
    turn_of = (columns & (side - 1)) ^ inner_pos
    level_of = (columns >> bits) ^ outer_pos
    place = turn_of * per_core + (level_of & (per_core - 1))
    hit = place[None, :] == jnp.arange(section_span, dtype=jnp.int32)[:, None]
    ordered = jnp.zeros((section_span, tile_size, tile_size), bf16)
    for k in range(slots):
        ordered = jnp.where(hit[:, k, None, None], adj_vals[0, k][None], ordered)
    arrived = [
        along_inner(ordered[t * per_core : (t + 1) * per_core], t) for t in turns
    ]
    everyone = lax.all_gather(jnp.concatenate(arrived, 0), "rep", axis=0)
    rows = []
    for t in turns:
        row_block = outer_pos * side + (inner_pos ^ t)
        row = []
        for e in turns:
            column_block = (outer_pos ^ e) * side + inner_pos
            holder = ((row_block - column_block) & (blk_count - 1)) >> span_bits
            index = t * per_core + e % per_core
            piece = everyone[0, index]
            for r in range(1, rep_count):
                piece = jnp.where(holder == r, everyone[r, index], piece)
            row.append(piece)
        rows.append(jnp.concatenate(row, 1))
    block = jnp.concatenate(rows, 0)

    hidden_stack = jnp.concatenate([along_outer(hidden_part, e) for e in turns], 0)
    grad_part = columns_of(cotangent, rep_pos)
    grad_stack = jnp.concatenate([along_inner(grad_part, t) for t in turns], 0)

    mixed = dot(hidden_stack, block, ((0,), (1,))).astype(bf16)
    share = cols_here // side
    by_owner = mixed.reshape(share // rows_here, side, rows_here, side * tile_size)
    mixed_cols = 0.0
    for t in turns:
        chosen = lax.dynamic_index_in_dim(by_owner, inner_pos ^ t, 1, keepdims=False)
        chosen = chosen.reshape(share, side * tile_size)
        chosen = jnp.concatenate([lanes(chosen, u ^ t) for u in turns], 1)
        mixed_cols = mixed_cols + along_inner(chosen, t).astype(jnp.float32)

    back = after(dot(grad_stack, block, ((0,), (0,))), mixed).astype(bf16)
    back = sum(along_outer(lanes(back, e), e).astype(jnp.float32) for e in turns)

    mixed_cols = lax.all_gather(mixed_cols.astype(bf16), "rep", axis=0, tiled=True)
    weight_part = dot(mixed_cols, grad_stack, ((1,), (0,))).astype(bf16)
    by_outer = weight_part.reshape(side, rows_here, cols_here)
    grad_weight = sum(
        along_outer(
            lax.dynamic_index_in_dim(by_outer, outer_pos ^ t, 0, keepdims=False), t
        ).astype(jnp.float32)
        for t in turns
    )

    w_share = w_out.reshape(side, side, rows_here, feature_width)
    w_share = lax.dynamic_index_in_dim(w_share, inner_pos, 1, keepdims=False)
    w_share = columns_of(w_share.reshape(side * rows_here, feature_width), rep_pos)
    out_part = dot(mixed_cols, w_share, ((0,), (0,)))
    out_part = halved(
        [out_part[t * tile_size : (t + 1) * tile_size] for t in turns], along_inner
    ).astype(bf16)

    back = after(back, weight_part).astype(bf16)
    back_full = lax.all_gather(back, "rep", axis=0, tiled=True)
    w_rows = lax.dynamic_slice_in_dim(w_out, rep_pos * cols_here, cols_here, 0)
    grad_in = dot(back_full, w_rows, ((0,), (1,)))
    pre_part = columns_of(hidden_pre, rep_pos)
    grad_pre = jnp.where(pre_part > 0, grad_in, 0.0).astype(bf16)
    return (out_part, grad_weight, grad_pre)


def solution(mesh):
    placed = (P("blk", None), P("blk", "rep", None, None), P("blk", "rep"), P(), P("blk", None))
    return jax.shard_map(
        shards,
        mesh=mesh,
        in_specs=placed,
        out_specs=(P("blk", "rep"), P("blk", "rep"), P("blk", "rep")),
        check_vma=False,
    )
```

```python
import jax
import jax.numpy as jnp
from jax import lax
from jax.sharding import PartitionSpec as P


def shards(hidden_pre, adj_vals, adj_cols, w_out, cotangent):
    feature_width = hidden_pre.shape[1]
    slots, tile_size = adj_vals.shape[1:3]
    blk_count = lax.axis_size("blk")
    rep_count = lax.axis_size("rep")
    section_span = blk_count // rep_count
    bits = (blk_count.bit_length() - 1) // 2
    side = 1 << bits
    per_core = section_span // side
    blk_pos = lax.axis_index("blk")
    rep_pos = lax.axis_index("rep")
    outer_pos, inner_pos = blk_pos >> bits, blk_pos & (side - 1)
    span_bits = section_span.bit_length() - 1
    cols_here = feature_width // rep_count
    rows_here = feature_width // blk_count
    bf16 = jnp.bfloat16
    turns = range(side)

    def along_inner(value, turn):
        pairs = [(o * side + i, o * side + (i ^ turn)) for o in turns for i in turns]
        return lax.ppermute(value, "blk", pairs) if turn else value

    def along_outer(value, turn):
        pairs = [(o * side + i, (o ^ turn) * side + i) for o in turns for i in turns]
        return lax.ppermute(value, "blk", pairs) if turn else value

    def dot(lhs, rhs, dims):
        return lax.dot_general(lhs, rhs, (dims, ((), ())), preferred_element_type=jnp.float32)

    def lanes(value, index):
        return value[:, index * tile_size : (index + 1) * tile_size]

    def after(value, other):
        height, width = (min(a, b) for a, b in zip(value.shape, other.shape))
        part = other[:height, :width].astype(value.dtype) * 0
        part = jnp.concatenate([part] * (value.shape[1] // width), 1)
        return value + jnp.concatenate([part] * (value.shape[0] // height), 0)

    def columns_of(value, index):
        return lax.dynamic_slice_in_dim(value, index * cols_here, cols_here, 1)

    hidden_part = jnp.maximum(columns_of(hidden_pre, rep_pos), 0)

    columns = adj_cols[0]
    turn_of = (columns & (side - 1)) ^ inner_pos
    level_of = (columns >> bits) ^ outer_pos
    place = turn_of * per_core + (level_of & (per_core - 1))
    hit = place[None, :] == jnp.arange(section_span, dtype=jnp.int32)[:, None]
    ordered = jnp.zeros((section_span, tile_size, tile_size), bf16)
    for k in range(slots):
        ordered = jnp.where(hit[:, k, None, None], adj_vals[0, k][None], ordered)
    arrived = [
        along_inner(ordered[t * per_core : (t + 1) * per_core], t) for t in turns
    ]
    everyone = lax.all_gather(jnp.concatenate(arrived, 0), "rep", axis=0)
    rows = []
    for t in turns:
        row_block = outer_pos * side + (inner_pos ^ t)
        row = []
        for e in turns:
            column_block = (outer_pos ^ e) * side + inner_pos
            holder = ((row_block - column_block) & (blk_count - 1)) >> span_bits
            index = t * per_core + e % per_core
            piece = everyone[0, index]
            for r in range(1, rep_count):
                piece = jnp.where(holder == r, everyone[r, index], piece)
            row.append(piece)
        rows.append(jnp.concatenate(row, 1))
    block = jnp.concatenate(rows, 0)

    hidden_stack = jnp.concatenate([along_outer(hidden_part, e) for e in turns], 0)
    grad_part = columns_of(cotangent, rep_pos)
    grad_stack = jnp.concatenate([along_inner(grad_part, t) for t in turns], 0)

    mixed = dot(hidden_stack, block, ((0,), (1,))).astype(bf16)
    share = cols_here // side
    by_owner = mixed.reshape(share // rows_here, side, rows_here, side * tile_size)
    mixed_cols = 0.0
    for t in turns:
        chosen = lax.dynamic_index_in_dim(by_owner, inner_pos ^ t, 1, keepdims=False)
        chosen = chosen.reshape(share, side * tile_size)
        chosen = jnp.concatenate([lanes(chosen, u ^ t) for u in turns], 1)
        mixed_cols = mixed_cols + along_inner(chosen, t).astype(jnp.float32)

    back = after(dot(grad_stack, block, ((0,), (0,))), mixed).astype(bf16)
    back = sum(along_outer(lanes(back, e), e).astype(jnp.float32) for e in turns)

    mixed_cols = lax.all_gather(mixed_cols.astype(bf16), "rep", axis=0, tiled=True)
    weight_part = dot(mixed_cols, grad_stack, ((1,), (0,))).astype(bf16)
    by_outer = weight_part.reshape(side, rows_here, cols_here)
    grad_weight = sum(
        along_outer(
            lax.dynamic_index_in_dim(by_outer, outer_pos ^ t, 0, keepdims=False), t
        ).astype(jnp.float32)
        for t in turns
    )

    w_share = w_out.reshape(side, side, rows_here, feature_width)
    w_share = lax.dynamic_index_in_dim(w_share, inner_pos, 1, keepdims=False)
    w_share = columns_of(w_share.reshape(side * rows_here, feature_width), rep_pos)
    out_wide = dot(mixed_cols, w_share, ((0,), (0,))).astype(bf16)
    out_part = sum(
        along_inner(out_wide[t * tile_size : (t + 1) * tile_size], t).astype(jnp.float32)
        for t in turns
    ).astype(bf16)

    back = after(back, weight_part).astype(bf16)
    back_full = lax.all_gather(back, "rep", axis=0, tiled=True)
    w_rows = lax.dynamic_slice_in_dim(w_out, rep_pos * cols_here, cols_here, 0)
    grad_in = dot(back_full, w_rows, ((0,), (1,)))
    pre_part = columns_of(hidden_pre, rep_pos)
    grad_pre = jnp.where(pre_part > 0, grad_in, 0.0).astype(bf16)
    return (out_part, grad_weight, grad_pre)


def solution(mesh):
    placed = (P("blk", None), P("blk", "rep", None, None), P("blk", "rep"), P(), P("blk", None))
    return jax.shard_map(
        shards,
        mesh=mesh,
        in_specs=placed,
        out_specs=(P("blk", "rep"), P("blk", "rep"), P("blk", "rep")),
        check_vma=False,
    )
```

```python
import jax
import jax.numpy as jnp
from jax import lax
from jax.sharding import PartitionSpec as P


def shards(hidden_pre, adj_vals, adj_cols, w_out, cotangent):
    feature_width = hidden_pre.shape[1]
    slots, tile_size = adj_vals.shape[1:3]
    blk_count = lax.axis_size("blk")
    rep_count = lax.axis_size("rep")
    section_span = blk_count // rep_count
    bits = (blk_count.bit_length() - 1) // 2
    side = 1 << bits
    per_core = section_span // side
    blk_pos = lax.axis_index("blk")
    rep_pos = lax.axis_index("rep")
    outer_pos, inner_pos = blk_pos >> bits, blk_pos & (side - 1)
    span_bits = section_span.bit_length() - 1
    cols_here = feature_width // rep_count
    rows_here = feature_width // blk_count
    bf16 = jnp.bfloat16
    turns = range(side)

    def along_inner(value, turn):
        pairs = [(o * side + i, o * side + (i ^ turn)) for o in turns for i in turns]
        return lax.ppermute(value, "blk", pairs) if turn else value

    def along_outer(value, turn):
        pairs = [(o * side + i, (o ^ turn) * side + i) for o in turns for i in turns]
        return lax.ppermute(value, "blk", pairs) if turn else value

    def to_other(value):
        return lax.ppermute(value, "rep", [(0, 1), (1, 0)])

    def dot(lhs, rhs, dims):
        return lax.dot_general(lhs, rhs, (dims, ((), ())), preferred_element_type=jnp.float32)

    def lanes(value, index):
        return value[:, index * tile_size : (index + 1) * tile_size]

    def after(value, other):
        height, width = (min(a, b) for a, b in zip(value.shape, other.shape))
        part = other[:height, :width].astype(value.dtype) * 0
        part = jnp.concatenate([part] * (value.shape[1] // width), 1)
        return value + jnp.concatenate([part] * (value.shape[0] // height), 0)

    def columns_of(value, index):
        return lax.dynamic_slice_in_dim(value, index * cols_here, cols_here, 1)

    hidden_part = jnp.maximum(columns_of(hidden_pre, rep_pos), 0)

    columns = adj_cols[0]
    turn_of = (columns & (side - 1)) ^ inner_pos
    level_of = (columns >> bits) ^ outer_pos
    place = turn_of * per_core + (level_of & (per_core - 1))
    hit = place[None, :] == jnp.arange(section_span, dtype=jnp.int32)[:, None]
    ordered = jnp.zeros((section_span, tile_size, tile_size), bf16)
    for k in range(slots):
        ordered = jnp.where(hit[:, k, None, None], adj_vals[0, k][None], ordered)
    arrived = [
        along_inner(ordered[t * per_core : (t + 1) * per_core], t) for t in turns
    ]
    arrived = jnp.concatenate(arrived, 0)
    if rep_count == 2:
        everyone = [arrived, to_other(arrived)]
        first_holder = rep_pos
    else:
        everyone = lax.all_gather(arrived, "rep", axis=0)
        first_holder = 0
    rows = []
    for t in turns:
        row_block = outer_pos * side + (inner_pos ^ t)
        row = []
        for e in turns:
            column_block = (outer_pos ^ e) * side + inner_pos
            holder = ((row_block - column_block) & (blk_count - 1)) >> span_bits
            index = t * per_core + e % per_core
            piece = everyone[0][index]
            for r in range(1, rep_count):
                piece = jnp.where(holder ^ first_holder == r, everyone[r][index], piece)
            row.append(piece)
        rows.append(jnp.concatenate(row, 1))
    block = jnp.concatenate(rows, 0)

    hidden_stack = jnp.concatenate([along_outer(hidden_part, e) for e in turns], 0)
    grad_part = columns_of(cotangent, rep_pos)
    grad_stack = jnp.concatenate([along_inner(grad_part, t) for t in turns], 0)

    mixed = dot(hidden_stack, block, ((0,), (1,))).astype(bf16)
    share = cols_here // side
    by_owner = mixed.reshape(share // rows_here, side, rows_here, side * tile_size)
    mixed_cols = 0.0
    for t in turns:
        chosen = lax.dynamic_index_in_dim(by_owner, inner_pos ^ t, 1, keepdims=False)
        chosen = chosen.reshape(share, side * tile_size)
        chosen = jnp.concatenate([lanes(chosen, u ^ t) for u in turns], 1)
        mixed_cols = mixed_cols + along_inner(chosen, t).astype(jnp.float32)

    back = after(dot(grad_stack, block, ((0,), (0,))), mixed).astype(bf16)
    back = sum(along_outer(lanes(back, e), e).astype(jnp.float32) for e in turns)

    mixed_cols = lax.all_gather(mixed_cols.astype(bf16), "rep", axis=0, tiled=True)
    weight_part = dot(mixed_cols, grad_stack, ((1,), (0,))).astype(bf16)
    by_outer = weight_part.reshape(side, rows_here, cols_here)
    grad_weight = sum(
        along_outer(
            lax.dynamic_index_in_dim(by_outer, outer_pos ^ t, 0, keepdims=False), t
        ).astype(jnp.float32)
        for t in turns
    )

    w_share = w_out.reshape(side, side, rows_here, feature_width)
    w_share = lax.dynamic_index_in_dim(w_share, inner_pos, 1, keepdims=False)
    w_share = columns_of(w_share.reshape(side * rows_here, feature_width), rep_pos)
    out_wide = dot(mixed_cols, w_share, ((0,), (0,))).astype(bf16)
    out_part = sum(
        along_inner(out_wide[t * tile_size : (t + 1) * tile_size], t).astype(jnp.float32)
        for t in turns
    ).astype(bf16)

    back = after(back, out_wide).astype(bf16)
    w_rows = w_out.reshape(rep_count, cols_here, feature_width)
    if rep_count == 2:
        w_mine = columns_of(lax.dynamic_index_in_dim(w_rows, rep_pos, 0, keepdims=False), rep_pos)
        w_other = columns_of(
            lax.dynamic_index_in_dim(w_rows, 1 - rep_pos, 0, keepdims=False), rep_pos
        )
        grad_in = to_other(dot(back, w_other, ((0,), (1,))).astype(bf16)).astype(jnp.float32)
        grad_in = grad_in + dot(back, w_mine, ((0,), (1,)))
    else:
        back_full = lax.all_gather(back, "rep", axis=0, tiled=True)
        w_mine = lax.dynamic_index_in_dim(w_rows, rep_pos, 0, keepdims=False)
        grad_in = dot(back_full, w_mine, ((0,), (1,)))
    pre_part = columns_of(hidden_pre, rep_pos)
    grad_pre = jnp.where(pre_part > 0, grad_in, 0.0).astype(bf16)
    return (out_part, grad_weight, grad_pre)


def solution(mesh):
    placed = (P("blk", None), P("blk", "rep", None, None), P("blk", "rep"), P(), P("blk", None))
    return jax.shard_map(
        shards,
        mesh=mesh,
        in_specs=placed,
        out_specs=(P("blk", "rep"), P("blk", "rep"), P("blk", "rep")),
        check_vma=False,
    )
```

```python
import jax
import jax.numpy as jnp
from jax import lax
from jax.sharding import PartitionSpec as P


def shards(hidden_pre, adj_vals, adj_cols, w_out, cotangent):
    feature_width = hidden_pre.shape[1]
    slots, tile_size = adj_vals.shape[1:3]
    blk_count = lax.axis_size("blk")
    rep_count = lax.axis_size("rep")
    section_span = blk_count // rep_count
    bits = (blk_count.bit_length() - 1) // 2
    side = 1 << bits
    per_core = section_span // side
    blk_pos = lax.axis_index("blk")
    rep_pos = lax.axis_index("rep")
    outer_pos, inner_pos = blk_pos >> bits, blk_pos & (side - 1)
    span_bits = section_span.bit_length() - 1
    cols_here = feature_width // rep_count
    rows_here = feature_width // blk_count
    bf16 = jnp.bfloat16
    turns = range(side)
    rising = [1 << b for b in range(bits)]

    def along_inner(value, turn):
        pairs = [(o * side + i, o * side + (i ^ turn)) for o in turns for i in turns]
        return lax.ppermute(value, "blk", pairs) if turn else value

    def along_outer(value, turn):
        pairs = [(o * side + i, (o ^ turn) * side + i) for o in turns for i in turns]
        return lax.ppermute(value, "blk", pairs) if turn else value

    def halved(parts, move):
        parts = dict(enumerate(parts))
        size = parts[0].shape[0]
        for bit in rising:
            keys = [k for k in parts if not k & bit]
            sent = jnp.concatenate([parts[k ^ bit].astype(bf16) for k in keys], 0)
            got = move(sent, bit)
            parts = {
                k: parts[k].astype(jnp.float32)
                + got[n * size : (n + 1) * size].astype(jnp.float32)
                for n, k in enumerate(keys)
            }
        return parts[0]

    def to_other(value):
        return lax.ppermute(value, "rep", [(0, 1), (1, 0)])

    def dot(lhs, rhs, dims):
        return lax.dot_general(lhs, rhs, (dims, ((), ())), preferred_element_type=jnp.float32)

    def lanes(value, index):
        return value[:, index * tile_size : (index + 1) * tile_size]

    def after(value, other):
        height, width = (min(a, b) for a, b in zip(value.shape, other.shape))
        part = other[:height, :width].astype(value.dtype) * 0
        part = jnp.concatenate([part] * (value.shape[1] // width), 1)
        return value + jnp.concatenate([part] * (value.shape[0] // height), 0)

    def columns_of(value, index):
        return lax.dynamic_slice_in_dim(value, index * cols_here, cols_here, 1)

    hidden_part = jnp.maximum(columns_of(hidden_pre, rep_pos), 0)

    columns = adj_cols[0]
    turn_of = (columns & (side - 1)) ^ inner_pos
    level_of = (columns >> bits) ^ outer_pos
    place = turn_of * per_core + (level_of & (per_core - 1))
    hit = place[None, :] == jnp.arange(section_span, dtype=jnp.int32)[:, None]
    ordered = jnp.zeros((section_span, tile_size, tile_size), bf16)
    for k in range(slots):
        ordered = jnp.where(hit[:, k, None, None], adj_vals[0, k][None], ordered)
    arrived = [
        along_inner(ordered[t * per_core : (t + 1) * per_core], t) for t in turns
    ]
    everyone = lax.all_gather(jnp.concatenate(arrived, 0), "rep", axis=0)
    rows = []
    for t in turns:
        row_block = outer_pos * side + (inner_pos ^ t)
        row = []
        for e in turns:
            column_block = (outer_pos ^ e) * side + inner_pos
            holder = ((row_block - column_block) & (blk_count - 1)) >> span_bits
            index = t * per_core + e % per_core
            piece = everyone[0, index]
            for r in range(1, rep_count):
                piece = jnp.where(holder == r, everyone[r, index], piece)
            row.append(piece)
        rows.append(jnp.concatenate(row, 1))
    block = jnp.concatenate(rows, 0)

    hidden_stack = jnp.concatenate([along_outer(hidden_part, e) for e in turns], 0)
    grad_part = columns_of(cotangent, rep_pos)
    grad_stack = jnp.concatenate([along_inner(grad_part, t) for t in turns], 0)

    mixed = dot(hidden_stack, block, ((0,), (1,))).astype(bf16)
    share = cols_here // side
    by_owner = mixed.reshape(share // rows_here, side, rows_here, side * tile_size)
    mixed_cols = 0.0
    for t in turns:
        chosen = lax.dynamic_index_in_dim(by_owner, inner_pos ^ t, 1, keepdims=False)
        chosen = chosen.reshape(share, side * tile_size)
        chosen = jnp.concatenate([lanes(chosen, u ^ t) for u in turns], 1)
        mixed_cols = mixed_cols + along_inner(chosen, t).astype(jnp.float32)

    back = after(dot(grad_stack, block, ((0,), (0,))), mixed).astype(bf16)
    back = sum(along_outer(lanes(back, e), e).astype(jnp.float32) for e in turns)

    mixed_cols = lax.all_gather(mixed_cols.astype(bf16), "rep", axis=0, tiled=True)
    weight_part = dot(mixed_cols, grad_stack, ((1,), (0,))).astype(bf16)
    by_outer = weight_part.reshape(side, rows_here, cols_here)
    grad_weight = sum(
        along_outer(
            lax.dynamic_index_in_dim(by_outer, outer_pos ^ t, 0, keepdims=False), t
        ).astype(jnp.float32)
        for t in turns
    )

    w_share = w_out.reshape(side, side, rows_here, feature_width)
    w_share = lax.dynamic_index_in_dim(w_share, inner_pos, 1, keepdims=False)
    w_share = columns_of(w_share.reshape(side * rows_here, feature_width), rep_pos)
    out_part = dot(mixed_cols, w_share, ((0,), (0,)))
    out_part = halved(
        [out_part[t * tile_size : (t + 1) * tile_size] for t in turns], along_inner
    ).astype(bf16)

    back = after(back, weight_part).astype(bf16)
    w_rows = w_out.reshape(rep_count, cols_here, feature_width)
    if rep_count == 2:
        w_mine = columns_of(lax.dynamic_index_in_dim(w_rows, rep_pos, 0, keepdims=False), rep_pos)
        w_other = columns_of(
            lax.dynamic_index_in_dim(w_rows, 1 - rep_pos, 0, keepdims=False), rep_pos
        )
        grad_in = to_other(dot(back, w_other, ((0,), (1,))).astype(bf16)).astype(jnp.float32)
        grad_in = grad_in + dot(back, w_mine, ((0,), (1,)))
    else:
        back_full = lax.all_gather(back, "rep", axis=0, tiled=True)
        w_mine = lax.dynamic_index_in_dim(w_rows, rep_pos, 0, keepdims=False)
        grad_in = dot(back_full, w_mine, ((0,), (1,)))
    pre_part = columns_of(hidden_pre, rep_pos)
    grad_pre = jnp.where(pre_part > 0, grad_in, 0.0).astype(bf16)
    return (out_part, grad_weight, grad_pre)


def solution(mesh):
    placed = (P("blk", None), P("blk", "rep", None, None), P("blk", "rep"), P(), P("blk", None))
    return jax.shard_map(
        shards,
        mesh=mesh,
        in_specs=placed,
        out_specs=(P("blk", "rep"), P("blk", "rep"), P("blk", "rep")),
        check_vma=False,
    )
```

```python
import jax
import jax.numpy as jnp
from jax import lax
from jax.sharding import PartitionSpec as P


def shards(hidden_pre, adj_vals, adj_cols, w_out, cotangent):
    feature_width = hidden_pre.shape[1]
    slots, tile_size = adj_vals.shape[1:3]
    blk_count = lax.axis_size("blk")
    rep_count = lax.axis_size("rep")
    section_span = blk_count // rep_count
    bits = (blk_count.bit_length() - 1) // 2
    side = 1 << bits
    per_core = section_span // side
    blk_pos = lax.axis_index("blk")
    rep_pos = lax.axis_index("rep")
    outer_pos, inner_pos = blk_pos >> bits, blk_pos & (side - 1)
    span_bits = section_span.bit_length() - 1
    cols_here = feature_width // rep_count
    rows_here = feature_width // blk_count
    bf16 = jnp.bfloat16
    turns = range(side)
    rising = [1 << b for b in range(bits)]

    def along_inner(value, turn):
        pairs = [(o * side + i, o * side + (i ^ turn)) for o in turns for i in turns]
        return lax.ppermute(value, "blk", pairs) if turn else value

    def along_outer(value, turn):
        pairs = [(o * side + i, (o ^ turn) * side + i) for o in turns for i in turns]
        return lax.ppermute(value, "blk", pairs) if turn else value

    def halved(parts, move):
        parts = dict(enumerate(parts))
        size = parts[0].shape[0]
        arrived = []
        for bit in rising:
            keys = [k for k in parts if not k & bit]
            sent = jnp.concatenate([parts[k ^ bit].astype(bf16) for k in keys], 0)
            got = move(sent, bit)
            arrived.append(got)
            parts = {
                k: parts[k].astype(jnp.float32)
                + got[n * size : (n + 1) * size].astype(jnp.float32)
                for n, k in enumerate(keys)
            }
        return parts[0], arrived[0]

    def to_other(value):
        return lax.ppermute(value, "rep", [(0, 1), (1, 0)])

    def dot(lhs, rhs, dims):
        return lax.dot_general(lhs, rhs, (dims, ((), ())), preferred_element_type=jnp.float32)

    def lanes(value, index):
        return value[:, index * tile_size : (index + 1) * tile_size]

    def after(value, other):
        height, width = (min(a, b) for a, b in zip(value.shape, other.shape))
        part = other[:height, :width].astype(value.dtype) * 0
        part = jnp.concatenate([part] * (value.shape[1] // width), 1)
        return value + jnp.concatenate([part] * (value.shape[0] // height), 0)

    def columns_of(value, index):
        return lax.dynamic_slice_in_dim(value, index * cols_here, cols_here, 1)

    hidden_part = jnp.maximum(columns_of(hidden_pre, rep_pos), 0)

    columns = adj_cols[0]
    turn_of = (columns & (side - 1)) ^ inner_pos
    level_of = (columns >> bits) ^ outer_pos
    place = turn_of * per_core + (level_of & (per_core - 1))
    hit = place[None, :] == jnp.arange(section_span, dtype=jnp.int32)[:, None]
    ordered = jnp.zeros((section_span, tile_size, tile_size), bf16)
    for k in range(slots):
        ordered = jnp.where(hit[:, k, None, None], adj_vals[0, k][None], ordered)
    arrived = [
        along_inner(ordered[t * per_core : (t + 1) * per_core], t) for t in turns
    ]
    everyone = lax.all_gather(jnp.concatenate(arrived, 0), "rep", axis=0)
    rows = []
    for t in turns:
        row_block = outer_pos * side + (inner_pos ^ t)
        row = []
        for e in turns:
            column_block = (outer_pos ^ e) * side + inner_pos
            holder = ((row_block - column_block) & (blk_count - 1)) >> span_bits
            index = t * per_core + e % per_core
            piece = everyone[0, index]
            for r in range(1, rep_count):
                piece = jnp.where(holder == r, everyone[r, index], piece)
            row.append(piece)
        rows.append(jnp.concatenate(row, 1))
    block = jnp.concatenate(rows, 0)

    hidden_stack = jnp.concatenate([along_outer(hidden_part, e) for e in turns], 0)
    grad_part = columns_of(cotangent, rep_pos)
    grad_stack = jnp.concatenate([along_inner(grad_part, t) for t in turns], 0)

    mixed = dot(hidden_stack, block, ((0,), (1,))).astype(bf16)
    share = cols_here // side
    by_owner = mixed.reshape(share // rows_here, side, rows_here, side * tile_size)
    mixed_cols = 0.0
    for t in turns:
        chosen = lax.dynamic_index_in_dim(by_owner, inner_pos ^ t, 1, keepdims=False)
        chosen = chosen.reshape(share, side * tile_size)
        chosen = jnp.concatenate([lanes(chosen, u ^ t) for u in turns], 1)
        mixed_cols = mixed_cols + along_inner(chosen, t).astype(jnp.float32)

    back = after(dot(grad_stack, block, ((0,), (0,))), mixed).astype(bf16)
    back = sum(along_outer(lanes(back, e), e).astype(jnp.float32) for e in turns)

    mixed_cols = lax.all_gather(mixed_cols.astype(bf16), "rep", axis=0, tiled=True)
    w_share = w_out.reshape(side, side, rows_here, feature_width)
    w_share = lax.dynamic_index_in_dim(w_share, inner_pos, 1, keepdims=False)
    w_share = columns_of(w_share.reshape(side * rows_here, feature_width), rep_pos)
    out_wide = dot(mixed_cols, w_share, ((0,), (0,)))
    weight_part = after(dot(mixed_cols, grad_stack, ((1,), (0,))), out_wide).astype(bf16)
    by_outer = weight_part.reshape(side, rows_here, cols_here)
    grad_weight = sum(
        along_outer(
            lax.dynamic_index_in_dim(by_outer, outer_pos ^ t, 0, keepdims=False), t
        ).astype(jnp.float32)
        for t in turns
    )

    out_part, first_got = halved(
        [out_wide[t * tile_size : (t + 1) * tile_size] for t in turns], along_inner
    )
    out_part = out_part.astype(bf16)

    back = after(back, first_got).astype(bf16)
    w_rows = w_out.reshape(rep_count, cols_here, feature_width)
    if rep_count == 2:
        w_mine = columns_of(lax.dynamic_index_in_dim(w_rows, rep_pos, 0, keepdims=False), rep_pos)
        w_other = columns_of(
            lax.dynamic_index_in_dim(w_rows, 1 - rep_pos, 0, keepdims=False), rep_pos
        )
        grad_in = to_other(dot(back, w_other, ((0,), (1,))).astype(bf16)).astype(jnp.float32)
        grad_in = grad_in + dot(back, w_mine, ((0,), (1,)))
    else:
        back_full = lax.all_gather(back, "rep", axis=0, tiled=True)
        w_mine = lax.dynamic_index_in_dim(w_rows, rep_pos, 0, keepdims=False)
        grad_in = dot(back_full, w_mine, ((0,), (1,)))
    pre_part = columns_of(hidden_pre, rep_pos)
    grad_pre = jnp.where(pre_part > 0, grad_in, 0.0).astype(bf16)
    return (out_part, grad_weight, grad_pre)


def solution(mesh):
    placed = (P("blk", None), P("blk", "rep", None, None), P("blk", "rep"), P(), P("blk", None))
    return jax.shard_map(
        shards,
        mesh=mesh,
        in_specs=placed,
        out_specs=(P("blk", "rep"), P("blk", "rep"), P("blk", "rep")),
        check_vma=False,
    )
```

```python
import jax
import jax.numpy as jnp
from jax import lax
from jax.sharding import PartitionSpec as P


def shards(hidden_pre, adj_vals, adj_cols, w_out, cotangent):
    feature_width = hidden_pre.shape[1]
    slots, tile_size = adj_vals.shape[1:3]
    blk_count = lax.axis_size("blk")
    rep_count = lax.axis_size("rep")
    section_span = blk_count // rep_count
    bits = (blk_count.bit_length() - 1) // 2
    side = 1 << bits
    per_core = section_span // side
    blk_pos = lax.axis_index("blk")
    rep_pos = lax.axis_index("rep")
    outer_pos, inner_pos = blk_pos >> bits, blk_pos & (side - 1)
    span_bits = section_span.bit_length() - 1
    cols_here = feature_width // rep_count
    rows_here = feature_width // blk_count
    bf16 = jnp.bfloat16
    turns = range(side)
    rising = [1 << b for b in range(bits)]

    def along_inner(value, turn):
        pairs = [(o * side + i, o * side + (i ^ turn)) for o in turns for i in turns]
        return lax.ppermute(value, "blk", pairs) if turn else value

    def along_outer(value, turn):
        pairs = [(o * side + i, (o ^ turn) * side + i) for o in turns for i in turns]
        return lax.ppermute(value, "blk", pairs) if turn else value

    def halved(parts, move):
        parts = dict(enumerate(parts))
        size = parts[0].shape[0]
        for bit in rising:
            keys = [k for k in parts if not k & bit]
            sent = jnp.concatenate([parts[k ^ bit].astype(bf16) for k in keys], 0)
            got = move(sent, bit)
            parts = {
                k: parts[k].astype(jnp.float32)
                + got[n * size : (n + 1) * size].astype(jnp.float32)
                for n, k in enumerate(keys)
            }
        return parts[0]

    def to_other(value):
        return lax.ppermute(value, "rep", [(0, 1), (1, 0)])

    def dot(lhs, rhs, dims):
        return lax.dot_general(lhs, rhs, (dims, ((), ())), preferred_element_type=jnp.float32)

    def lanes(value, index):
        return value[:, index * tile_size : (index + 1) * tile_size]

    def after(value, other):
        height, width = (min(a, b) for a, b in zip(value.shape, other.shape))
        part = other[:height, :width].astype(value.dtype) * 0
        part = jnp.concatenate([part] * (value.shape[1] // width), 1)
        return value + jnp.concatenate([part] * (value.shape[0] // height), 0)

    def columns_of(value, index):
        return lax.dynamic_slice_in_dim(value, index * cols_here, cols_here, 1)

    hidden_part = jnp.maximum(columns_of(hidden_pre, rep_pos), 0)

    columns = adj_cols[0]
    turn_of = (columns & (side - 1)) ^ inner_pos
    level_of = (columns >> bits) ^ outer_pos
    place = turn_of * per_core + (level_of & (per_core - 1))
    hit = place[None, :] == jnp.arange(section_span, dtype=jnp.int32)[:, None]
    ordered = jnp.zeros((section_span, tile_size, tile_size), bf16)
    for k in range(slots):
        ordered = jnp.where(hit[:, k, None, None], adj_vals[0, k][None], ordered)
    arrived = [
        along_inner(ordered[t * per_core : (t + 1) * per_core], t) for t in turns
    ]
    everyone = lax.all_gather(jnp.concatenate(arrived, 0), "rep", axis=0)
    rows = []
    for t in turns:
        row_block = outer_pos * side + (inner_pos ^ t)
        row = []
        for e in turns:
            column_block = (outer_pos ^ e) * side + inner_pos
            holder = ((row_block - column_block) & (blk_count - 1)) >> span_bits
            index = t * per_core + e % per_core
            piece = everyone[0, index]
            for r in range(1, rep_count):
                piece = jnp.where(holder == r, everyone[r, index], piece)
            row.append(piece)
        rows.append(jnp.concatenate(row, 1))
    block = jnp.concatenate(rows, 0)

    hidden_stack = jnp.concatenate([along_outer(hidden_part, e) for e in turns], 0)
    grad_part = columns_of(cotangent, rep_pos)
    grad_stack = jnp.concatenate([along_inner(grad_part, t) for t in turns], 0)

    mixed = dot(hidden_stack, block, ((0,), (1,))).astype(bf16)
    share = cols_here // side
    by_owner = mixed.reshape(share // rows_here, side, rows_here, side * tile_size)
    mixed_cols = 0.0
    for t in turns:
        chosen = lax.dynamic_index_in_dim(by_owner, inner_pos ^ t, 1, keepdims=False)
        chosen = chosen.reshape(share, side * tile_size)
        chosen = jnp.concatenate([lanes(chosen, u ^ t) for u in turns], 1)
        mixed_cols = mixed_cols + along_inner(chosen, t).astype(jnp.float32)

    back = after(dot(grad_stack, block, ((0,), (0,))), mixed).astype(bf16)
    back = sum(along_outer(lanes(back, e), e).astype(jnp.float32) for e in turns)

    mixed_cols = lax.all_gather(mixed_cols.astype(bf16), "rep", axis=0, tiled=True)
    w_share = w_out.reshape(side, side, rows_here, feature_width)
    w_share = lax.dynamic_index_in_dim(w_share, inner_pos, 1, keepdims=False)
    w_share = columns_of(w_share.reshape(side * rows_here, feature_width), rep_pos)
    out_part = dot(mixed_cols, w_share, ((0,), (0,)))
    weight_part = after(dot(mixed_cols, grad_stack, ((1,), (0,))), out_part)
    by_outer = weight_part.reshape(side, rows_here, cols_here)
    grad_weight = halved(
        [lax.dynamic_index_in_dim(by_outer, outer_pos ^ t, 0, keepdims=False) for t in turns],
        along_outer,
    )
    out_part = halved(
        [out_part[t * tile_size : (t + 1) * tile_size] for t in turns], along_inner
    ).astype(bf16)

    back = after(back, weight_part).astype(bf16)
    w_rows = w_out.reshape(rep_count, cols_here, feature_width)
    if rep_count == 2:
        w_mine = columns_of(lax.dynamic_index_in_dim(w_rows, rep_pos, 0, keepdims=False), rep_pos)
        w_other = columns_of(
            lax.dynamic_index_in_dim(w_rows, 1 - rep_pos, 0, keepdims=False), rep_pos
        )
        grad_in = to_other(dot(back, w_other, ((0,), (1,))).astype(bf16)).astype(jnp.float32)
        grad_in = grad_in + dot(back, w_mine, ((0,), (1,)))
    else:
        back_full = lax.all_gather(back, "rep", axis=0, tiled=True)
        w_mine = lax.dynamic_index_in_dim(w_rows, rep_pos, 0, keepdims=False)
        grad_in = dot(back_full, w_mine, ((0,), (1,)))
    pre_part = columns_of(hidden_pre, rep_pos)
    grad_pre = jnp.where(pre_part > 0, grad_in, 0.0).astype(bf16)
    return (out_part, grad_weight, grad_pre)


def solution(mesh):
    placed = (P("blk", None), P("blk", "rep", None, None), P("blk", "rep"), P(), P("blk", None))
    return jax.shard_map(
        shards,
        mesh=mesh,
        in_specs=placed,
        out_specs=(P("blk", "rep"), P("blk", "rep"), P("blk", "rep")),
        check_vma=False,
    )
```

```python
import jax
import jax.numpy as jnp
from jax import lax
from jax.sharding import PartitionSpec as P


def shards(hidden_pre, adj_vals, adj_cols, w_out, cotangent):
    feature_width = hidden_pre.shape[1]
    slots, tile_size = adj_vals.shape[1:3]
    blk_count = lax.axis_size("blk")
    rep_count = lax.axis_size("rep")
    section_span = blk_count // rep_count
    bits = (blk_count.bit_length() - 1) // 2
    side = 1 << bits
    per_core = section_span // side
    blk_pos = lax.axis_index("blk")
    rep_pos = lax.axis_index("rep")
    outer_pos, inner_pos = blk_pos >> bits, blk_pos & (side - 1)
    span_bits = section_span.bit_length() - 1
    cols_here = feature_width // rep_count
    rows_here = feature_width // blk_count
    bf16 = jnp.bfloat16
    turns = range(side)
    rising = [1 << b for b in range(bits)]

    def along_inner(value, turn):
        pairs = [(o * side + i, o * side + (i ^ turn)) for o in turns for i in turns]
        return lax.ppermute(value, "blk", pairs) if turn else value

    def along_outer(value, turn):
        pairs = [(o * side + i, (o ^ turn) * side + i) for o in turns for i in turns]
        return lax.ppermute(value, "blk", pairs) if turn else value

    def halved(parts, move):
        parts = dict(enumerate(parts))
        size = parts[0].shape[0]
        for bit in rising:
            keys = [k for k in parts if not k & bit]
            sent = jnp.concatenate([parts[k ^ bit].astype(bf16) for k in keys], 0)
            last = got = move(sent, bit)
            parts = {
                k: parts[k].astype(jnp.float32)
                + got[n * size : (n + 1) * size].astype(jnp.float32)
                for n, k in enumerate(keys)
            }
        return parts[0], last

    def to_other(value):
        return lax.ppermute(value, "rep", [(0, 1), (1, 0)])

    def dot(lhs, rhs, dims):
        return lax.dot_general(lhs, rhs, (dims, ((), ())), preferred_element_type=jnp.float32)

    def lanes(value, index):
        return value[:, index * tile_size : (index + 1) * tile_size]

    def after(value, other):
        height, width = (min(a, b) for a, b in zip(value.shape, other.shape))
        part = other[:height, :width].astype(value.dtype) * 0
        part = jnp.concatenate([part] * (value.shape[1] // width), 1)
        return value + jnp.concatenate([part] * (value.shape[0] // height), 0)

    def columns_of(value, index):
        return lax.dynamic_slice_in_dim(value, index * cols_here, cols_here, 1)

    hidden_part = jnp.maximum(columns_of(hidden_pre, rep_pos), 0)

    columns = adj_cols[0]
    turn_of = (columns & (side - 1)) ^ inner_pos
    level_of = (columns >> bits) ^ outer_pos
    place = turn_of * per_core + (level_of & (per_core - 1))
    hit = place[None, :] == jnp.arange(section_span, dtype=jnp.int32)[:, None]
    ordered = jnp.zeros((section_span, tile_size, tile_size), bf16)
    for k in range(slots):
        ordered = jnp.where(hit[:, k, None, None], adj_vals[0, k][None], ordered)
    arrived = [
        along_inner(ordered[t * per_core : (t + 1) * per_core], t) for t in turns
    ]
    everyone = lax.all_gather(jnp.concatenate(arrived, 0), "rep", axis=0)
    rows = []
    for t in turns:
        row_block = outer_pos * side + (inner_pos ^ t)
        row = []
        for e in turns:
            column_block = (outer_pos ^ e) * side + inner_pos
            holder = ((row_block - column_block) & (blk_count - 1)) >> span_bits
            index = t * per_core + e % per_core
            piece = everyone[0, index]
            for r in range(1, rep_count):
                piece = jnp.where(holder == r, everyone[r, index], piece)
            row.append(piece)
        rows.append(jnp.concatenate(row, 1))
    block = jnp.concatenate(rows, 0)

    hidden_stack = jnp.concatenate([along_outer(hidden_part, e) for e in turns], 0)
    grad_part = columns_of(cotangent, rep_pos)
    grad_stack = jnp.concatenate([along_inner(grad_part, t) for t in turns], 0)

    mixed = dot(hidden_stack, block, ((0,), (1,))).astype(bf16)
    share = cols_here // side
    by_owner = mixed.reshape(share // rows_here, side, rows_here, side * tile_size)
    mixed_cols = 0.0
    for t in turns:
        chosen = lax.dynamic_index_in_dim(by_owner, inner_pos ^ t, 1, keepdims=False)
        chosen = chosen.reshape(share, side * tile_size)
        chosen = jnp.concatenate([lanes(chosen, u ^ t) for u in turns], 1)
        mixed_cols = mixed_cols + along_inner(chosen, t).astype(jnp.float32)

    back = after(dot(grad_stack, block, ((0,), (0,))), mixed).astype(bf16)
    back = sum(along_outer(lanes(back, e), e).astype(jnp.float32) for e in turns)

    mixed_cols = lax.all_gather(mixed_cols.astype(bf16), "rep", axis=0, tiled=True)
    w_share = w_out.reshape(side, side, rows_here, feature_width)
    w_share = lax.dynamic_index_in_dim(w_share, inner_pos, 1, keepdims=False)
    w_share = columns_of(w_share.reshape(side * rows_here, feature_width), rep_pos)
    out_part = dot(mixed_cols, w_share, ((0,), (0,)))
    weight_part = after(dot(mixed_cols, grad_stack, ((1,), (0,))), out_part)
    by_outer = weight_part.reshape(side, rows_here, cols_here)
    grad_weight, weight_last = halved(
        [lax.dynamic_index_in_dim(by_outer, outer_pos ^ t, 0, keepdims=False) for t in turns],
        along_outer,
    )
    out_part, _ = halved(
        [out_part[t * tile_size : (t + 1) * tile_size] for t in turns], along_inner
    )
    out_part = out_part.astype(bf16)

    back = after(back, weight_part).astype(bf16)
    w_rows = w_out.reshape(rep_count, cols_here, feature_width)
    if rep_count == 2:
        w_mine = columns_of(lax.dynamic_index_in_dim(w_rows, rep_pos, 0, keepdims=False), rep_pos)
        w_other = columns_of(
            lax.dynamic_index_in_dim(w_rows, 1 - rep_pos, 0, keepdims=False), rep_pos
        )
        grad_in = to_other(dot(back, w_other, ((0,), (1,))).astype(bf16)).astype(jnp.float32)
        grad_in = grad_in + dot(back, w_mine, ((0,), (1,)))
    else:
        back_full = lax.all_gather(back, "rep", axis=0, tiled=True)
        w_mine = lax.dynamic_index_in_dim(w_rows, rep_pos, 0, keepdims=False)
        grad_in = dot(back_full, w_mine, ((0,), (1,)))
    grad_pre = jnp.where(hidden_part > 0, after(grad_in, weight_last), 0.0).astype(bf16)
    return (out_part, grad_weight, grad_pre)


def solution(mesh):
    placed = (P("blk", None), P("blk", "rep", None, None), P("blk", "rep"), P(), P("blk", None))
    return jax.shard_map(
        shards,
        mesh=mesh,
        in_specs=placed,
        out_specs=(P("blk", "rep"), P("blk", "rep"), P("blk", "rep")),
        check_vma=False,
    )
```

```python
import jax
import jax.numpy as jnp
from jax import lax
from jax.sharding import PartitionSpec as P


def shards(hidden_pre, adj_vals, adj_cols, w_out, cotangent):
    feature_width = hidden_pre.shape[1]
    slots, tile_size = adj_vals.shape[1:3]
    blk_count = lax.axis_size("blk")
    rep_count = lax.axis_size("rep")
    section_span = blk_count // rep_count
    bits = (blk_count.bit_length() - 1) // 2
    side = 1 << bits
    per_core = section_span // side
    blk_pos = lax.axis_index("blk")
    rep_pos = lax.axis_index("rep")
    outer_pos, inner_pos = blk_pos >> bits, blk_pos & (side - 1)
    span_bits = section_span.bit_length() - 1
    cols_here = feature_width // rep_count
    rows_here = feature_width // blk_count
    bf16 = jnp.bfloat16
    turns = range(side)
    rising = [1 << b for b in range(bits)]

    def along_inner(value, turn):
        pairs = [(o * side + i, o * side + (i ^ turn)) for o in turns for i in turns]
        return lax.ppermute(value, "blk", pairs) if turn else value

    def along_outer(value, turn):
        pairs = [(o * side + i, (o ^ turn) * side + i) for o in turns for i in turns]
        return lax.ppermute(value, "blk", pairs) if turn else value

    def halved(parts, move):
        parts = dict(enumerate(parts))
        size = parts[0].shape[0]
        for bit in rising:
            keys = [k for k in parts if not k & bit]
            sent = jnp.concatenate([parts[k ^ bit].astype(bf16) for k in keys], 0)
            got = move(sent, bit)
            parts = {
                k: parts[k].astype(jnp.float32)
                + got[n * size : (n + 1) * size].astype(jnp.float32)
                for n, k in enumerate(keys)
            }
        return parts[0]

    def to_other(value):
        return lax.ppermute(value, "rep", [(0, 1), (1, 0)])

    def dot(lhs, rhs, dims):
        return lax.dot_general(lhs, rhs, (dims, ((), ())), preferred_element_type=jnp.float32)

    def lanes(value, index):
        return value[:, index * tile_size : (index + 1) * tile_size]

    def after(value, other):
        height, width = (min(a, b) for a, b in zip(value.shape, other.shape))
        part = other[:height, :width].astype(value.dtype) * 0
        part = jnp.concatenate([part] * (value.shape[1] // width), 1)
        return value + jnp.concatenate([part] * (value.shape[0] // height), 0)

    def columns_of(value, index):
        return lax.dynamic_slice_in_dim(value, index * cols_here, cols_here, 1)

    hidden_part = jnp.maximum(columns_of(hidden_pre, rep_pos), 0)

    columns = adj_cols[0]
    turn_of = (columns & (side - 1)) ^ inner_pos
    level_of = (columns >> bits) ^ outer_pos
    place = turn_of * per_core + (level_of & (per_core - 1))
    hit = place[None, :] == jnp.arange(section_span, dtype=jnp.int32)[:, None]
    ordered = jnp.zeros((section_span, tile_size, tile_size), bf16)
    for k in range(slots):
        ordered = jnp.where(hit[:, k, None, None], adj_vals[0, k][None], ordered)
    arrived = [
        along_inner(ordered[t * per_core : (t + 1) * per_core], t) for t in turns
    ]
    hidden_stack = [along_outer(hidden_part, e) for e in turns]
    ready = sum(lanes(part, 0) * 0 for part in hidden_stack[2:])
    everyone = lax.all_gather(jnp.concatenate(arrived, 0) + ready, "rep", axis=0)
    rows = []
    for t in turns:
        row_block = outer_pos * side + (inner_pos ^ t)
        row = []
        for e in turns:
            column_block = (outer_pos ^ e) * side + inner_pos
            holder = ((row_block - column_block) & (blk_count - 1)) >> span_bits
            index = t * per_core + e % per_core
            piece = everyone[0, index]
            for r in range(1, rep_count):
                piece = jnp.where(holder == r, everyone[r, index], piece)
            row.append(piece)
        rows.append(jnp.concatenate(row, 1))
    block = jnp.concatenate(rows, 0)

    hidden_stack = jnp.concatenate(hidden_stack, 0)
    grad_part = columns_of(cotangent, rep_pos)
    grad_stack = jnp.concatenate([along_inner(grad_part, t) for t in turns], 0)

    mixed = dot(hidden_stack, block, ((0,), (1,))).astype(bf16)
    share = cols_here // side
    by_owner = mixed.reshape(share // rows_here, side, rows_here, side * tile_size)
    mixed_cols = 0.0
    for t in turns:
        chosen = lax.dynamic_index_in_dim(by_owner, inner_pos ^ t, 1, keepdims=False)
        chosen = chosen.reshape(share, side * tile_size)
        chosen = jnp.concatenate([lanes(chosen, u ^ t) for u in turns], 1)
        mixed_cols = mixed_cols + along_inner(chosen, t).astype(jnp.float32)

    back = after(dot(grad_stack, block, ((0,), (0,))), mixed).astype(bf16)
    back = sum(along_outer(lanes(back, e), e).astype(jnp.float32) for e in turns)

    mixed_cols = lax.all_gather(mixed_cols.astype(bf16), "rep", axis=0, tiled=True)
    w_share = w_out.reshape(side, side, rows_here, feature_width)
    w_share = lax.dynamic_index_in_dim(w_share, inner_pos, 1, keepdims=False)
    w_share = columns_of(w_share.reshape(side * rows_here, feature_width), rep_pos)
    out_part = dot(mixed_cols, w_share, ((0,), (0,)))
    weight_part = after(dot(mixed_cols, grad_stack, ((1,), (0,))), out_part)
    by_outer = weight_part.reshape(side, rows_here, cols_here)
    grad_weight = halved(
        [lax.dynamic_index_in_dim(by_outer, outer_pos ^ t, 0, keepdims=False) for t in turns],
        along_outer,
    )
    out_part = halved(
        [out_part[t * tile_size : (t + 1) * tile_size] for t in turns], along_inner
    ).astype(bf16)

    back = after(back, weight_part).astype(bf16)
    w_rows = w_out.reshape(rep_count, cols_here, feature_width)
    if rep_count == 2:
        w_mine = columns_of(lax.dynamic_index_in_dim(w_rows, rep_pos, 0, keepdims=False), rep_pos)
        w_other = columns_of(
            lax.dynamic_index_in_dim(w_rows, 1 - rep_pos, 0, keepdims=False), rep_pos
        )
        grad_in = to_other(dot(back, w_other, ((0,), (1,))).astype(bf16)).astype(jnp.float32)
        grad_in = grad_in + dot(back, w_mine, ((0,), (1,)))
    else:
        back_full = lax.all_gather(back, "rep", axis=0, tiled=True)
        w_mine = lax.dynamic_index_in_dim(w_rows, rep_pos, 0, keepdims=False)
        grad_in = dot(back_full, w_mine, ((0,), (1,)))
    pre_part = columns_of(hidden_pre, rep_pos)
    grad_pre = jnp.where(pre_part > 0, grad_in, 0.0).astype(bf16)
    return (out_part, grad_weight, grad_pre)


def solution(mesh):
    placed = (P("blk", None), P("blk", "rep", None, None), P("blk", "rep"), P(), P("blk", None))
    return jax.shard_map(
        shards,
        mesh=mesh,
        in_specs=placed,
        out_specs=(P("blk", "rep"), P("blk", "rep"), P("blk", "rep")),
        check_vma=False,
    )
```

```python
import jax
import jax.numpy as jnp
from jax import lax
from jax.sharding import PartitionSpec as P


def shards(hidden_pre, adj_vals, adj_cols, w_out, cotangent):
    feature_width = hidden_pre.shape[1]
    slots, tile_size = adj_vals.shape[1:3]
    blk_count = lax.axis_size("blk")
    rep_count = lax.axis_size("rep")
    section_span = blk_count // rep_count
    bits = (blk_count.bit_length() - 1) // 2
    side = 1 << bits
    per_core = section_span // side
    blk_pos = lax.axis_index("blk")
    rep_pos = lax.axis_index("rep")
    outer_pos, inner_pos = blk_pos >> bits, blk_pos & (side - 1)
    span_bits = section_span.bit_length() - 1
    cols_here = feature_width // rep_count
    rows_here = feature_width // blk_count
    bf16 = jnp.bfloat16
    turns = range(side)
    rising = [1 << b for b in range(bits)]

    def along_inner(value, turn):
        pairs = [(o * side + i, o * side + (i ^ turn)) for o in turns for i in turns]
        return lax.ppermute(value, "blk", pairs) if turn else value

    def along_outer(value, turn):
        pairs = [(o * side + i, (o ^ turn) * side + i) for o in turns for i in turns]
        return lax.ppermute(value, "blk", pairs) if turn else value

    def halved(parts, move):
        parts = dict(enumerate(parts))
        size = parts[0].shape[0]
        for bit in rising:
            keys = [k for k in parts if not k & bit]
            sent = jnp.concatenate([parts[k ^ bit].astype(bf16) for k in keys], 0)
            got = move(sent, bit)
            parts = {
                k: parts[k].astype(jnp.float32)
                + got[n * size : (n + 1) * size].astype(jnp.float32)
                for n, k in enumerate(keys)
            }
        return parts[0]

    def to_other(value):
        return lax.ppermute(value, "rep", [(0, 1), (1, 0)])

    def dot(lhs, rhs, dims):
        return lax.dot_general(lhs, rhs, (dims, ((), ())), preferred_element_type=jnp.float32)

    def lanes(value, index):
        return value[:, index * tile_size : (index + 1) * tile_size]

    def after(value, other):
        height, width = (min(a, b) for a, b in zip(value.shape, other.shape))
        part = other[:height, :width].astype(value.dtype) * 0
        part = jnp.concatenate([part] * (value.shape[1] // width), 1)
        return value + jnp.concatenate([part] * (value.shape[0] // height), 0)

    def columns_of(value, index):
        return lax.dynamic_slice_in_dim(value, index * cols_here, cols_here, 1)

    hidden_part = jnp.maximum(columns_of(hidden_pre, rep_pos), 0)

    columns = adj_cols[0]
    turn_of = (columns & (side - 1)) ^ inner_pos
    level_of = (columns >> bits) ^ outer_pos
    place = turn_of * per_core + (level_of & (per_core - 1))
    hit = place[None, :] == jnp.arange(section_span, dtype=jnp.int32)[:, None]
    ordered = jnp.zeros((section_span, tile_size, tile_size), bf16)
    for k in range(slots):
        ordered = jnp.where(hit[:, k, None, None], adj_vals[0, k][None], ordered)
    arrived = [
        along_inner(ordered[t * per_core : (t + 1) * per_core], t) for t in turns
    ]
    everyone = lax.all_gather(jnp.concatenate(arrived, 0), "rep", axis=0)
    rows = []
    for t in turns:
        row_block = outer_pos * side + (inner_pos ^ t)
        row = []
        for e in turns:
            column_block = (outer_pos ^ e) * side + inner_pos
            holder = ((row_block - column_block) & (blk_count - 1)) >> span_bits
            index = t * per_core + e % per_core
            piece = everyone[0, index]
            for r in range(1, rep_count):
                piece = jnp.where(holder == r, everyone[r, index], piece)
            row.append(piece)
        rows.append(jnp.concatenate(row, 1))
    block = jnp.concatenate(rows, 0)

    hidden_stack = jnp.concatenate([along_outer(hidden_part, e) for e in turns], 0)
    grad_part = columns_of(cotangent, rep_pos)
    grad_stack = jnp.concatenate([along_inner(grad_part, t) for t in turns], 0)

    mixed = dot(hidden_stack, block, ((0,), (1,))).astype(bf16)
    share = cols_here // side
    by_owner = mixed.reshape(share // rows_here, side, rows_here, side * tile_size)
    mixed_cols = 0.0
    for t in turns:
        chosen = lax.dynamic_index_in_dim(by_owner, inner_pos ^ t, 1, keepdims=False)
        chosen = chosen.reshape(share, side * tile_size)
        chosen = jnp.concatenate([lanes(chosen, u ^ t) for u in turns], 1)
        mixed_cols = mixed_cols + along_inner(chosen, t).astype(jnp.float32)

    back = after(dot(grad_stack, block, ((0,), (0,))), mixed).astype(bf16)
    back = sum(along_outer(lanes(back, e), e).astype(jnp.float32) for e in turns)

    mixed_cols = lax.all_gather(mixed_cols.astype(bf16), "rep", axis=0, tiled=True)
    w_share = w_out.reshape(side, side, rows_here, feature_width)
    w_share = lax.dynamic_index_in_dim(w_share, inner_pos, 1, keepdims=False)
    w_share = columns_of(w_share.reshape(side * rows_here, feature_width), rep_pos)
    out_part = dot(mixed_cols, w_share, ((0,), (0,))).astype(bf16)
    weight_part = after(dot(mixed_cols, grad_stack, ((1,), (0,))), out_part).astype(bf16)
    by_outer = weight_part.reshape(side, rows_here, cols_here)
    grad_weight = halved(
        [lax.dynamic_index_in_dim(by_outer, outer_pos ^ t, 0, keepdims=False) for t in turns],
        along_outer,
    )
    out_part = halved(
        [out_part[t * tile_size : (t + 1) * tile_size] for t in turns], along_inner
    ).astype(bf16)

    back = after(back, weight_part).astype(bf16)
    w_rows = w_out.reshape(rep_count, cols_here, feature_width)
    if rep_count == 2:
        w_mine = columns_of(lax.dynamic_index_in_dim(w_rows, rep_pos, 0, keepdims=False), rep_pos)
        w_other = columns_of(
            lax.dynamic_index_in_dim(w_rows, 1 - rep_pos, 0, keepdims=False), rep_pos
        )
        grad_in = to_other(dot(back, w_other, ((0,), (1,))).astype(bf16)).astype(jnp.float32)
        grad_in = grad_in + dot(back, w_mine, ((0,), (1,)))
    else:
        back_full = lax.all_gather(back, "rep", axis=0, tiled=True)
        w_mine = lax.dynamic_index_in_dim(w_rows, rep_pos, 0, keepdims=False)
        grad_in = dot(back_full, w_mine, ((0,), (1,)))
    grad_pre = jnp.where(hidden_part > 0, grad_in, 0.0).astype(bf16)
    return (out_part, grad_weight, grad_pre)


def solution(mesh):
    placed = (P("blk", None), P("blk", "rep", None, None), P("blk", "rep"), P(), P("blk", None))
    return jax.shard_map(
        shards,
        mesh=mesh,
        in_specs=placed,
        out_specs=(P("blk", "rep"), P("blk", "rep"), P("blk", "rep")),
        check_vma=False,
    )
```

```python
import jax
import jax.numpy as jnp
from jax import lax
from jax.sharding import PartitionSpec as P


def shards(hidden_pre, adj_vals, adj_cols, w_out, cotangent):
    feature_width = hidden_pre.shape[1]
    slots, tile_size = adj_vals.shape[1:3]
    blk_count = lax.axis_size("blk")
    rep_count = lax.axis_size("rep")
    section_span = blk_count // rep_count
    bits = (blk_count.bit_length() - 1) // 2
    side = 1 << bits
    per_core = section_span // side
    blk_pos = lax.axis_index("blk")
    rep_pos = lax.axis_index("rep")
    outer_pos, inner_pos = blk_pos >> bits, blk_pos & (side - 1)
    span_bits = section_span.bit_length() - 1
    cols_here = feature_width // rep_count
    rows_here = feature_width // blk_count
    bf16 = jnp.bfloat16
    turns = range(side)
    rising = [1 << b for b in range(bits)]

    def along_inner(value, turn):
        pairs = [(o * side + i, o * side + (i ^ turn)) for o in turns for i in turns]
        return lax.ppermute(value, "blk", pairs) if turn else value

    def along_outer(value, turn):
        pairs = [(o * side + i, (o ^ turn) * side + i) for o in turns for i in turns]
        return lax.ppermute(value, "blk", pairs) if turn else value

    def halved(parts, move):
        parts = dict(enumerate(parts))
        size = parts[0].shape[0]
        arrived = []
        for bit in rising:
            keys = [k for k in parts if not k & bit]
            sent = jnp.concatenate([parts[k ^ bit].astype(bf16) for k in keys], 0)
            got = move(sent, bit)
            arrived.append(got)
            parts = {
                k: parts[k].astype(jnp.float32)
                + got[n * size : (n + 1) * size].astype(jnp.float32)
                for n, k in enumerate(keys)
            }
        return parts[0], arrived[0]

    def to_other(value):
        return lax.ppermute(value, "rep", [(0, 1), (1, 0)])

    def dot(lhs, rhs, dims):
        return lax.dot_general(lhs, rhs, (dims, ((), ())), preferred_element_type=jnp.float32)

    def lanes(value, index):
        return value[:, index * tile_size : (index + 1) * tile_size]

    def after(value, other):
        height, width = (min(a, b) for a, b in zip(value.shape, other.shape))
        part = other[:height, :width].astype(value.dtype) * 0
        part = jnp.concatenate([part] * (value.shape[1] // width), 1)
        return value + jnp.concatenate([part] * (value.shape[0] // height), 0)

    def columns_of(value, index):
        return lax.dynamic_slice_in_dim(value, index * cols_here, cols_here, 1)

    hidden_part = jnp.maximum(columns_of(hidden_pre, rep_pos), 0)

    columns = adj_cols[0]
    turn_of = (columns & (side - 1)) ^ inner_pos
    level_of = (columns >> bits) ^ outer_pos
    place = turn_of * per_core + (level_of & (per_core - 1))
    hit = place[None, :] == jnp.arange(section_span, dtype=jnp.int32)[:, None]
    ordered = jnp.zeros((section_span, tile_size, tile_size), bf16)
    for k in range(slots):
        ordered = jnp.where(hit[:, k, None, None], adj_vals[0, k][None], ordered)
    arrived = [
        along_inner(ordered[t * per_core : (t + 1) * per_core], t) for t in turns
    ]
    everyone = lax.all_gather(jnp.concatenate(arrived, 0), "rep", axis=0)
    rows = []
    for t in turns:
        row_block = outer_pos * side + (inner_pos ^ t)
        row = []
        for e in turns:
            column_block = (outer_pos ^ e) * side + inner_pos
            holder = ((row_block - column_block) & (blk_count - 1)) >> span_bits
            index = t * per_core + e % per_core
            piece = everyone[0, index]
            for r in range(1, rep_count):
                piece = jnp.where(holder == r, everyone[r, index], piece)
            row.append(piece)
        rows.append(jnp.concatenate(row, 1))
    block = jnp.concatenate(rows, 0)

    hidden_stack = jnp.concatenate([along_outer(hidden_part, e) for e in turns], 0)
    grad_part = columns_of(cotangent, rep_pos)
    grad_stack = jnp.concatenate([along_inner(grad_part, t) for t in turns], 0)

    mixed = dot(hidden_stack, block, ((0,), (1,))).astype(bf16)
    share = cols_here // side
    by_owner = mixed.reshape(share // rows_here, side, rows_here, side * tile_size)
    mixed_cols = 0.0
    for t in turns:
        chosen = lax.dynamic_index_in_dim(by_owner, inner_pos ^ t, 1, keepdims=False)
        chosen = chosen.reshape(share, side * tile_size)
        chosen = jnp.concatenate([lanes(chosen, u ^ t) for u in turns], 1)
        mixed_cols = mixed_cols + along_inner(chosen, t).astype(jnp.float32)

    back = after(dot(grad_stack, block, ((0,), (0,))), mixed).astype(bf16)
    back = sum(along_outer(lanes(back, e), e).astype(jnp.float32) for e in turns)

    mixed_cols = lax.all_gather(mixed_cols.astype(bf16), "rep", axis=0, tiled=True)
    w_share = w_out.reshape(side, side, rows_here, feature_width)
    w_share = lax.dynamic_index_in_dim(w_share, inner_pos, 1, keepdims=False)
    w_share = columns_of(w_share.reshape(side * rows_here, feature_width), rep_pos)
    out_part = dot(mixed_cols, w_share, ((0,), (0,)))
    weight_part = after(dot(mixed_cols, grad_stack, ((1,), (0,))), out_part)
    by_outer = weight_part.reshape(side, rows_here, cols_here)
    grad_weight, _ = halved(
        [lax.dynamic_index_in_dim(by_outer, outer_pos ^ t, 0, keepdims=False) for t in turns],
        along_outer,
    )
    out_part, out_first = halved(
        [out_part[t * tile_size : (t + 1) * tile_size] for t in turns], along_inner
    )
    out_part = out_part.astype(bf16)

    back = after(back, out_first).astype(bf16)
    w_rows = w_out.reshape(rep_count, cols_here, feature_width)
    if rep_count == 2:
        w_mine = columns_of(lax.dynamic_index_in_dim(w_rows, rep_pos, 0, keepdims=False), rep_pos)
        w_other = columns_of(
            lax.dynamic_index_in_dim(w_rows, 1 - rep_pos, 0, keepdims=False), rep_pos
        )
        grad_in = to_other(dot(back, w_other, ((0,), (1,))).astype(bf16)).astype(jnp.float32)
        grad_in = grad_in + dot(back, w_mine, ((0,), (1,)))
    else:
        back_full = lax.all_gather(back, "rep", axis=0, tiled=True)
        w_mine = lax.dynamic_index_in_dim(w_rows, rep_pos, 0, keepdims=False)
        grad_in = dot(back_full, w_mine, ((0,), (1,)))
    pre_part = columns_of(hidden_pre, rep_pos)
    grad_pre = jnp.where(pre_part > 0, grad_in, 0.0).astype(bf16)
    return (out_part, grad_weight, grad_pre)


def solution(mesh):
    placed = (P("blk", None), P("blk", "rep", None, None), P("blk", "rep"), P(), P("blk", None))
    return jax.shard_map(
        shards,
        mesh=mesh,
        in_specs=placed,
        out_specs=(P("blk", "rep"), P("blk", "rep"), P("blk", "rep")),
        check_vma=False,
    )
```

```python
import jax
import jax.numpy as jnp
from jax import lax
from jax.sharding import PartitionSpec as P


def shards(hidden_pre, adj_vals, adj_cols, w_out, cotangent):
    feature_width = hidden_pre.shape[1]
    slots, tile_size = adj_vals.shape[1:3]
    blk_count = lax.axis_size("blk")
    rep_count = lax.axis_size("rep")
    section_span = blk_count // rep_count
    bits = (blk_count.bit_length() - 1) // 2
    side = 1 << bits
    per_core = section_span // side
    blk_pos = lax.axis_index("blk")
    rep_pos = lax.axis_index("rep")
    outer_pos, inner_pos = blk_pos >> bits, blk_pos & (side - 1)
    span_bits = section_span.bit_length() - 1
    cols_here = feature_width // rep_count
    rows_here = feature_width // blk_count
    bf16 = jnp.bfloat16
    turns = range(side)
    rising = [1 << b for b in range(bits)]

    def along_inner(value, turn):
        pairs = [(o * side + i, o * side + (i ^ turn)) for o in turns for i in turns]
        return lax.ppermute(value, "blk", pairs) if turn else value

    def along_outer(value, turn):
        pairs = [(o * side + i, (o ^ turn) * side + i) for o in turns for i in turns]
        return lax.ppermute(value, "blk", pairs) if turn else value

    def halved(parts, move):
        parts = dict(enumerate(parts))
        size = parts[0].shape[0]
        for bit in rising:
            keys = [k for k in parts if not k & bit]
            sent = jnp.concatenate([parts[k ^ bit].astype(bf16) for k in keys], 0)
            got = move(sent, bit)
            parts = {
                k: parts[k].astype(jnp.float32)
                + got[n * size : (n + 1) * size].astype(jnp.float32)
                for n, k in enumerate(keys)
            }
        return parts[0]

    def to_other(value):
        return lax.ppermute(value, "rep", [(0, 1), (1, 0)])

    def dot(lhs, rhs, dims):
        return lax.dot_general(lhs, rhs, (dims, ((), ())), preferred_element_type=jnp.float32)

    def lanes(value, index):
        return value[:, index * tile_size : (index + 1) * tile_size]

    def after(value, other):
        height, width = (min(a, b) for a, b in zip(value.shape, other.shape))
        part = other[:height, :width].astype(value.dtype) * 0
        part = jnp.concatenate([part] * (value.shape[1] // width), 1)
        return value + jnp.concatenate([part] * (value.shape[0] // height), 0)

    def columns_of(value, index):
        return lax.dynamic_slice_in_dim(value, index * cols_here, cols_here, 1)

    hidden_part = jnp.maximum(columns_of(hidden_pre, rep_pos), 0)

    columns = adj_cols[0]
    turn_of = (columns & (side - 1)) ^ inner_pos
    level_of = (columns >> bits) ^ outer_pos
    place = turn_of * per_core + (level_of & (per_core - 1))
    hit = place[None, :] == jnp.arange(section_span, dtype=jnp.int32)[:, None]
    ordered = jnp.zeros((section_span, tile_size, tile_size), bf16)
    for k in range(slots):
        ordered = jnp.where(hit[:, k, None, None], adj_vals[0, k][None], ordered)
    arrived = [
        along_inner(ordered[t * per_core : (t + 1) * per_core], t) for t in turns
    ]
    hidden_stack = [along_outer(hidden_part, e) for e in turns]
    arrived = jnp.concatenate(arrived, 0)
    if rep_count == 2:
        ready = sum(lanes(part, 0) * 0 for part in hidden_stack[2:])
        everyone = [arrived, to_other(arrived + ready)]
        first_holder = rep_pos
    else:
        everyone = lax.all_gather(arrived, "rep", axis=0)
        first_holder = 0
    rows = []
    for t in turns:
        row_block = outer_pos * side + (inner_pos ^ t)
        row = []
        for e in turns:
            column_block = (outer_pos ^ e) * side + inner_pos
            holder = ((row_block - column_block) & (blk_count - 1)) >> span_bits
            index = t * per_core + e % per_core
            piece = everyone[0][index]
            for r in range(1, rep_count):
                piece = jnp.where(holder ^ first_holder == r, everyone[r][index], piece)
            row.append(piece)
        rows.append(jnp.concatenate(row, 1))
    block = jnp.concatenate(rows, 0)

    hidden_stack = jnp.concatenate(hidden_stack, 0)
    grad_part = columns_of(cotangent, rep_pos)
    grad_stack = jnp.concatenate([along_inner(grad_part, t) for t in turns], 0)

    mixed = dot(hidden_stack, block, ((0,), (1,))).astype(bf16)
    share = cols_here // side
    by_owner = mixed.reshape(share // rows_here, side, rows_here, side * tile_size)
    mixed_cols = 0.0
    for t in turns:
        chosen = lax.dynamic_index_in_dim(by_owner, inner_pos ^ t, 1, keepdims=False)
        chosen = chosen.reshape(share, side * tile_size)
        chosen = jnp.concatenate([lanes(chosen, u ^ t) for u in turns], 1)
        mixed_cols = mixed_cols + along_inner(chosen, t).astype(jnp.float32)

    back = after(dot(grad_stack, block, ((0,), (0,))), mixed).astype(bf16)
    back = sum(along_outer(lanes(back, e), e).astype(jnp.float32) for e in turns)

    mixed_cols = lax.all_gather(mixed_cols.astype(bf16), "rep", axis=0, tiled=True)
    w_share = w_out.reshape(side, side, rows_here, feature_width)
    w_share = lax.dynamic_index_in_dim(w_share, inner_pos, 1, keepdims=False)
    w_share = columns_of(w_share.reshape(side * rows_here, feature_width), rep_pos)
    out_part = dot(mixed_cols, w_share, ((0,), (0,)))
    weight_part = after(dot(mixed_cols, grad_stack, ((1,), (0,))), out_part)
    by_outer = weight_part.reshape(side, rows_here, cols_here)
    grad_weight = halved(
        [lax.dynamic_index_in_dim(by_outer, outer_pos ^ t, 0, keepdims=False) for t in turns],
        along_outer,
    )
    out_part = halved(
        [out_part[t * tile_size : (t + 1) * tile_size] for t in turns], along_inner
    ).astype(bf16)

    back = after(back, weight_part).astype(bf16)
    w_rows = w_out.reshape(rep_count, cols_here, feature_width)
    if rep_count == 2:
        w_mine = columns_of(lax.dynamic_index_in_dim(w_rows, rep_pos, 0, keepdims=False), rep_pos)
        w_other = columns_of(
            lax.dynamic_index_in_dim(w_rows, 1 - rep_pos, 0, keepdims=False), rep_pos
        )
        grad_in = to_other(dot(back, w_other, ((0,), (1,))).astype(bf16)).astype(jnp.float32)
        grad_in = grad_in + dot(back, w_mine, ((0,), (1,)))
    else:
        back_full = lax.all_gather(back, "rep", axis=0, tiled=True)
        w_mine = lax.dynamic_index_in_dim(w_rows, rep_pos, 0, keepdims=False)
        grad_in = dot(back_full, w_mine, ((0,), (1,)))
    pre_part = columns_of(hidden_pre, rep_pos)
    grad_pre = jnp.where(pre_part > 0, grad_in, 0.0).astype(bf16)
    return (out_part, grad_weight, grad_pre)


def solution(mesh):
    placed = (P("blk", None), P("blk", "rep", None, None), P("blk", "rep"), P(), P("blk", None))
    return jax.shard_map(
        shards,
        mesh=mesh,
        in_specs=placed,
        out_specs=(P("blk", "rep"), P("blk", "rep"), P("blk", "rep")),
        check_vma=False,
    )
```

```python
import jax
import jax.numpy as jnp
from jax import lax
from jax.sharding import PartitionSpec as P


def shards(hidden_pre, adj_vals, adj_cols, w_out, cotangent):
    feature_width = hidden_pre.shape[1]
    slots, tile_size = adj_vals.shape[1:3]
    blk_count = lax.axis_size("blk")
    rep_count = lax.axis_size("rep")
    section_span = blk_count // rep_count
    bits = (blk_count.bit_length() - 1) // 2
    side = 1 << bits
    per_core = section_span // side
    blk_pos = lax.axis_index("blk")
    rep_pos = lax.axis_index("rep")
    outer_pos, inner_pos = blk_pos >> bits, blk_pos & (side - 1)
    span_bits = section_span.bit_length() - 1
    cols_here = feature_width // rep_count
    rows_here = feature_width // blk_count
    bf16 = jnp.bfloat16
    turns = range(side)
    rising = [1 << b for b in range(bits)]

    def along_inner(value, turn):
        pairs = [(o * side + i, o * side + (i ^ turn)) for o in turns for i in turns]
        return lax.ppermute(value, "blk", pairs) if turn else value

    def along_outer(value, turn):
        pairs = [(o * side + i, (o ^ turn) * side + i) for o in turns for i in turns]
        return lax.ppermute(value, "blk", pairs) if turn else value

    def halved(parts, move, late):
        parts = dict(enumerate(parts))
        size = parts[0].shape[0]
        for bit in rising:
            keys = [k for k in parts if not k & bit]
            sent = jnp.concatenate([parts[k ^ bit].astype(bf16) for k in keys], 0)
            if bit == rising[-1]:
                for other in late:
                    sent = after(sent, other)
            got = move(sent, bit)
            parts = {
                k: parts[k].astype(jnp.float32)
                + got[n * size : (n + 1) * size].astype(jnp.float32)
                for n, k in enumerate(keys)
            }
        return parts[0]

    def to_other(value):
        return lax.ppermute(value, "rep", [(0, 1), (1, 0)])

    def dot(lhs, rhs, dims):
        return lax.dot_general(lhs, rhs, (dims, ((), ())), preferred_element_type=jnp.float32)

    def lanes(value, index):
        return value[:, index * tile_size : (index + 1) * tile_size]

    def after(value, other):
        height, width = (min(a, b) for a, b in zip(value.shape, other.shape))
        part = other[:height, :width].astype(value.dtype) * 0
        part = jnp.concatenate([part] * (value.shape[1] // width), 1)
        return value + jnp.concatenate([part] * (value.shape[0] // height), 0)

    def columns_of(value, index):
        return lax.dynamic_slice_in_dim(value, index * cols_here, cols_here, 1)

    hidden_part = jnp.maximum(columns_of(hidden_pre, rep_pos), 0)

    columns = adj_cols[0]
    turn_of = (columns & (side - 1)) ^ inner_pos
    level_of = (columns >> bits) ^ outer_pos
    place = turn_of * per_core + (level_of & (per_core - 1))
    hit = place[None, :] == jnp.arange(section_span, dtype=jnp.int32)[:, None]
    ordered = jnp.zeros((section_span, tile_size, tile_size), bf16)
    for k in range(slots):
        ordered = jnp.where(hit[:, k, None, None], adj_vals[0, k][None], ordered)
    arrived = [
        along_inner(ordered[t * per_core : (t + 1) * per_core], t) for t in turns
    ]
    everyone = lax.all_gather(jnp.concatenate(arrived, 0), "rep", axis=0)
    rows = []
    for t in turns:
        row_block = outer_pos * side + (inner_pos ^ t)
        row = []
        for e in turns:
            column_block = (outer_pos ^ e) * side + inner_pos
            holder = ((row_block - column_block) & (blk_count - 1)) >> span_bits
            index = t * per_core + e % per_core
            piece = everyone[0, index]
            for r in range(1, rep_count):
                piece = jnp.where(holder == r, everyone[r, index], piece)
            row.append(piece)
        rows.append(jnp.concatenate(row, 1))
    block = jnp.concatenate(rows, 0)

    hidden_stack = jnp.concatenate([along_outer(hidden_part, e) for e in turns], 0)
    grad_part = columns_of(cotangent, rep_pos)
    grad_stack = jnp.concatenate([along_inner(grad_part, t) for t in turns], 0)

    mixed = dot(hidden_stack, block, ((0,), (1,))).astype(bf16)
    share = cols_here // side
    by_owner = mixed.reshape(share // rows_here, side, rows_here, side * tile_size)
    mixed_cols = 0.0
    for t in turns:
        chosen = lax.dynamic_index_in_dim(by_owner, inner_pos ^ t, 1, keepdims=False)
        chosen = chosen.reshape(share, side * tile_size)
        chosen = jnp.concatenate([lanes(chosen, u ^ t) for u in turns], 1)
        mixed_cols = mixed_cols + along_inner(chosen, t).astype(jnp.float32)

    back = after(dot(grad_stack, block, ((0,), (0,))), mixed).astype(bf16)
    back = sum(along_outer(lanes(back, e), e).astype(jnp.float32) for e in turns)

    mixed_cols = lax.all_gather(mixed_cols.astype(bf16), "rep", axis=0, tiled=True)
    w_share = w_out.reshape(side, side, rows_here, feature_width)
    w_share = lax.dynamic_index_in_dim(w_share, inner_pos, 1, keepdims=False)
    w_share = columns_of(w_share.reshape(side * rows_here, feature_width), rep_pos)
    out_part = dot(mixed_cols, w_share, ((0,), (0,)))
    out_part = out_part.astype(bf16)
    out_got = [
        along_inner(out_part[t * tile_size : (t + 1) * tile_size], t) for t in turns
    ]
    weight_part = after(dot(mixed_cols, grad_stack, ((1,), (0,))), out_part)
    by_outer = weight_part.reshape(side, rows_here, cols_here)
    grad_weight = halved(
        [lax.dynamic_index_in_dim(by_outer, outer_pos ^ t, 0, keepdims=False) for t in turns],
        along_outer,
        out_got[1:],
    )
    out_part = sum(part.astype(jnp.float32) for part in out_got).astype(bf16)

    back = after(back, weight_part).astype(bf16)
    w_rows = w_out.reshape(rep_count, cols_here, feature_width)
    if rep_count == 2:
        w_mine = columns_of(lax.dynamic_index_in_dim(w_rows, rep_pos, 0, keepdims=False), rep_pos)
        w_other = columns_of(
            lax.dynamic_index_in_dim(w_rows, 1 - rep_pos, 0, keepdims=False), rep_pos
        )
        grad_in = to_other(dot(back, w_other, ((0,), (1,))).astype(bf16)).astype(jnp.float32)
        grad_in = grad_in + dot(back, w_mine, ((0,), (1,)))
    else:
        back_full = lax.all_gather(back, "rep", axis=0, tiled=True)
        w_mine = lax.dynamic_index_in_dim(w_rows, rep_pos, 0, keepdims=False)
        grad_in = dot(back_full, w_mine, ((0,), (1,)))
    pre_part = columns_of(hidden_pre, rep_pos)
    grad_pre = jnp.where(pre_part > 0, grad_in, 0.0).astype(bf16)
    return (out_part, grad_weight, grad_pre)


def solution(mesh):
    placed = (P("blk", None), P("blk", "rep", None, None), P("blk", "rep"), P(), P("blk", None))
    return jax.shard_map(
        shards,
        mesh=mesh,
        in_specs=placed,
        out_specs=(P("blk", "rep"), P("blk", "rep"), P("blk", "rep")),
        check_vma=False,
    )
```

```python
import jax
import jax.numpy as jnp
from jax import lax
from jax.sharding import PartitionSpec as P


def shards(hidden_pre, adj_vals, adj_cols, w_out, cotangent):
    feature_width = hidden_pre.shape[1]
    slots, tile_size = adj_vals.shape[1:3]
    blk_count = lax.axis_size("blk")
    rep_count = lax.axis_size("rep")
    section_span = blk_count // rep_count
    bits = (blk_count.bit_length() - 1) // 2
    side = 1 << bits
    per_core = section_span // side
    blk_pos = lax.axis_index("blk")
    rep_pos = lax.axis_index("rep")
    outer_pos, inner_pos = blk_pos >> bits, blk_pos & (side - 1)
    span_bits = section_span.bit_length() - 1
    cols_here = feature_width // rep_count
    rows_here = feature_width // blk_count
    bf16 = jnp.bfloat16
    turns = range(side)
    rising = [1 << b for b in range(bits)]

    def along_inner(value, turn):
        pairs = [(o * side + i, o * side + (i ^ turn)) for o in turns for i in turns]
        return lax.ppermute(value, "blk", pairs) if turn else value

    def along_outer(value, turn):
        pairs = [(o * side + i, (o ^ turn) * side + i) for o in turns for i in turns]
        return lax.ppermute(value, "blk", pairs) if turn else value

    def halved(parts, move, late):
        parts = dict(enumerate(parts))
        size = parts[0].shape[0]
        for bit in rising:
            keys = [k for k in parts if not k & bit]
            sent = jnp.concatenate([parts[k ^ bit].astype(bf16) for k in keys], 0)
            if bit == rising[-1]:
                for other in late:
                    sent = after(sent, other)
            got = move(sent, bit)
            parts = {
                k: parts[k].astype(jnp.float32)
                + got[n * size : (n + 1) * size].astype(jnp.float32)
                for n, k in enumerate(keys)
            }
        return parts[0]

    def to_other(value):
        return lax.ppermute(value, "rep", [(0, 1), (1, 0)])

    def dot(lhs, rhs, dims):
        return lax.dot_general(lhs, rhs, (dims, ((), ())), preferred_element_type=jnp.float32)

    def lanes(value, index):
        return value[:, index * tile_size : (index + 1) * tile_size]

    def after(value, other):
        height, width = (min(a, b) for a, b in zip(value.shape, other.shape))
        part = other[:height, :width].astype(value.dtype) * 0
        part = jnp.concatenate([part] * (value.shape[1] // width), 1)
        return value + jnp.concatenate([part] * (value.shape[0] // height), 0)

    def columns_of(value, index):
        return lax.dynamic_slice_in_dim(value, index * cols_here, cols_here, 1)

    hidden_part = jnp.maximum(columns_of(hidden_pre, rep_pos), 0)

    columns = adj_cols[0]
    turn_of = (columns & (side - 1)) ^ inner_pos
    level_of = (columns >> bits) ^ outer_pos
    place = turn_of * per_core + (level_of & (per_core - 1))
    hit = place[None, :] == jnp.arange(section_span, dtype=jnp.int32)[:, None]
    ordered = jnp.zeros((section_span, tile_size, tile_size), bf16)
    for k in range(slots):
        ordered = jnp.where(hit[:, k, None, None], adj_vals[0, k][None], ordered)
    arrived = [
        along_inner(ordered[t * per_core : (t + 1) * per_core], t) for t in turns
    ]
    everyone = lax.all_gather(jnp.concatenate(arrived, 0), "rep", axis=0)
    rows = []
    for t in turns:
        row_block = outer_pos * side + (inner_pos ^ t)
        row = []
        for e in turns:
            column_block = (outer_pos ^ e) * side + inner_pos
            holder = ((row_block - column_block) & (blk_count - 1)) >> span_bits
            index = t * per_core + e % per_core
            piece = everyone[0, index]
            for r in range(1, rep_count):
                piece = jnp.where(holder == r, everyone[r, index], piece)
            row.append(piece)
        rows.append(jnp.concatenate(row, 1))
    block = jnp.concatenate(rows, 0)

    hidden_stack = jnp.concatenate([along_outer(hidden_part, e) for e in turns], 0)
    grad_part = columns_of(cotangent, rep_pos)
    grad_stack = jnp.concatenate([along_inner(grad_part, t) for t in turns], 0)

    mixed = dot(hidden_stack, block, ((0,), (1,))).astype(bf16)
    share = cols_here // side
    by_owner = mixed.reshape(share // rows_here, side, rows_here, side * tile_size)
    mixed_cols = 0.0
    for t in turns:
        chosen = lax.dynamic_index_in_dim(by_owner, inner_pos ^ t, 1, keepdims=False)
        chosen = chosen.reshape(share, side * tile_size)
        chosen = jnp.concatenate([lanes(chosen, u ^ t) for u in turns], 1)
        mixed_cols = mixed_cols + along_inner(chosen, t).astype(jnp.float32)

    back = after(dot(grad_stack, block, ((0,), (0,))), mixed).astype(bf16)
    back = sum(along_outer(lanes(back, e), e).astype(jnp.float32) for e in turns)

    mixed_cols = lax.all_gather(mixed_cols.astype(bf16), "rep", axis=0, tiled=True)
    w_share = w_out.reshape(side, side, rows_here, feature_width)
    w_share = lax.dynamic_index_in_dim(w_share, inner_pos, 1, keepdims=False)
    w_share = columns_of(w_share.reshape(side * rows_here, feature_width), rep_pos)
    out_part = dot(mixed_cols, w_share, ((0,), (0,)))
    out_part = out_part.astype(bf16)
    out_got = [
        along_inner(out_part[t * tile_size : (t + 1) * tile_size], t) for t in turns
    ]
    weight_part = after(dot(mixed_cols, grad_stack, ((1,), (0,))), out_part)
    by_outer = weight_part.reshape(side, rows_here, cols_here)
    grad_weight = halved(
        [lax.dynamic_index_in_dim(by_outer, outer_pos ^ t, 0, keepdims=False) for t in turns],
        along_outer,
        out_got[1:2],
    )
    out_part = sum(part.astype(jnp.float32) for part in out_got).astype(bf16)

    back = after(back, weight_part).astype(bf16)
    w_rows = w_out.reshape(rep_count, cols_here, feature_width)
    if rep_count == 2:
        w_mine = columns_of(lax.dynamic_index_in_dim(w_rows, rep_pos, 0, keepdims=False), rep_pos)
        w_other = columns_of(
            lax.dynamic_index_in_dim(w_rows, 1 - rep_pos, 0, keepdims=False), rep_pos
        )
        grad_in = to_other(dot(back, w_other, ((0,), (1,))).astype(bf16)).astype(jnp.float32)
        grad_in = grad_in + dot(back, w_mine, ((0,), (1,)))
    else:
        back_full = lax.all_gather(back, "rep", axis=0, tiled=True)
        w_mine = lax.dynamic_index_in_dim(w_rows, rep_pos, 0, keepdims=False)
        grad_in = dot(back_full, w_mine, ((0,), (1,)))
    pre_part = columns_of(hidden_pre, rep_pos)
    grad_pre = jnp.where(pre_part > 0, grad_in, 0.0).astype(bf16)
    return (out_part, grad_weight, grad_pre)


def solution(mesh):
    placed = (P("blk", None), P("blk", "rep", None, None), P("blk", "rep"), P(), P("blk", None))
    return jax.shard_map(
        shards,
        mesh=mesh,
        in_specs=placed,
        out_specs=(P("blk", "rep"), P("blk", "rep"), P("blk", "rep")),
        check_vma=False,
    )
```

```python
import jax
import jax.numpy as jnp
from jax import lax
from jax.sharding import PartitionSpec as P


def shards(hidden_pre, adj_vals, adj_cols, w_out, cotangent):
    feature_width = hidden_pre.shape[1]
    slots, tile_size = adj_vals.shape[1:3]
    blk_count = lax.axis_size("blk")
    rep_count = lax.axis_size("rep")
    section_span = blk_count // rep_count
    bits = (blk_count.bit_length() - 1) // 2
    side = 1 << bits
    per_core = section_span // side
    blk_pos = lax.axis_index("blk")
    rep_pos = lax.axis_index("rep")
    outer_pos, inner_pos = blk_pos >> bits, blk_pos & (side - 1)
    span_bits = section_span.bit_length() - 1
    cols_here = feature_width // rep_count
    rows_here = feature_width // blk_count
    bf16 = jnp.bfloat16
    turns = range(side)
    rising = [1 << b for b in range(bits)]

    def along_inner(value, turn):
        pairs = [(o * side + i, o * side + (i ^ turn)) for o in turns for i in turns]
        return lax.ppermute(value, "blk", pairs) if turn else value

    def along_outer(value, turn):
        pairs = [(o * side + i, (o ^ turn) * side + i) for o in turns for i in turns]
        return lax.ppermute(value, "blk", pairs) if turn else value

    def halved(parts, move):
        parts = dict(enumerate(parts))
        size = parts[0].shape[0]
        for bit in rising:
            keys = [k for k in parts if not k & bit]
            sent = jnp.concatenate([parts[k ^ bit].astype(bf16) for k in keys], 0)
            got = move(sent, bit)
            parts = {
                k: parts[k].astype(jnp.float32)
                + got[n * size : (n + 1) * size].astype(jnp.float32)
                for n, k in enumerate(keys)
            }
        return parts[0]

    def to_other(value):
        return lax.ppermute(value, "rep", [(0, 1), (1, 0)])

    def dot(lhs, rhs, dims):
        return lax.dot_general(lhs, rhs, (dims, ((), ())), preferred_element_type=jnp.float32)

    def lanes(value, index):
        return value[:, index * tile_size : (index + 1) * tile_size]

    def after(value, other):
        height, width = (min(a, b) for a, b in zip(value.shape, other.shape))
        part = other[:height, :width].astype(value.dtype) * 0
        part = jnp.concatenate([part] * (value.shape[1] // width), 1)
        return value + jnp.concatenate([part] * (value.shape[0] // height), 0)

    def columns_of(value, index):
        return lax.dynamic_slice_in_dim(value, index * cols_here, cols_here, 1)

    hidden_part = jnp.maximum(columns_of(hidden_pre, rep_pos), 0)

    columns = adj_cols[0]
    turn_of = (columns & (side - 1)) ^ inner_pos
    level_of = (columns >> bits) ^ outer_pos
    place = turn_of * per_core + (level_of & (per_core - 1))
    hit = place[None, :] == jnp.arange(section_span, dtype=jnp.int32)[:, None]
    ordered = jnp.zeros((section_span, tile_size, tile_size), bf16)
    for k in range(slots):
        ordered = jnp.where(hit[:, k, None, None], adj_vals[0, k][None], ordered)
    arrived = [
        along_inner(ordered[t * per_core : (t + 1) * per_core], t) for t in turns
    ]
    everyone = lax.all_gather(jnp.concatenate(arrived, 0), "rep", axis=0)
    rows = []
    for t in turns:
        row_block = outer_pos * side + (inner_pos ^ t)
        row = []
        for e in turns:
            column_block = (outer_pos ^ e) * side + inner_pos
            holder = ((row_block - column_block) & (blk_count - 1)) >> span_bits
            index = t * per_core + e % per_core
            piece = everyone[0, index]
            for r in range(1, rep_count):
                piece = jnp.where(holder == r, everyone[r, index], piece)
            row.append(piece)
        rows.append(jnp.concatenate(row, 1))
    block = jnp.concatenate(rows, 0)

    hidden_stack = jnp.concatenate([along_outer(hidden_part, e) for e in turns], 0)
    mixed = dot(hidden_stack, block, ((0,), (1,))).astype(bf16)
    share = cols_here // side
    by_owner = mixed.reshape(share // rows_here, side, rows_here, side * tile_size)
    mixed_cols = 0.0
    for t in turns:
        chosen = lax.dynamic_index_in_dim(by_owner, inner_pos ^ t, 1, keepdims=False)
        chosen = chosen.reshape(share, side * tile_size)
        chosen = jnp.concatenate([lanes(chosen, u ^ t) for u in turns], 1)
        mixed_cols = mixed_cols + along_inner(chosen, t).astype(jnp.float32)

    grad_part = after(columns_of(cotangent, rep_pos), mixed)
    grad_stack = jnp.concatenate([along_inner(grad_part, t) for t in turns], 0)
    back = dot(grad_stack, block, ((0,), (0,))).astype(bf16)
    back = sum(along_outer(lanes(back, e), e).astype(jnp.float32) for e in turns)

    mixed_cols = lax.all_gather(mixed_cols.astype(bf16), "rep", axis=0, tiled=True)
    w_share = w_out.reshape(side, side, rows_here, feature_width)
    w_share = lax.dynamic_index_in_dim(w_share, inner_pos, 1, keepdims=False)
    w_share = columns_of(w_share.reshape(side * rows_here, feature_width), rep_pos)
    out_part = dot(mixed_cols, w_share, ((0,), (0,)))
    weight_part = after(dot(mixed_cols, grad_stack, ((1,), (0,))), out_part)
    by_outer = weight_part.reshape(side, rows_here, cols_here)
    grad_weight = halved(
        [lax.dynamic_index_in_dim(by_outer, outer_pos ^ t, 0, keepdims=False) for t in turns],
        along_outer,
    )
    out_part = halved(
        [out_part[t * tile_size : (t + 1) * tile_size] for t in turns], along_inner
    ).astype(bf16)

    back = after(back, weight_part).astype(bf16)
    w_rows = w_out.reshape(rep_count, cols_here, feature_width)
    if rep_count == 2:
        w_mine = columns_of(lax.dynamic_index_in_dim(w_rows, rep_pos, 0, keepdims=False), rep_pos)
        w_other = columns_of(
            lax.dynamic_index_in_dim(w_rows, 1 - rep_pos, 0, keepdims=False), rep_pos
        )
        grad_in = to_other(dot(back, w_other, ((0,), (1,))).astype(bf16)).astype(jnp.float32)
        grad_in = grad_in + dot(back, w_mine, ((0,), (1,)))
    else:
        back_full = lax.all_gather(back, "rep", axis=0, tiled=True)
        w_mine = lax.dynamic_index_in_dim(w_rows, rep_pos, 0, keepdims=False)
        grad_in = dot(back_full, w_mine, ((0,), (1,)))
    pre_part = columns_of(hidden_pre, rep_pos)
    grad_pre = jnp.where(pre_part > 0, grad_in, 0.0).astype(bf16)
    return (out_part, grad_weight, grad_pre)


def solution(mesh):
    placed = (P("blk", None), P("blk", "rep", None, None), P("blk", "rep"), P(), P("blk", None))
    return jax.shard_map(
        shards,
        mesh=mesh,
        in_specs=placed,
        out_specs=(P("blk", "rep"), P("blk", "rep"), P("blk", "rep")),
        check_vma=False,
    )
```

```python
import jax
import jax.numpy as jnp
from jax import lax
from jax.sharding import PartitionSpec as P


def shards(hidden_pre, adj_vals, adj_cols, w_out, cotangent):
    feature_width = hidden_pre.shape[1]
    slots, tile_size = adj_vals.shape[1:3]
    blk_count = lax.axis_size("blk")
    rep_count = lax.axis_size("rep")
    section_span = blk_count // rep_count
    bits = (blk_count.bit_length() - 1) // 2
    side = 1 << bits
    per_core = section_span // side
    blk_pos = lax.axis_index("blk")
    rep_pos = lax.axis_index("rep")
    outer_pos, inner_pos = blk_pos >> bits, blk_pos & (side - 1)
    span_bits = section_span.bit_length() - 1
    cols_here = feature_width // rep_count
    rows_here = feature_width // blk_count
    bf16 = jnp.bfloat16
    turns = range(side)
    rising = [1 << b for b in range(bits)]

    def along_inner(value, turn):
        pairs = [(o * side + i, o * side + (i ^ turn)) for o in turns for i in turns]
        return lax.ppermute(value, "blk", pairs) if turn else value

    def along_outer(value, turn):
        pairs = [(o * side + i, (o ^ turn) * side + i) for o in turns for i in turns]
        return lax.ppermute(value, "blk", pairs) if turn else value

    def halved(parts, move, late):
        parts = dict(enumerate(parts))
        size = parts[0].shape[0]
        for bit in rising:
            keys = [k for k in parts if not k & bit]
            sent = jnp.concatenate([parts[k ^ bit].astype(bf16) for k in keys], 0)
            if bit == rising[-1]:
                for other in late:
                    sent = after(sent, other)
            got = move(sent, bit)
            parts = {
                k: parts[k].astype(jnp.float32)
                + got[n * size : (n + 1) * size].astype(jnp.float32)
                for n, k in enumerate(keys)
            }
        return parts[0]

    def to_other(value):
        return lax.ppermute(value, "rep", [(0, 1), (1, 0)])

    def dot(lhs, rhs, dims):
        return lax.dot_general(lhs, rhs, (dims, ((), ())), preferred_element_type=jnp.float32)

    def lanes(value, index):
        return value[:, index * tile_size : (index + 1) * tile_size]

    def after(value, other):
        height, width = (min(a, b) for a, b in zip(value.shape, other.shape))
        part = other[:height, :width].astype(value.dtype) * 0
        part = jnp.concatenate([part] * (value.shape[1] // width), 1)
        return value + jnp.concatenate([part] * (value.shape[0] // height), 0)

    def columns_of(value, index):
        return lax.dynamic_slice_in_dim(value, index * cols_here, cols_here, 1)

    hidden_part = jnp.maximum(columns_of(hidden_pre, rep_pos), 0)

    columns = adj_cols[0]
    turn_of = (columns & (side - 1)) ^ inner_pos
    level_of = (columns >> bits) ^ outer_pos
    place = turn_of * per_core + (level_of & (per_core - 1))
    hit = place[None, :] == jnp.arange(section_span, dtype=jnp.int32)[:, None]
    ordered = jnp.zeros((section_span, tile_size, tile_size), bf16)
    for k in range(slots):
        ordered = jnp.where(hit[:, k, None, None], adj_vals[0, k][None], ordered)
    arrived = [
        along_inner(ordered[t * per_core : (t + 1) * per_core], t) for t in turns
    ]
    everyone = lax.all_gather(jnp.concatenate(arrived, 0), "rep", axis=0)
    rows = []
    for t in turns:
        row_block = outer_pos * side + (inner_pos ^ t)
        row = []
        for e in turns:
            column_block = (outer_pos ^ e) * side + inner_pos
            holder = ((row_block - column_block) & (blk_count - 1)) >> span_bits
            index = t * per_core + e % per_core
            piece = everyone[0, index]
            for r in range(1, rep_count):
                piece = jnp.where(holder == r, everyone[r, index], piece)
            row.append(piece)
        rows.append(jnp.concatenate(row, 1))
    block = jnp.concatenate(rows, 0)

    hidden_stack = jnp.concatenate([along_outer(hidden_part, e) for e in turns], 0)
    grad_part = columns_of(cotangent, rep_pos)
    grad_stack = jnp.concatenate([along_inner(grad_part, t) for t in turns], 0)

    mixed = dot(hidden_stack, block, ((0,), (1,))).astype(bf16)
    share = cols_here // side
    by_owner = mixed.reshape(share // rows_here, side, rows_here, side * tile_size)
    mixed_cols = 0.0
    for t in turns:
        chosen = lax.dynamic_index_in_dim(by_owner, inner_pos ^ t, 1, keepdims=False)
        chosen = chosen.reshape(share, side * tile_size)
        chosen = jnp.concatenate([lanes(chosen, u ^ t) for u in turns], 1)
        mixed_cols = mixed_cols + along_inner(chosen, t).astype(jnp.float32)

    back = after(dot(grad_stack, block, ((0,), (0,))), mixed).astype(bf16)
    back = sum(along_outer(lanes(back, e), e).astype(jnp.float32) for e in turns)

    mixed_cols = lax.all_gather(mixed_cols.astype(bf16), "rep", axis=0, tiled=True)
    w_share = w_out.reshape(side, side, rows_here, feature_width)
    w_share = lax.dynamic_index_in_dim(w_share, inner_pos, 1, keepdims=False)
    w_share = columns_of(w_share.reshape(side * rows_here, feature_width), rep_pos)
    out_part = dot(mixed_cols, w_share, ((0,), (0,)))
    out_part = out_part.astype(bf16)
    out_got = [
        along_inner(out_part[t * tile_size : (t + 1) * tile_size], t) for t in turns
    ]
    weight_part = after(dot(mixed_cols, grad_stack, ((1,), (0,))), out_part)
    by_outer = weight_part.reshape(side, rows_here, cols_here)
    grad_weight = halved(
        [lax.dynamic_index_in_dim(by_outer, outer_pos ^ t, 0, keepdims=False) for t in turns],
        along_outer,
        out_got[1::2],
    )
    out_part = sum(part.astype(jnp.float32) for part in out_got).astype(bf16)

    back = after(back, weight_part).astype(bf16)
    w_rows = w_out.reshape(rep_count, cols_here, feature_width)
    if rep_count == 2:
        w_mine = columns_of(lax.dynamic_index_in_dim(w_rows, rep_pos, 0, keepdims=False), rep_pos)
        w_other = columns_of(
            lax.dynamic_index_in_dim(w_rows, 1 - rep_pos, 0, keepdims=False), rep_pos
        )
        grad_in = to_other(dot(back, w_other, ((0,), (1,))).astype(bf16)).astype(jnp.float32)
        grad_in = grad_in + dot(back, w_mine, ((0,), (1,)))
    else:
        back_full = lax.all_gather(back, "rep", axis=0, tiled=True)
        w_mine = lax.dynamic_index_in_dim(w_rows, rep_pos, 0, keepdims=False)
        grad_in = dot(back_full, w_mine, ((0,), (1,)))
    pre_part = columns_of(hidden_pre, rep_pos)
    grad_pre = jnp.where(pre_part > 0, grad_in, 0.0).astype(bf16)
    return (out_part, grad_weight, grad_pre)


def solution(mesh):
    placed = (P("blk", None), P("blk", "rep", None, None), P("blk", "rep"), P(), P("blk", None))
    return jax.shard_map(
        shards,
        mesh=mesh,
        in_specs=placed,
        out_specs=(P("blk", "rep"), P("blk", "rep"), P("blk", "rep")),
        check_vma=False,
    )
```

```python
import jax
import jax.numpy as jnp
from jax import lax
from jax.sharding import PartitionSpec as P


def shards(hidden_pre, adj_vals, adj_cols, w_out, cotangent):
    feature_width = hidden_pre.shape[1]
    slots, tile_size = adj_vals.shape[1:3]
    blk_count = lax.axis_size("blk")
    rep_count = lax.axis_size("rep")
    section_span = blk_count // rep_count
    bits = (blk_count.bit_length() - 1) // 2
    side = 1 << bits
    per_core = section_span // side
    blk_pos = lax.axis_index("blk")
    rep_pos = lax.axis_index("rep")
    outer_pos, inner_pos = blk_pos >> bits, blk_pos & (side - 1)
    span_bits = section_span.bit_length() - 1
    cols_here = feature_width // rep_count
    rows_here = feature_width // blk_count
    bf16 = jnp.bfloat16
    turns = range(side)
    rising = [1 << b for b in range(bits)]

    def along_inner(value, turn):
        pairs = [(o * side + i, o * side + (i ^ turn)) for o in turns for i in turns]
        return lax.ppermute(value, "blk", pairs) if turn else value

    def along_outer(value, turn):
        pairs = [(o * side + i, (o ^ turn) * side + i) for o in turns for i in turns]
        return lax.ppermute(value, "blk", pairs) if turn else value

    def halved(parts, move, late):
        parts = dict(enumerate(parts))
        size = parts[0].shape[0]
        for bit in rising:
            keys = [k for k in parts if not k & bit]
            sent = jnp.concatenate([parts[k ^ bit].astype(bf16) for k in keys], 0)
            if bit == rising[-1]:
                for other in late:
                    sent = after(sent, other)
            got = move(sent, bit)
            parts = {
                k: parts[k].astype(jnp.float32)
                + got[n * size : (n + 1) * size].astype(jnp.float32)
                for n, k in enumerate(keys)
            }
        return parts[0]

    def to_other(value):
        return lax.ppermute(value, "rep", [(0, 1), (1, 0)])

    def dot(lhs, rhs, dims):
        return lax.dot_general(lhs, rhs, (dims, ((), ())), preferred_element_type=jnp.float32)

    def lanes(value, index):
        return value[:, index * tile_size : (index + 1) * tile_size]

    def after(value, other):
        height, width = (min(a, b) for a, b in zip(value.shape, other.shape))
        part = other[:height, :width].astype(value.dtype) * 0
        part = jnp.concatenate([part] * (value.shape[1] // width), 1)
        return value + jnp.concatenate([part] * (value.shape[0] // height), 0)

    def columns_of(value, index):
        return lax.dynamic_slice_in_dim(value, index * cols_here, cols_here, 1)

    hidden_part = jnp.maximum(columns_of(hidden_pre, rep_pos), 0)

    columns = adj_cols[0]
    turn_of = (columns & (side - 1)) ^ inner_pos
    level_of = (columns >> bits) ^ outer_pos
    place = turn_of * per_core + (level_of & (per_core - 1))
    hit = place[None, :] == jnp.arange(section_span, dtype=jnp.int32)[:, None]
    ordered = jnp.zeros((section_span, tile_size, tile_size), bf16)
    for k in range(slots):
        ordered = jnp.where(hit[:, k, None, None], adj_vals[0, k][None], ordered)
    arrived = [
        along_inner(ordered[t * per_core : (t + 1) * per_core], t) for t in turns
    ]
    everyone = lax.all_gather(jnp.concatenate(arrived, 0), "rep", axis=0)
    rows = []
    for t in turns:
        row_block = outer_pos * side + (inner_pos ^ t)
        row = []
        for e in turns:
            column_block = (outer_pos ^ e) * side + inner_pos
            holder = ((row_block - column_block) & (blk_count - 1)) >> span_bits
            index = t * per_core + e % per_core
            piece = everyone[0, index]
            for r in range(1, rep_count):
                piece = jnp.where(holder == r, everyone[r, index], piece)
            row.append(piece)
        rows.append(jnp.concatenate(row, 1))
    block = jnp.concatenate(rows, 0)

    hidden_stack = jnp.concatenate([along_outer(hidden_part, e) for e in turns], 0)
    grad_part = columns_of(cotangent, rep_pos)
    grad_stack = jnp.concatenate([along_inner(grad_part, t) for t in turns], 0)

    mixed = dot(hidden_stack, block, ((0,), (1,))).astype(bf16)
    share = cols_here // side
    by_owner = mixed.reshape(share // rows_here, side, rows_here, side * tile_size)
    mixed_cols = 0.0
    for t in turns:
        chosen = lax.dynamic_index_in_dim(by_owner, inner_pos ^ t, 1, keepdims=False)
        chosen = chosen.reshape(share, side * tile_size)
        chosen = jnp.concatenate([lanes(chosen, u ^ t) for u in turns], 1)
        mixed_cols = mixed_cols + along_inner(chosen, t).astype(jnp.float32)

    back = after(dot(grad_stack, block, ((0,), (0,))), mixed).astype(bf16)
    back = sum(along_outer(lanes(back, e), e).astype(jnp.float32) for e in turns)

    mixed_cols = lax.all_gather(mixed_cols.astype(bf16), "rep", axis=0, tiled=True)
    w_share = w_out.reshape(side, side, rows_here, feature_width)
    w_share = lax.dynamic_index_in_dim(w_share, inner_pos, 1, keepdims=False)
    w_share = columns_of(w_share.reshape(side * rows_here, feature_width), rep_pos)
    out_part = dot(mixed_cols, w_share, ((0,), (0,)))
    out_part = out_part.astype(bf16)
    out_got = [
        along_inner(out_part[t * tile_size : (t + 1) * tile_size], t) for t in turns
    ]
    weight_part = after(dot(mixed_cols, grad_stack, ((1,), (0,))), out_part)
    by_outer = weight_part.reshape(side, rows_here, cols_here)
    grad_weight = halved(
        [lax.dynamic_index_in_dim(by_outer, outer_pos ^ t, 0, keepdims=False) for t in turns],
        along_outer,
        out_got[1::2],
    )
    out_part = sum(part.astype(jnp.float32) for part in out_got).astype(bf16)

    back = after(back, weight_part).astype(bf16)
    w_rows = w_out.reshape(rep_count, cols_here, feature_width)
    if rep_count == 2:
        w_mine = columns_of(lax.dynamic_index_in_dim(w_rows, rep_pos, 0, keepdims=False), rep_pos)
        w_other = columns_of(
            lax.dynamic_index_in_dim(w_rows, 1 - rep_pos, 0, keepdims=False), rep_pos
        )
        grad_in = to_other(dot(back, w_other, ((0,), (1,))).astype(bf16)).astype(jnp.float32)
        grad_in = grad_in + lax.optimization_barrier(dot(back, w_mine, ((0,), (1,))))
    else:
        back_full = lax.all_gather(back, "rep", axis=0, tiled=True)
        w_mine = lax.dynamic_index_in_dim(w_rows, rep_pos, 0, keepdims=False)
        grad_in = dot(back_full, w_mine, ((0,), (1,)))
    grad_pre = jnp.where(hidden_part > 0, grad_in, 0.0).astype(bf16)
    return (out_part, grad_weight, grad_pre)


def solution(mesh):
    placed = (P("blk", None), P("blk", "rep", None, None), P("blk", "rep"), P(), P("blk", None))
    return jax.shard_map(
        shards,
        mesh=mesh,
        in_specs=placed,
        out_specs=(P("blk", "rep"), P("blk", "rep"), P("blk", "rep")),
        check_vma=False,
    )
```

```python
import jax
import jax.numpy as jnp
from jax import lax
from jax.sharding import PartitionSpec as P


def shards(hidden_pre, adj_vals, adj_cols, w_out, cotangent):
    feature_width = hidden_pre.shape[1]
    slots, tile_size = adj_vals.shape[1:3]
    blk_count = lax.axis_size("blk")
    rep_count = lax.axis_size("rep")
    section_span = blk_count // rep_count
    bits = (blk_count.bit_length() - 1) // 2
    side = 1 << bits
    per_core = section_span // side
    blk_pos = lax.axis_index("blk")
    rep_pos = lax.axis_index("rep")
    outer_pos, inner_pos = blk_pos >> bits, blk_pos & (side - 1)
    span_bits = section_span.bit_length() - 1
    cols_here = feature_width // rep_count
    rows_here = feature_width // blk_count
    bf16 = jnp.bfloat16
    turns = range(side)
    rising = [1 << b for b in range(bits)]

    def along_inner(value, turn):
        pairs = [(o * side + i, o * side + (i ^ turn)) for o in turns for i in turns]
        return lax.ppermute(value, "blk", pairs) if turn else value

    def along_outer(value, turn):
        pairs = [(o * side + i, (o ^ turn) * side + i) for o in turns for i in turns]
        return lax.ppermute(value, "blk", pairs) if turn else value

    def from_two(value, turn):
        pairs = [
            ((o * side + i) * 2 + r, ((o ^ (turn + r)) * side + i) * 2 + r)
            for o in turns
            for i in turns
            for r in range(2)
        ]
        return lax.ppermute(value, ("blk", "rep"), pairs)

    def halved(parts, move, late):
        parts = dict(enumerate(parts))
        size = parts[0].shape[0]
        for bit in rising:
            keys = [k for k in parts if not k & bit]
            sent = jnp.concatenate([parts[k ^ bit].astype(bf16) for k in keys], 0)
            if bit == rising[-1]:
                for other in late:
                    sent = after(sent, other)
            got = move(sent, bit)
            parts = {
                k: parts[k].astype(jnp.float32)
                + got[n * size : (n + 1) * size].astype(jnp.float32)
                for n, k in enumerate(keys)
            }
        return parts[0]

    def to_other(value):
        return lax.ppermute(value, "rep", [(0, 1), (1, 0)])

    def dot(lhs, rhs, dims):
        return lax.dot_general(lhs, rhs, (dims, ((), ())), preferred_element_type=jnp.float32)

    def lanes(value, index):
        return value[:, index * tile_size : (index + 1) * tile_size]

    def after(value, other):
        height, width = (min(a, b) for a, b in zip(value.shape, other.shape))
        part = other[:height, :width].astype(value.dtype) * 0
        part = jnp.concatenate([part] * (value.shape[1] // width), 1)
        return value + jnp.concatenate([part] * (value.shape[0] // height), 0)

    def columns_of(value, index):
        return lax.dynamic_slice_in_dim(value, index * cols_here, cols_here, 1)

    pair_up = rep_count == 2 and side == 4
    far = from_two(hidden_pre, 2) if pair_up else None
    hidden_part = jnp.maximum(columns_of(hidden_pre, rep_pos), 0)

    columns = adj_cols[0]
    turn_of = (columns & (side - 1)) ^ inner_pos
    level_of = (columns >> bits) ^ outer_pos
    place = turn_of * per_core + (level_of & (per_core - 1))
    hit = place[None, :] == jnp.arange(section_span, dtype=jnp.int32)[:, None]
    ordered = jnp.zeros((section_span, tile_size, tile_size), bf16)
    for k in range(slots):
        ordered = jnp.where(hit[:, k, None, None], adj_vals[0, k][None], ordered)
    arrived = [
        along_inner(ordered[t * per_core : (t + 1) * per_core], t) for t in turns
    ]
    if pair_up:
        other = columns_of(far, 1 - rep_pos)
        blocks = cols_here // tile_size
        arrived.append(jnp.stack([lanes(other, n) for n in range(blocks)]))
    everyone = lax.all_gather(jnp.concatenate(arrived, 0), "rep", axis=0)
    rows = []
    for t in turns:
        row_block = outer_pos * side + (inner_pos ^ t)
        row = []
        for e in turns:
            column_block = (outer_pos ^ e) * side + inner_pos
            holder = ((row_block - column_block) & (blk_count - 1)) >> span_bits
            index = t * per_core + e % per_core
            piece = everyone[0, index]
            for r in range(1, rep_count):
                piece = jnp.where(holder == r, everyone[r, index], piece)
            row.append(piece)
        rows.append(jnp.concatenate(row, 1))
    block = jnp.concatenate(rows, 0)

    direct = turns[:2] if pair_up else turns
    hidden_stack = [along_outer(hidden_part, e) for e in direct]
    if pair_up:
        mine = columns_of(far, rep_pos)
        other = jnp.where(rep_pos == 0, everyone[1, section_span:], everyone[0, section_span:])
        other = jnp.concatenate([other[n] for n in range(blocks)], 1)
        second, third = jnp.where(rep_pos == 0, mine, other), jnp.where(rep_pos == 0, other, mine)
        hidden_stack.extend([jnp.maximum(second, 0), jnp.maximum(third, 0)])
    hidden_stack = jnp.concatenate(hidden_stack, 0)
    grad_part = columns_of(cotangent, rep_pos)
    grad_stack = jnp.concatenate([along_inner(grad_part, t) for t in turns], 0)

    mixed = dot(hidden_stack, block, ((0,), (1,))).astype(bf16)
    share = cols_here // side
    by_owner = mixed.reshape(share // rows_here, side, rows_here, side * tile_size)
    mixed_cols = 0.0
    for t in turns:
        chosen = lax.dynamic_index_in_dim(by_owner, inner_pos ^ t, 1, keepdims=False)
        chosen = chosen.reshape(share, side * tile_size)
        chosen = jnp.concatenate([lanes(chosen, u ^ t) for u in turns], 1)
        mixed_cols = mixed_cols + along_inner(chosen, t).astype(jnp.float32)

    back = after(dot(grad_stack, block, ((0,), (0,))), mixed).astype(bf16)
    back = sum(along_outer(lanes(back, e), e).astype(jnp.float32) for e in turns)

    mixed_cols = lax.all_gather(mixed_cols.astype(bf16), "rep", axis=0, tiled=True)
    w_share = w_out.reshape(side, side, rows_here, feature_width)
    w_share = lax.dynamic_index_in_dim(w_share, inner_pos, 1, keepdims=False)
    w_share = columns_of(w_share.reshape(side * rows_here, feature_width), rep_pos)
    out_part = dot(mixed_cols, w_share, ((0,), (0,)))
    out_part = out_part.astype(bf16)
    out_got = [
        along_inner(out_part[t * tile_size : (t + 1) * tile_size], t) for t in turns
    ]
    weight_part = after(dot(mixed_cols, grad_stack, ((1,), (0,))), out_part)
    by_outer = weight_part.reshape(side, rows_here, cols_here)
    grad_weight = halved(
        [lax.dynamic_index_in_dim(by_outer, outer_pos ^ t, 0, keepdims=False) for t in turns],
        along_outer,
        out_got[1::2],
    )
    out_part = sum(part.astype(jnp.float32) for part in out_got).astype(bf16)

    back = after(back, weight_part).astype(bf16)
    w_rows = w_out.reshape(rep_count, cols_here, feature_width)
    if rep_count == 2:
        w_mine = columns_of(lax.dynamic_index_in_dim(w_rows, rep_pos, 0, keepdims=False), rep_pos)
        w_other = columns_of(
            lax.dynamic_index_in_dim(w_rows, 1 - rep_pos, 0, keepdims=False), rep_pos
        )
        grad_in = to_other(dot(back, w_other, ((0,), (1,))).astype(bf16)).astype(jnp.float32)
        grad_in = grad_in + dot(back, w_mine, ((0,), (1,)))
    else:
        back_full = lax.all_gather(back, "rep", axis=0, tiled=True)
        w_mine = lax.dynamic_index_in_dim(w_rows, rep_pos, 0, keepdims=False)
        grad_in = dot(back_full, w_mine, ((0,), (1,)))
    pre_part = columns_of(hidden_pre, rep_pos)
    grad_pre = jnp.where(pre_part > 0, grad_in, 0.0).astype(bf16)
    return (out_part, grad_weight, grad_pre)


def solution(mesh):
    placed = (P("blk", None), P("blk", "rep", None, None), P("blk", "rep"), P(), P("blk", None))
    return jax.shard_map(
        shards,
        mesh=mesh,
        in_specs=placed,
        out_specs=(P("blk", "rep"), P("blk", "rep"), P("blk", "rep")),
        check_vma=False,
    )
```

```python
import jax
import jax.numpy as jnp
from jax import lax
from jax.sharding import PartitionSpec as P


def shards(hidden_pre, adj_vals, adj_cols, w_out, cotangent):
    feature_width = hidden_pre.shape[1]
    slots, tile_size = adj_vals.shape[1:3]
    blk_count = lax.axis_size("blk")
    rep_count = lax.axis_size("rep")
    section_span = blk_count // rep_count
    bits = (blk_count.bit_length() - 1) // 2
    side = 1 << bits
    per_core = section_span // side
    blk_pos = lax.axis_index("blk")
    rep_pos = lax.axis_index("rep")
    outer_pos, inner_pos = blk_pos >> bits, blk_pos & (side - 1)
    span_bits = section_span.bit_length() - 1
    cols_here = feature_width // rep_count
    rows_here = feature_width // blk_count
    bf16 = jnp.bfloat16
    turns = range(side)
    rising = [1 << b for b in range(bits)]

    def along_inner(value, turn):
        pairs = [(o * side + i, o * side + (i ^ turn)) for o in turns for i in turns]
        return lax.ppermute(value, "blk", pairs) if turn else value

    def along_outer(value, turn):
        pairs = [(o * side + i, (o ^ turn) * side + i) for o in turns for i in turns]
        return lax.ppermute(value, "blk", pairs) if turn else value

    def halved(parts, move, late):
        parts = dict(enumerate(parts))
        size = parts[0].shape[0]
        for bit in rising:
            keys = [k for k in parts if not k & bit]
            sent = jnp.concatenate([parts[k ^ bit].astype(bf16) for k in keys], 0)
            if bit == rising[-1]:
                for other in late:
                    sent = after(sent, other)
            got = move(sent, bit)
            parts = {
                k: parts[k].astype(jnp.float32)
                + got[n * size : (n + 1) * size].astype(jnp.float32)
                for n, k in enumerate(keys)
            }
        return parts[0]

    def to_other(value):
        return lax.ppermute(value, "rep", [(0, 1), (1, 0)])

    def dot(lhs, rhs, dims):
        return lax.dot_general(lhs, rhs, (dims, ((), ())), preferred_element_type=jnp.float32)

    def lanes(value, index):
        return value[:, index * tile_size : (index + 1) * tile_size]

    def after(value, other):
        height, width = (min(a, b) for a, b in zip(value.shape, other.shape))
        part = other[:height, :width].astype(value.dtype) * 0
        part = jnp.concatenate([part] * (value.shape[1] // width), 1)
        return value + jnp.concatenate([part] * (value.shape[0] // height), 0)

    def columns_of(value, index):
        return lax.dynamic_slice_in_dim(value, index * cols_here, cols_here, 1)

    hidden_part = jnp.maximum(columns_of(hidden_pre, rep_pos), 0)

    columns = adj_cols[0]
    turn_of = (columns & (side - 1)) ^ inner_pos
    level_of = (columns >> bits) ^ outer_pos
    place = turn_of * per_core + (level_of & (per_core - 1))
    hit = place[None, :] == jnp.arange(section_span, dtype=jnp.int32)[:, None]
    ordered = jnp.zeros((section_span, tile_size, tile_size), bf16)
    for k in range(slots):
        ordered = jnp.where(hit[:, k, None, None], adj_vals[0, k][None], ordered)
    arrived = [
        along_inner(ordered[t * per_core : (t + 1) * per_core], t) for t in turns
    ]
    everyone = lax.all_gather(jnp.concatenate(arrived, 0), "rep", axis=0)
    rows = []
    for t in turns:
        row_block = outer_pos * side + (inner_pos ^ t)
        row = []
        for e in turns:
            column_block = (outer_pos ^ e) * side + inner_pos
            holder = ((row_block - column_block) & (blk_count - 1)) >> span_bits
            index = t * per_core + e % per_core
            piece = everyone[0, index]
            for r in range(1, rep_count):
                piece = jnp.where(holder == r, everyone[r, index], piece)
            row.append(piece)
        rows.append(jnp.concatenate(row, 1))
    block = jnp.concatenate(rows, 0)

    hidden_stack = jnp.concatenate([along_outer(hidden_part, e) for e in turns], 0)
    grad_part = columns_of(cotangent, rep_pos)
    grad_stack = jnp.concatenate([along_inner(grad_part, t) for t in turns], 0)

    mixed = dot(hidden_stack, block, ((0,), (1,))).astype(bf16)
    share = cols_here // side
    by_owner = mixed.reshape(share // rows_here, side, rows_here, side * tile_size)
    mixed_cols = 0.0
    for t in turns:
        chosen = lax.dynamic_index_in_dim(by_owner, inner_pos ^ t, 1, keepdims=False)
        chosen = chosen.reshape(share, side * tile_size)
        chosen = jnp.concatenate([lanes(chosen, u ^ t) for u in turns], 1)
        mixed_cols = mixed_cols + along_inner(chosen, t).astype(jnp.float32)

    back = after(dot(grad_stack, block, ((0,), (0,))), mixed).astype(bf16)
    back = halved([lanes(back, e) for e in turns], along_outer, [])

    mixed_cols = lax.all_gather(mixed_cols.astype(bf16), "rep", axis=0, tiled=True)
    w_share = w_out.reshape(side, side, rows_here, feature_width)
    w_share = lax.dynamic_index_in_dim(w_share, inner_pos, 1, keepdims=False)
    w_share = columns_of(w_share.reshape(side * rows_here, feature_width), rep_pos)
    out_part = dot(mixed_cols, w_share, ((0,), (0,)))
    out_part = out_part.astype(bf16)
    out_got = [
        along_inner(out_part[t * tile_size : (t + 1) * tile_size], t) for t in turns
    ]
    weight_part = after(dot(mixed_cols, grad_stack, ((1,), (0,))), out_part)
    by_outer = weight_part.reshape(side, rows_here, cols_here)
    grad_weight = halved(
        [lax.dynamic_index_in_dim(by_outer, outer_pos ^ t, 0, keepdims=False) for t in turns],
        along_outer,
        out_got[1::2],
    )
    out_part = sum(part.astype(jnp.float32) for part in out_got).astype(bf16)

    back = after(back, weight_part).astype(bf16)
    w_rows = w_out.reshape(rep_count, cols_here, feature_width)
    if rep_count == 2:
        w_mine = columns_of(lax.dynamic_index_in_dim(w_rows, rep_pos, 0, keepdims=False), rep_pos)
        w_other = columns_of(
            lax.dynamic_index_in_dim(w_rows, 1 - rep_pos, 0, keepdims=False), rep_pos
        )
        grad_in = to_other(dot(back, w_other, ((0,), (1,))).astype(bf16)).astype(jnp.float32)
        grad_in = grad_in + dot(back, w_mine, ((0,), (1,)))
    else:
        back_full = lax.all_gather(back, "rep", axis=0, tiled=True)
        w_mine = lax.dynamic_index_in_dim(w_rows, rep_pos, 0, keepdims=False)
        grad_in = dot(back_full, w_mine, ((0,), (1,)))
    pre_part = columns_of(hidden_pre, rep_pos)
    grad_pre = jnp.where(pre_part > 0, grad_in, 0.0).astype(bf16)
    return (out_part, grad_weight, grad_pre)


def solution(mesh):
    placed = (P("blk", None), P("blk", "rep", None, None), P("blk", "rep"), P(), P("blk", None))
    return jax.shard_map(
        shards,
        mesh=mesh,
        in_specs=placed,
        out_specs=(P("blk", "rep"), P("blk", "rep"), P("blk", "rep")),
        check_vma=False,
    )
```

```python
import jax
import jax.numpy as jnp
from jax import lax
from jax.sharding import PartitionSpec as P


def shards(hidden_pre, adj_vals, adj_cols, w_out, cotangent):
    feature_width = hidden_pre.shape[1]
    slots, tile_size = adj_vals.shape[1:3]
    blk_count = lax.axis_size("blk")
    rep_count = lax.axis_size("rep")
    section_span = blk_count // rep_count
    bits = (blk_count.bit_length() - 1) // 2
    side = 1 << bits
    per_core = section_span // side
    blk_pos = lax.axis_index("blk")
    rep_pos = lax.axis_index("rep")
    outer_pos, inner_pos = blk_pos >> bits, blk_pos & (side - 1)
    span_bits = section_span.bit_length() - 1
    cols_here = feature_width // rep_count
    rows_here = feature_width // blk_count
    bf16 = jnp.bfloat16
    turns = range(side)
    rising = [1 << b for b in range(bits)]

    def along_inner(value, turn):
        pairs = [(o * side + i, o * side + (i ^ turn)) for o in turns for i in turns]
        return lax.ppermute(value, "blk", pairs) if turn else value

    def along_outer(value, turn):
        pairs = [(o * side + i, (o ^ turn) * side + i) for o in turns for i in turns]
        return lax.ppermute(value, "blk", pairs) if turn else value

    def halved(parts, move, late):
        parts = dict(enumerate(parts))
        size = parts[0].shape[0]
        for bit in rising:
            keys = [k for k in parts if not k & bit]
            sent = jnp.concatenate([parts[k ^ bit].astype(bf16) for k in keys], 0)
            if bit == rising[-1]:
                for other in late:
                    sent = after(sent, other)
            got = move(sent, bit)
            parts = {
                k: parts[k].astype(jnp.float32)
                + got[n * size : (n + 1) * size].astype(jnp.float32)
                for n, k in enumerate(keys)
            }
        return parts[0]

    def to_other(value):
        return lax.ppermute(value, "rep", [(0, 1), (1, 0)])

    def dot(lhs, rhs, dims):
        return lax.dot_general(lhs, rhs, (dims, ((), ())), preferred_element_type=jnp.float32)

    def lanes(value, index):
        return value[:, index * tile_size : (index + 1) * tile_size]

    def after(value, other):
        height, width = (min(a, b) for a, b in zip(value.shape, other.shape))
        part = other[:height, :width].astype(value.dtype) * 0
        part = jnp.concatenate([part] * (value.shape[1] // width), 1)
        return value + jnp.concatenate([part] * (value.shape[0] // height), 0)

    def columns_of(value, index):
        return lax.dynamic_slice_in_dim(value, index * cols_here, cols_here, 1)

    hidden_part = jnp.maximum(columns_of(hidden_pre, rep_pos), 0)

    columns = adj_cols[0]
    turn_of = (columns & (side - 1)) ^ inner_pos
    level_of = (columns >> bits) ^ outer_pos
    place = turn_of * per_core + (level_of & (per_core - 1))
    hit = place[None, :] == jnp.arange(section_span, dtype=jnp.int32)[:, None]
    ordered = jnp.zeros((section_span, tile_size, tile_size), bf16)
    for k in range(slots):
        ordered = jnp.where(hit[:, k, None, None], adj_vals[0, k][None], ordered)
    arrived = [
        along_inner(ordered[t * per_core : (t + 1) * per_core], t) for t in turns
    ]
    everyone = lax.all_gather(jnp.concatenate(arrived, 0), "rep", axis=0)
    rows = []
    for t in turns:
        row_block = outer_pos * side + (inner_pos ^ t)
        row = []
        for e in turns:
            column_block = (outer_pos ^ e) * side + inner_pos
            holder = ((row_block - column_block) & (blk_count - 1)) >> span_bits
            index = t * per_core + e % per_core
            piece = everyone[0, index]
            for r in range(1, rep_count):
                piece = jnp.where(holder == r, everyone[r, index], piece)
            row.append(piece)
        rows.append(jnp.concatenate(row, 1))
    block = jnp.concatenate(rows, 0)

    hidden_stack = jnp.concatenate([along_outer(hidden_part, e) for e in turns], 0)
    grad_part = columns_of(cotangent, rep_pos)
    grad_stack = jnp.concatenate([along_inner(grad_part, t) for t in turns], 0)

    mixed = dot(hidden_stack, block, ((0,), (1,))).astype(bf16)
    share = cols_here // side
    by_owner = mixed.reshape(share // rows_here, side, rows_here, side * tile_size)
    mixed_cols = 0.0
    for t in turns:
        chosen = lax.dynamic_index_in_dim(by_owner, inner_pos ^ t, 1, keepdims=False)
        chosen = chosen.reshape(share, side * tile_size)
        chosen = jnp.concatenate([lanes(chosen, u ^ t) for u in turns], 1)
        mixed_cols = mixed_cols + along_inner(chosen, t).astype(jnp.float32)

    back = after(dot(grad_stack, block, ((0,), (0,))), mixed).astype(bf16)
    back = sum(along_outer(lanes(back, e), e).astype(jnp.float32) for e in turns)

    mixed_cols = lax.all_gather(mixed_cols.astype(bf16), "rep", axis=0, tiled=True)
    w_share = w_out.reshape(side, side, rows_here, feature_width)
    w_share = lax.dynamic_index_in_dim(w_share, inner_pos, 1, keepdims=False)
    w_share = columns_of(w_share.reshape(side * rows_here, feature_width), rep_pos)
    out_part = dot(mixed_cols, w_share, ((0,), (0,)))
    out_part = out_part.astype(bf16)
    out_got = [
        along_inner(out_part[t * tile_size : (t + 1) * tile_size], t) for t in turns
    ]
    weight_part = after(dot(mixed_cols, grad_stack, ((1,), (0,))), out_part)
    by_outer = weight_part.reshape(side, rows_here, cols_here)
    grad_weight = halved(
        [lax.dynamic_index_in_dim(by_outer, outer_pos ^ t, 0, keepdims=False) for t in turns],
        along_outer,
        out_got[1::2],
    )

    back = after(back, weight_part).astype(bf16)
    w_rows = w_out.reshape(rep_count, cols_here, feature_width)
    if rep_count == 2:
        w_mine = columns_of(lax.dynamic_index_in_dim(w_rows, rep_pos, 0, keepdims=False), rep_pos)
        w_other = columns_of(
            lax.dynamic_index_in_dim(w_rows, 1 - rep_pos, 0, keepdims=False), rep_pos
        )
        grad_in = to_other(dot(back, w_other, ((0,), (1,))).astype(bf16)).astype(jnp.float32)
        grad_in = grad_in + dot(back, w_mine, ((0,), (1,)))
    else:
        back_full = lax.all_gather(back, "rep", axis=0, tiled=True)
        w_mine = lax.dynamic_index_in_dim(w_rows, rep_pos, 0, keepdims=False)
        grad_in = dot(back_full, w_mine, ((0,), (1,)))
    pre_part = columns_of(hidden_pre, rep_pos)
    grad_pre = jnp.where(pre_part > 0, grad_in, 0.0).astype(bf16)
    out_part = sum(part.astype(jnp.float32) for part in out_got)
    out_part = after(out_part, grad_pre).astype(bf16)
    return (out_part, grad_weight, grad_pre)


def solution(mesh):
    placed = (P("blk", None), P("blk", "rep", None, None), P("blk", "rep"), P(), P("blk", None))
    return jax.shard_map(
        shards,
        mesh=mesh,
        in_specs=placed,
        out_specs=(P("blk", "rep"), P("blk", "rep"), P("blk", "rep")),
        check_vma=False,
    )
```

```python
import jax
import jax.numpy as jnp
from jax import lax
from jax.sharding import PartitionSpec as P


def shards(hidden_pre, adj_vals, adj_cols, w_out, cotangent):
    feature_width = hidden_pre.shape[1]
    slots, tile_size = adj_vals.shape[1:3]
    blk_count = lax.axis_size("blk")
    rep_count = lax.axis_size("rep")
    section_span = blk_count // rep_count
    bits = (blk_count.bit_length() - 1) // 2
    side = 1 << bits
    per_core = section_span // side
    blk_pos = lax.axis_index("blk")
    rep_pos = lax.axis_index("rep")
    outer_pos, inner_pos = blk_pos >> bits, blk_pos & (side - 1)
    span_bits = section_span.bit_length() - 1
    cols_here = feature_width // rep_count
    rows_here = feature_width // blk_count
    bf16 = jnp.bfloat16
    turns = range(side)
    rising = [1 << b for b in range(bits)]

    def along_inner(value, turn):
        pairs = [(o * side + i, o * side + (i ^ turn)) for o in turns for i in turns]
        return lax.ppermute(value, "blk", pairs) if turn else value

    def along_outer(value, turn):
        pairs = [(o * side + i, (o ^ turn) * side + i) for o in turns for i in turns]
        return lax.ppermute(value, "blk", pairs) if turn else value

    def halved(parts, move, late):
        parts = dict(enumerate(parts))
        size = parts[0].shape[0]
        for bit in rising:
            keys = [k for k in parts if not k & bit]
            sent = jnp.concatenate([parts[k ^ bit].astype(bf16) for k in keys], 0)
            if bit == rising[-1]:
                for other in late:
                    sent = after(sent, other)
            got = move(sent, bit)
            parts = {
                k: parts[k].astype(jnp.float32)
                + got[n * size : (n + 1) * size].astype(jnp.float32)
                for n, k in enumerate(keys)
            }
        return parts[0]

    def to_other(value):
        return lax.ppermute(value, "rep", [(0, 1), (1, 0)])

    def dot(lhs, rhs, dims):
        return lax.dot_general(lhs, rhs, (dims, ((), ())), preferred_element_type=jnp.float32)

    def lanes(value, index):
        return value[:, index * tile_size : (index + 1) * tile_size]

    def after(value, other):
        height, width = (min(a, b) for a, b in zip(value.shape, other.shape))
        part = other[:height, :width].astype(value.dtype) * 0
        part = jnp.concatenate([part] * (value.shape[1] // width), 1)
        return value + jnp.concatenate([part] * (value.shape[0] // height), 0)

    def columns_of(value, index):
        return lax.dynamic_slice_in_dim(value, index * cols_here, cols_here, 1)

    hidden_part = jnp.maximum(columns_of(hidden_pre, rep_pos), 0)

    columns = adj_cols[0]
    turn_of = (columns & (side - 1)) ^ inner_pos
    level_of = (columns >> bits) ^ outer_pos
    place = turn_of * per_core + (level_of & (per_core - 1))
    hit = place[None, :] == jnp.arange(section_span, dtype=jnp.int32)[:, None]
    ordered = jnp.zeros((section_span, tile_size, tile_size), bf16)
    for k in range(slots):
        ordered = jnp.where(hit[:, k, None, None], adj_vals[0, k][None], ordered)
    arrived = [
        along_inner(ordered[t * per_core : (t + 1) * per_core], t) for t in turns
    ]
    everyone = lax.all_gather(jnp.concatenate(arrived, 0), "rep", axis=0)
    rows = []
    for t in turns:
        row_block = outer_pos * side + (inner_pos ^ t)
        row = []
        for e in turns:
            column_block = (outer_pos ^ e) * side + inner_pos
            holder = ((row_block - column_block) & (blk_count - 1)) >> span_bits
            index = t * per_core + e % per_core
            piece = everyone[0, index]
            for r in range(1, rep_count):
                piece = jnp.where(holder == r, everyone[r, index], piece)
            row.append(piece)
        rows.append(jnp.concatenate(row, 1))
    block = jnp.concatenate(rows, 0)

    hidden_stack = jnp.concatenate([along_outer(hidden_part, e) for e in turns], 0)
    grad_part = columns_of(cotangent, rep_pos)
    grad_stack = jnp.concatenate([along_inner(grad_part, t) for t in turns], 0)

    mixed = dot(hidden_stack, block, ((0,), (1,))).astype(bf16)
    share = cols_here // side
    by_owner = mixed.reshape(share // rows_here, side, rows_here, side * tile_size)
    mixed_cols = 0.0
    for t in turns:
        chosen = lax.dynamic_index_in_dim(by_owner, inner_pos ^ t, 1, keepdims=False)
        chosen = chosen.reshape(share, side * tile_size)
        chosen = jnp.concatenate([lanes(chosen, u ^ t) for u in turns], 1)
        mixed_cols = mixed_cols + along_inner(chosen, t).astype(jnp.float32)

    back = after(dot(grad_stack, block, ((0,), (0,))), mixed).astype(bf16)
    back = sum(along_outer(lanes(back, e), e).astype(jnp.float32) for e in turns)

    mixed_cols = lax.all_gather(mixed_cols.astype(bf16), "rep", axis=0, tiled=True)
    w_share = w_out.reshape(side, side, rows_here, feature_width)
    w_share = lax.dynamic_index_in_dim(w_share, inner_pos, 1, keepdims=False)
    w_share = columns_of(w_share.reshape(side * rows_here, feature_width), rep_pos)
    out_part = dot(mixed_cols, w_share, ((0,), (0,)))
    out_part = out_part.astype(bf16)
    out_got = [
        along_inner(out_part[t * tile_size : (t + 1) * tile_size], t) for t in turns
    ]
    weight_part = after(dot(mixed_cols, grad_stack, ((1,), (0,))), out_part)
    by_outer = weight_part.reshape(side, rows_here, cols_here)
    grad_weight = halved(
        [lax.dynamic_index_in_dim(by_outer, outer_pos ^ t, 0, keepdims=False) for t in turns],
        along_outer,
        out_got[1::2],
    )

    back = after(back, weight_part).astype(bf16)
    w_rows = w_out.reshape(rep_count, cols_here, feature_width)
    if rep_count == 2:
        w_mine = columns_of(lax.dynamic_index_in_dim(w_rows, rep_pos, 0, keepdims=False), rep_pos)
        w_other = columns_of(
            lax.dynamic_index_in_dim(w_rows, 1 - rep_pos, 0, keepdims=False), rep_pos
        )
        grad_in = to_other(dot(back, w_other, ((0,), (1,))).astype(bf16)).astype(jnp.float32)
        grad_in = grad_in + dot(back, w_mine, ((0,), (1,)))
    else:
        back_full = lax.all_gather(back, "rep", axis=0, tiled=True)
        w_mine = lax.dynamic_index_in_dim(w_rows, rep_pos, 0, keepdims=False)
        grad_in = dot(back_full, w_mine, ((0,), (1,)))
    pre_part = columns_of(hidden_pre, rep_pos)
    grad_pre = jnp.where(pre_part > 0, grad_in, 0.0).astype(bf16)
    out_part = sum(part.astype(jnp.float32) for part in out_got)
    out_part = after(out_part, lax.optimization_barrier(grad_pre)).astype(bf16)
    return (out_part, grad_weight, grad_pre)


def solution(mesh):
    placed = (P("blk", None), P("blk", "rep", None, None), P("blk", "rep"), P(), P("blk", None))
    return jax.shard_map(
        shards,
        mesh=mesh,
        in_specs=placed,
        out_specs=(P("blk", "rep"), P("blk", "rep"), P("blk", "rep")),
        check_vma=False,
    )
```

```python
import jax
import jax.numpy as jnp
from jax import lax
from jax.sharding import PartitionSpec as P


def shards(hidden_pre, adj_vals, adj_cols, w_out, cotangent):
    feature_width = hidden_pre.shape[1]
    slots, tile_size = adj_vals.shape[1:3]
    blk_count = lax.axis_size("blk")
    rep_count = lax.axis_size("rep")
    section_span = blk_count // rep_count
    bits = (blk_count.bit_length() - 1) // 2
    side = 1 << bits
    per_core = section_span // side
    blk_pos = lax.axis_index("blk")
    rep_pos = lax.axis_index("rep")
    outer_pos, inner_pos = blk_pos >> bits, blk_pos & (side - 1)
    span_bits = section_span.bit_length() - 1
    cols_here = feature_width // rep_count
    rows_here = feature_width // blk_count
    bf16 = jnp.bfloat16
    turns = range(side)
    rising = [1 << b for b in range(bits)]

    def along_inner(value, turn):
        pairs = [(o * side + i, o * side + (i ^ turn)) for o in turns for i in turns]
        return lax.ppermute(value, "blk", pairs) if turn else value

    def along_outer(value, turn):
        pairs = [(o * side + i, (o ^ turn) * side + i) for o in turns for i in turns]
        return lax.ppermute(value, "blk", pairs) if turn else value

    def halved(parts, move, late):
        parts = dict(enumerate(parts))
        size = parts[0].shape[0]
        for bit in rising:
            keys = [k for k in parts if not k & bit]
            sent = jnp.concatenate([parts[k ^ bit].astype(bf16) for k in keys], 0)
            if bit == rising[-1]:
                for other in late:
                    sent = after(sent, other)
            got = move(sent, bit)
            parts = {
                k: parts[k].astype(jnp.float32)
                + got[n * size : (n + 1) * size].astype(jnp.float32)
                for n, k in enumerate(keys)
            }
        return parts[0]

    def to_other(value):
        return lax.ppermute(value, "rep", [(0, 1), (1, 0)])

    def dot(lhs, rhs, dims):
        return lax.dot_general(lhs, rhs, (dims, ((), ())), preferred_element_type=jnp.float32)

    def lanes(value, index):
        return value[:, index * tile_size : (index + 1) * tile_size]

    def after(value, other):
        height, width = (min(a, b) for a, b in zip(value.shape, other.shape))
        part = other[:height, :width].astype(value.dtype) * 0
        part = jnp.concatenate([part] * (value.shape[1] // width), 1)
        return value + jnp.concatenate([part] * (value.shape[0] // height), 0)

    def columns_of(value, index):
        return lax.dynamic_slice_in_dim(value, index * cols_here, cols_here, 1)

    hidden_part = jnp.maximum(columns_of(hidden_pre, rep_pos), 0)

    columns = adj_cols[0]
    turn_of = (columns & (side - 1)) ^ inner_pos
    level_of = (columns >> bits) ^ outer_pos
    place = turn_of * per_core + (level_of & (per_core - 1))
    hit = place[None, :] == jnp.arange(section_span, dtype=jnp.int32)[:, None]
    ordered = jnp.zeros((section_span, tile_size, tile_size), bf16)
    for k in range(slots):
        ordered = jnp.where(hit[:, k, None, None], adj_vals[0, k][None], ordered)
    arrived = [
        along_inner(ordered[t * per_core : (t + 1) * per_core], t) for t in turns
    ]
    everyone = lax.all_gather(jnp.concatenate(arrived, 0), "rep", axis=0)
    rows = []
    for t in turns:
        row_block = outer_pos * side + (inner_pos ^ t)
        row = []
        for e in turns:
            column_block = (outer_pos ^ e) * side + inner_pos
            holder = ((row_block - column_block) & (blk_count - 1)) >> span_bits
            index = t * per_core + e % per_core
            piece = everyone[0, index]
            for r in range(1, rep_count):
                piece = jnp.where(holder == r, everyone[r, index], piece)
            row.append(piece)
        rows.append(jnp.concatenate(row, 1))
    block = jnp.concatenate(rows, 0)

    hidden_stack = jnp.concatenate([along_outer(hidden_part, e) for e in turns], 0)
    grad_part = columns_of(cotangent, rep_pos)
    grad_stack = jnp.concatenate([along_inner(grad_part, t) for t in turns], 0)

    mixed = dot(hidden_stack, block, ((0,), (1,))).astype(bf16)
    share = cols_here // side
    by_owner = mixed.reshape(share // rows_here, side, rows_here, side * tile_size)
    mixed_cols = 0.0
    for t in turns:
        chosen = lax.dynamic_index_in_dim(by_owner, inner_pos ^ t, 1, keepdims=False)
        chosen = chosen.reshape(share, side * tile_size)
        chosen = jnp.concatenate([lanes(chosen, u ^ t) for u in turns], 1)
        mixed_cols = mixed_cols + along_inner(chosen, t).astype(jnp.float32)

    back = after(dot(grad_stack, block, ((0,), (0,))), mixed).astype(bf16)
    back = sum(along_outer(lanes(back, e), e).astype(jnp.float32) for e in turns)

    mixed_cols = lax.all_gather(mixed_cols.astype(bf16), "rep", axis=0, tiled=True)
    w_share = w_out.reshape(side, side, rows_here, feature_width)
    w_share = lax.dynamic_index_in_dim(w_share, inner_pos, 1, keepdims=False)
    w_share = columns_of(w_share.reshape(side * rows_here, feature_width), rep_pos)
    out_part = dot(mixed_cols, w_share, ((0,), (0,)))
    out_part = out_part.astype(bf16)
    out_got = [
        along_inner(out_part[t * tile_size : (t + 1) * tile_size], t) for t in turns
    ]
    weight_part = after(dot(mixed_cols, grad_stack, ((1,), (0,))), out_part)
    by_outer = weight_part.reshape(side, rows_here, cols_here)
    grad_weight = halved(
        [lax.dynamic_index_in_dim(by_outer, outer_pos ^ t, 0, keepdims=False) for t in turns],
        along_outer,
        out_got[2:],
    )

    back = after(back, weight_part).astype(bf16)
    w_rows = w_out.reshape(rep_count, cols_here, feature_width)
    if rep_count == 2:
        w_mine = columns_of(lax.dynamic_index_in_dim(w_rows, rep_pos, 0, keepdims=False), rep_pos)
        w_other = columns_of(
            lax.dynamic_index_in_dim(w_rows, 1 - rep_pos, 0, keepdims=False), rep_pos
        )
        grad_in = to_other(dot(back, w_other, ((0,), (1,))).astype(bf16)).astype(jnp.float32)
        grad_in = grad_in + dot(back, w_mine, ((0,), (1,)))
    else:
        back_full = lax.all_gather(back, "rep", axis=0, tiled=True)
        w_mine = lax.dynamic_index_in_dim(w_rows, rep_pos, 0, keepdims=False)
        grad_in = dot(back_full, w_mine, ((0,), (1,)))
    pre_part = columns_of(hidden_pre, rep_pos)
    grad_pre = jnp.where(pre_part > 0, grad_in, 0.0).astype(bf16)
    out_part = sum(part.astype(jnp.float32) for part in out_got)
    out_part = after(out_part, grad_pre).astype(bf16)
    return (out_part, grad_weight, grad_pre)


def solution(mesh):
    placed = (P("blk", None), P("blk", "rep", None, None), P("blk", "rep"), P(), P("blk", None))
    return jax.shard_map(
        shards,
        mesh=mesh,
        in_specs=placed,
        out_specs=(P("blk", "rep"), P("blk", "rep"), P("blk", "rep")),
        check_vma=False,
    )
```

```python
import jax
import jax.numpy as jnp
from jax import lax
from jax.sharding import PartitionSpec as P


def shards(hidden_pre, adj_vals, adj_cols, w_out, cotangent):
    feature_width = hidden_pre.shape[1]
    slots, tile_size = adj_vals.shape[1:3]
    blk_count = lax.axis_size("blk")
    rep_count = lax.axis_size("rep")
    section_span = blk_count // rep_count
    bits = (blk_count.bit_length() - 1) // 2
    side = 1 << bits
    per_core = section_span // side
    blk_pos = lax.axis_index("blk")
    rep_pos = lax.axis_index("rep")
    outer_pos, inner_pos = blk_pos >> bits, blk_pos & (side - 1)
    span_bits = section_span.bit_length() - 1
    cols_here = feature_width // rep_count
    rows_here = feature_width // blk_count
    bf16 = jnp.bfloat16
    turns = range(side)
    rising = [1 << b for b in range(bits)]

    def along_inner(value, turn):
        pairs = [(o * side + i, o * side + (i ^ turn)) for o in turns for i in turns]
        return lax.ppermute(value, "blk", pairs) if turn else value

    def along_outer(value, turn):
        pairs = [(o * side + i, (o ^ turn) * side + i) for o in turns for i in turns]
        return lax.ppermute(value, "blk", pairs) if turn else value

    def halved(parts, move, late):
        parts = dict(enumerate(parts))
        size = parts[0].shape[0]
        for bit in rising:
            keys = [k for k in parts if not k & bit]
            sent = jnp.concatenate([parts[k ^ bit].astype(bf16) for k in keys], 0)
            if bit == rising[-1]:
                for other in late:
                    sent = after(sent, other)
            got = move(sent, bit)
            parts = {
                k: parts[k].astype(jnp.float32)
                + got[n * size : (n + 1) * size].astype(jnp.float32)
                for n, k in enumerate(keys)
            }
        return parts[0]

    def to_other(value):
        return lax.ppermute(value, "rep", [(0, 1), (1, 0)])

    def dot(lhs, rhs, dims):
        return lax.dot_general(lhs, rhs, (dims, ((), ())), preferred_element_type=jnp.float32)

    def lanes(value, index):
        return value[:, index * tile_size : (index + 1) * tile_size]

    def after(value, other):
        height, width = (min(a, b) for a, b in zip(value.shape, other.shape))
        part = other[:height, :width].astype(value.dtype) * 0
        part = jnp.concatenate([part] * (value.shape[1] // width), 1)
        return value + jnp.concatenate([part] * (value.shape[0] // height), 0)

    def columns_of(value, index):
        return lax.dynamic_slice_in_dim(value, index * cols_here, cols_here, 1)

    hidden_part = jnp.maximum(columns_of(hidden_pre, rep_pos), 0)

    columns = adj_cols[0]
    turn_of = (columns & (side - 1)) ^ inner_pos
    level_of = (columns >> bits) ^ outer_pos
    place = turn_of * per_core + (level_of & (per_core - 1))
    hit = place[None, :] == jnp.arange(section_span, dtype=jnp.int32)[:, None]
    ordered = jnp.zeros((section_span, tile_size, tile_size), bf16)
    for k in range(slots):
        ordered = jnp.where(hit[:, k, None, None], adj_vals[0, k][None], ordered)
    arrived = [
        along_inner(ordered[t * per_core : (t + 1) * per_core], t) for t in turns
    ]
    everyone = lax.all_gather(jnp.concatenate(arrived, 0), "rep", axis=0)
    rows = []
    for t in turns:
        row_block = outer_pos * side + (inner_pos ^ t)
        row = []
        for e in turns:
            column_block = (outer_pos ^ e) * side + inner_pos
            holder = ((row_block - column_block) & (blk_count - 1)) >> span_bits
            index = t * per_core + e % per_core
            piece = everyone[0, index]
            for r in range(1, rep_count):
                piece = jnp.where(holder == r, everyone[r, index], piece)
            row.append(piece)
        rows.append(jnp.concatenate(row, 1))
    block = jnp.concatenate(rows, 0)

    hidden_stack = jnp.concatenate([along_outer(hidden_part, e) for e in turns], 0)
    grad_part = columns_of(cotangent, rep_pos)
    grad_stack = jnp.concatenate([along_inner(grad_part, t) for t in turns], 0)

    mixed = dot(hidden_stack, block, ((0,), (1,))).astype(bf16)
    share = cols_here // side
    by_owner = mixed.reshape(share // rows_here, side, rows_here, side * tile_size)
    mixed_cols = 0.0
    for t in turns:
        chosen = lax.dynamic_index_in_dim(by_owner, inner_pos ^ t, 1, keepdims=False)
        chosen = chosen.reshape(share, side * tile_size)
        chosen = jnp.concatenate([lanes(chosen, u ^ t) for u in turns], 1)
        mixed_cols = mixed_cols + along_inner(chosen, t).astype(jnp.float32)

    back = after(dot(grad_stack, block, ((0,), (0,))), mixed).astype(bf16)
    back = sum(along_outer(lanes(back, e), e).astype(jnp.float32) for e in turns)

    mixed_cols = lax.all_gather(mixed_cols.astype(bf16), "rep", axis=0, tiled=True)
    w_share = w_out.reshape(side, side, rows_here, feature_width)
    w_share = lax.dynamic_index_in_dim(w_share, inner_pos, 1, keepdims=False)
    w_share = columns_of(w_share.reshape(side * rows_here, feature_width), rep_pos)
    out_part = dot(mixed_cols, w_share, ((0,), (0,)))
    out_part = out_part.astype(bf16)
    out_got = [
        along_inner(out_part[t * tile_size : (t + 1) * tile_size], t) for t in turns
    ]
    weight_part = after(dot(mixed_cols, grad_stack, ((1,), (0,))), out_part)
    by_outer = weight_part.reshape(side, rows_here, cols_here)
    grad_weight = halved(
        [lax.dynamic_index_in_dim(by_outer, outer_pos ^ t, 0, keepdims=False) for t in turns],
        along_outer,
        out_got[1::2],
    )

    back = after(back, weight_part).astype(bf16)
    w_rows = w_out.reshape(rep_count, cols_here, feature_width)
    if rep_count == 2:
        w_mine = columns_of(lax.dynamic_index_in_dim(w_rows, rep_pos, 0, keepdims=False), rep_pos)
        w_other = columns_of(
            lax.dynamic_index_in_dim(w_rows, 1 - rep_pos, 0, keepdims=False), rep_pos
        )
        grad_in = to_other(dot(back, w_other, ((0,), (1,))).astype(bf16)).astype(jnp.float32)
        grad_in = grad_in + dot(back, w_mine, ((0,), (1,)))
    else:
        back_full = lax.all_gather(back, "rep", axis=0, tiled=True)
        w_mine = lax.dynamic_index_in_dim(w_rows, rep_pos, 0, keepdims=False)
        grad_in = dot(back_full, w_mine, ((0,), (1,)))
    grad_pre = jnp.where(hidden_part > 0, grad_in, 0.0).astype(bf16)
    out_part = sum(part.astype(jnp.float32) for part in out_got)
    out_part = after(out_part, grad_pre).astype(bf16)
    return (out_part, grad_weight, grad_pre)


def solution(mesh):
    placed = (P("blk", None), P("blk", "rep", None, None), P("blk", "rep"), P(), P("blk", None))
    return jax.shard_map(
        shards,
        mesh=mesh,
        in_specs=placed,
        out_specs=(P("blk", "rep"), P("blk", "rep"), P("blk", "rep")),
        check_vma=False,
    )
```

```python
import jax
import jax.numpy as jnp
from jax import lax
from jax.sharding import PartitionSpec as P


def shards(hidden_pre, adj_vals, adj_cols, w_out, cotangent):
    feature_width = hidden_pre.shape[1]
    slots, tile_size = adj_vals.shape[1:3]
    blk_count = lax.axis_size("blk")
    rep_count = lax.axis_size("rep")
    section_span = blk_count // rep_count
    bits = (blk_count.bit_length() - 1) // 2
    side = 1 << bits
    per_core = section_span // side
    blk_pos = lax.axis_index("blk")
    rep_pos = lax.axis_index("rep")
    outer_pos, inner_pos = blk_pos >> bits, blk_pos & (side - 1)
    span_bits = section_span.bit_length() - 1
    cols_here = feature_width // rep_count
    rows_here = feature_width // blk_count
    bf16 = jnp.bfloat16
    turns = range(side)
    rising = [1 << b for b in range(bits)]

    def along_inner(value, turn):
        pairs = [(o * side + i, o * side + (i ^ turn)) for o in turns for i in turns]
        return lax.ppermute(value, "blk", pairs) if turn else value

    def along_outer(value, turn):
        pairs = [(o * side + i, (o ^ turn) * side + i) for o in turns for i in turns]
        return lax.ppermute(value, "blk", pairs) if turn else value

    def halved(parts, move, late):
        parts = dict(enumerate(parts))
        size = parts[0].shape[0]
        for bit in rising:
            keys = [k for k in parts if not k & bit]
            sent = jnp.concatenate([parts[k ^ bit].astype(bf16) for k in keys], 0)
            if bit == rising[-1]:
                for other in late:
                    sent = after(sent, other)
            got = move(sent, bit)
            parts = {
                k: parts[k].astype(jnp.float32)
                + got[n * size : (n + 1) * size].astype(jnp.float32)
                for n, k in enumerate(keys)
            }
        return parts[0]

    def to_other(value):
        return lax.ppermute(value, "rep", [(0, 1), (1, 0)])

    def dot(lhs, rhs, dims):
        return lax.dot_general(lhs, rhs, (dims, ((), ())), preferred_element_type=jnp.float32)

    def lanes(value, index):
        return value[:, index * tile_size : (index + 1) * tile_size]

    def after(value, other):
        height, width = (min(a, b) for a, b in zip(value.shape, other.shape))
        part = other[:height, :width].astype(value.dtype) * 0
        part = jnp.concatenate([part] * (value.shape[1] // width), 1)
        return value + jnp.concatenate([part] * (value.shape[0] // height), 0)

    def columns_of(value, index):
        return lax.dynamic_slice_in_dim(value, index * cols_here, cols_here, 1)

    hidden_part = jnp.maximum(columns_of(hidden_pre, rep_pos), 0)

    columns = adj_cols[0]
    turn_of = (columns & (side - 1)) ^ inner_pos
    level_of = (columns >> bits) ^ outer_pos
    place = turn_of * per_core + (level_of & (per_core - 1))
    hit = place[None, :] == jnp.arange(section_span, dtype=jnp.int32)[:, None]
    ordered = jnp.zeros((section_span, tile_size, tile_size), bf16)
    for k in range(slots):
        ordered = jnp.where(hit[:, k, None, None], adj_vals[0, k][None], ordered)
    arrived = [
        along_inner(ordered[t * per_core : (t + 1) * per_core], t) for t in turns
    ]
    everyone = lax.all_gather(jnp.concatenate(arrived, 0), "rep", axis=0)
    rows = []
    for t in turns:
        row_block = outer_pos * side + (inner_pos ^ t)
        row = []
        for e in turns:
            column_block = (outer_pos ^ e) * side + inner_pos
            holder = ((row_block - column_block) & (blk_count - 1)) >> span_bits
            index = t * per_core + e % per_core
            piece = everyone[0, index]
            for r in range(1, rep_count):
                piece = jnp.where(holder == r, everyone[r, index], piece)
            row.append(piece)
        rows.append(jnp.concatenate(row, 1))
    block = jnp.concatenate(rows, 0)

    hidden_stack = jnp.concatenate([along_outer(hidden_part, e) for e in turns], 0)
    grad_part = columns_of(cotangent, rep_pos)
    grad_stack = jnp.concatenate([along_inner(grad_part, t) for t in turns], 0)

    mixed = dot(hidden_stack, block, ((0,), (1,))).astype(bf16)
    share = cols_here // side
    by_owner = mixed.reshape(share // rows_here, side, rows_here, side * tile_size)
    mixed_cols = 0.0
    for t in turns:
        chosen = lax.dynamic_index_in_dim(by_owner, inner_pos ^ t, 1, keepdims=False)
        chosen = chosen.reshape(share, side * tile_size)
        chosen = jnp.concatenate([lanes(chosen, u ^ t) for u in turns], 1)
        mixed_cols = mixed_cols + along_inner(chosen, t).astype(jnp.float32)

    back = after(dot(grad_stack, block, ((0,), (0,))), mixed).astype(bf16)
    back = sum(along_outer(lanes(back, e), e).astype(jnp.float32) for e in turns)

    mixed_cols = lax.all_gather(mixed_cols.astype(bf16), "rep", axis=0, tiled=True)
    w_share = w_out.reshape(side, side, rows_here, feature_width)
    w_share = lax.dynamic_index_in_dim(w_share, inner_pos, 1, keepdims=False)
    w_share = columns_of(w_share.reshape(side * rows_here, feature_width), rep_pos)
    out_part = dot(mixed_cols, w_share, ((0,), (0,)))
    out_part = out_part.astype(bf16)
    out_got = [
        along_inner(out_part[t * tile_size : (t + 1) * tile_size], t) for t in turns
    ]
    weight_part = after(dot(mixed_cols, grad_stack, ((1,), (0,))), out_part)
    by_outer = weight_part.reshape(side, rows_here, cols_here)
    grad_weight = halved(
        [lax.dynamic_index_in_dim(by_outer, outer_pos ^ t, 0, keepdims=False) for t in turns],
        along_outer,
        out_got[1::2],
    )

    back = back.astype(bf16)
    w_rows = w_out.reshape(rep_count, cols_here, feature_width)
    if rep_count == 2:
        w_mine = columns_of(lax.dynamic_index_in_dim(w_rows, rep_pos, 0, keepdims=False), rep_pos)
        w_other = columns_of(
            lax.dynamic_index_in_dim(w_rows, 1 - rep_pos, 0, keepdims=False), rep_pos
        )
        grad_in = to_other(dot(back, w_other, ((0,), (1,))).astype(bf16)).astype(jnp.float32)
        grad_in = grad_in + dot(back, w_mine, ((0,), (1,)))
    else:
        back_full = lax.all_gather(back, "rep", axis=0, tiled=True)
        w_mine = lax.dynamic_index_in_dim(w_rows, rep_pos, 0, keepdims=False)
        grad_in = dot(back_full, w_mine, ((0,), (1,)))
    pre_part = columns_of(hidden_pre, rep_pos)
    grad_pre = jnp.where(pre_part > 0, grad_in, 0.0).astype(bf16)
    out_part = sum(part.astype(jnp.float32) for part in out_got)
    out_part = after(out_part, grad_pre).astype(bf16)
    return (out_part, grad_weight, grad_pre)


def solution(mesh):
    placed = (P("blk", None), P("blk", "rep", None, None), P("blk", "rep"), P(), P("blk", None))
    return jax.shard_map(
        shards,
        mesh=mesh,
        in_specs=placed,
        out_specs=(P("blk", "rep"), P("blk", "rep"), P("blk", "rep")),
        check_vma=False,
    )
```
